32 devices in a mesh: seq: 16 (over z, x, core), mp: 2 (over y).
Axes of the slice: x: 2, y: 2, z: 4, core: 2. Of those that a mesh axis runs over, the one named last changes fastest.
Arguments:
- acoustic_features: bfloat16 [16384, 1024], P('seq'), may hold values from -6 to 6
- clip_durations: int32 [32], replicated, may hold values from 1 to 3008, as said below
- early_layernorm_scale: float32 [1024], replicated, may hold values from 0.25 to 1.75
- early_widening_matrix: bfloat16 [1024, 4096], P(None, 'mp'), may hold values from -0.1875 to 0.1875
- early_narrowing_matrix: bfloat16 [4096, 1024], P('mp'), may hold values from -0.09375 to 0.09375
- mixer_layernorm_scale: float32 [1024], replicated, may hold values from 0.25 to 1.75
- triple_matrix: bfloat16 [3, 1024, 1024], P(None, None, 'mp'), may hold values from -0.25 to 0.25
- mixer_exit_matrix: bfloat16 [1024, 1024], P('mp'), may hold values from -0.75 to 0.75
- filter_layernorm_scale: float32 [1024], replicated, may hold values from 0.25 to 1.75
- gating_pair_matrix: bfloat16 [2, 1024, 1024], P(None, None, 'mp'), may hold values from -0.1875 to 0.1875
- depthwise_filter: float32 [5, 1024], P(None, 'mp'), may hold values from -6 to 6
- running_stats_factor: float32 [1024], P('mp'), may hold values from 0.25 to 1.75
- running_stats_offset: float32 [1024], P('mp'), may hold values from -3 to 3
- filter_exit_projection: bfloat16 [1024, 1024], P('mp'), may hold values from -0.1875 to 0.1875
- later_layernorm_scale: float32 [1024], replicated, may hold values from 0.25 to 1.75
- later_widening_matrix: bfloat16 [1024, 4096], P(None, 'mp'), may hold values from -0.1875 to 0.1875
- later_narrowing_matrix: bfloat16 [4096, 1024], P('mp'), may hold values from -0.09375 to 0.09375
- last_layernorm_scale: float32 [1024], replicated, may hold values from 0.25 to 1.75
- quantizer_projection: bfloat16 [1024, 1024], P(None, 'mp'), may hold values from -0.1875 to 0.1875
- entry_vectors: bfloat16 [1024, 1024], P('mp'), may hold values from -6 to 6
- smoothing_level: float32 [1], replicated, may hold values from 0.5 to 2
- random_flat_samples: float32 [16384, 1024], P('seq', 'mp'), may hold values from 0.02 to 0.98
- expected_entries: int32 [16384], P('seq'), may hold values from 0 to 1023
- result_adjoint: bfloat16 [16384, 1024], P('seq'), may hold values from -6 to 6
- discrete_adjoint: bfloat16 [16384, 1024], P('seq'), may hold values from -6 to 6
Outputs:
- layer_out: bfloat16 [16384, 1024], P('seq')
- quantized: bfloat16 [16384, 1024], P('seq')
- frame_loss: float32 [16384], P('seq')
- grad_frames: bfloat16 [16384, 1024], P('seq')
- grad_ln_ffn1: float32 [1024], replicated
- grad_up1: float32 [1024, 4096], P(None, 'mp')
- grad_down1: float32 [4096, 1024], P('mp')
- grad_ln_att: float32 [1024], replicated
- grad_qkv: float32 [3, 1024, 1024], P(None, None, 'mp')
- grad_out: float32 [1024, 1024], P('mp')
- grad_ln_conv: float32 [1024], replicated
- grad_glu: float32 [2, 1024, 1024], P(None, None, 'mp')
- grad_kernel: float32 [5, 1024], P(None, 'mp')
- grad_bn_gain: float32 [1024], P('mp')
- grad_bn_bias: float32 [1024], P('mp')
- grad_point: float32 [1024, 1024], P('mp')
- grad_ln_ffn2: float32 [1024], replicated
- grad_up2: float32 [1024, 4096], P(None, 'mp')
- grad_down2: float32 [4096, 1024], P('mp')
- grad_ln_final: float32 [1024], replicated
- grad_w_code: float32 [1024, 1024], P(None, 'mp')
- grad_codebook: float32 [1024, 1024], P('mp')
- grad_temperature: float32 [1], replicated
The draws below stay inside these ranges and needn't reach their ends.
Inputs may be any that keep to these rules, and one draw needn't show every extreme that they name: `clip_durations`: the lengths sum to 16384; no clip has more than 3008 frames, and at least one clip has exactly 3008.
All inputs are finite; a program needn't handle non-finite values.
Results may differ from the reference program's by a relative error of at most 0.033.
Values may be sent and summed in bfloat16 or wider, within the bound.
A program may use at most 320 MiB of HBM per device.

```python
import math
import jax
import jax.numpy as jnp
import numpy as np
from jax import lax

D = 1024
HEADS = 8
HEAD = 128
FF = 4096
KERNEL = 5
CODES = 1024
TOK_DEV = 1024
FRAME_TOTAL = 16384
LONGEST = 3008
CLIPS = 32


def draw_clip_durations(key, part):
    key = jax.random.fold_in(key, 11)
    spot_key, start_key, order_key, cell_key = jax.random.split(key, 4)
    device_spot = jax.random.randint(spot_key, (), 0, FRAME_TOTAL // TOK_DEV - 3).astype(jnp.int32)
    inner_start = jax.random.randint(start_key, (), TOK_DEV // 16 + 1, TOK_DEV).astype(jnp.int32)
    long_start = device_spot * TOK_DEV + inner_start
    place = jnp.arange(1, FRAME_TOTAL, dtype=jnp.int32)
    relative = place - long_start
    cell_count_value = jnp.floor_divide(relative, LONGEST)
    forced = jnp.remainder(relative, LONGEST) == 0
    inside = jnp.logical_and(relative > 0, relative < LONGEST)
    cell_extent = FRAME_TOTAL // LONGEST + 1
    cell_weighting = jax.random.randint(cell_key, (2 * cell_extent + 1,), 0, 4).astype(jnp.int32)
    extra_credit = jnp.take(cell_weighting, jnp.clip(cell_count_value + cell_extent, 0, 2 * cell_extent)) * (FRAME_TOTAL // 4)
    sorting_order = jax.random.permutation(order_key, FRAME_TOTAL - 1).astype(jnp.int32)
    scoring_value = sorting_order + extra_credit
    scoring_value = jnp.where(forced, 2 * FRAME_TOTAL, scoring_value)
    scoring_value = jnp.where(inside, -1, scoring_value)
    keyed = scoring_value * FRAME_TOTAL + place
    chosen = jnp.sort(keyed)[FRAME_TOTAL - CLIPS:]
    cut_points = jnp.sort(jnp.remainder(chosen, FRAME_TOTAL)).astype(jnp.int32)
    edge_points = jnp.concatenate([jnp.zeros((1,), jnp.int32), cut_points, jnp.full((1,), FRAME_TOTAL, jnp.int32)])
    return (edge_points[1:] - edge_points[:-1]).astype(jnp.int32)


def place_ends(values, stream_key, smallest, largest):
    longest = values.shape.index(max(values.shape))
    spots = []
    for shift in (0, 1):
        where = [jax.random.randint(jax.random.fold_in(stream_key, axis), (), 0, length) for axis, length in enumerate(values.shape)]
        where[longest] = (where[longest] + shift) % values.shape[longest]
        spots.append(tuple(where))
    return values.at[spots[0]].set(smallest).at[spots[1]].set(largest)


def block_scale(stream_key, extent, shards, least, largest):
    level, own = 1.0, jax.random.fold_in(stream_key, 6)
    for dim, shards_of in shards:
        draws = jnp.exp(jax.random.uniform(jax.random.fold_in(own, dim), (shards_of,), jnp.float32, least / len(shards), largest / len(shards)))
        level = level * jnp.repeat(draws, extent[dim] // shards_of).reshape([-1 if axis == dim else 1 for axis in range(len(extent))])
    return level


def cumulative_ranks(count, lean):
    weights = [(1 << 20) // math.isqrt(standing ** lean) + 1 for standing in range(1, count + 1)]
    deviation = 1 + sum(weights) // (1 << 30)
    return np.cumsum(np.array([max(1, weight // deviation) for weight in weights]))


def ranked(key, extent, amount, slope):
    table = cumulative_ranks(amount, slope)
    lot = jax.random.randint(jax.random.fold_in(key, 1), extent, 0, int(table[amount - 1]))
    grade = jnp.searchsorted(jnp.asarray(table, jnp.int32), lot, side="right")
    return jax.random.permutation(jax.random.fold_in(key, 2), amount)[grade].astype(jnp.int32)


def noise(own_key, dims, spread, most, cuts=(), kind=jnp.bfloat16):
    values = jax.random.normal(own_key, dims, jnp.float32) * spread
    if len(cuts) > 0:
        values = block_scale(own_key, dims, cuts, -0.22, 0.18) * values
    return jnp.clip(values, min=-most, max=most).astype(kind)


def setup_inputs(seed: int = 0) -> dict:
    seeds = jax.random.split(jax.random.key(seed), 26)
    acoustic_features = noise(seeds[0], (FRAME_TOTAL, D), 1.0, 6.0, ((0, 16),))
    clip_durations = draw_clip_durations(jax.random.fold_in(seeds[25], 71), 0)
    early_layernorm_scale = jnp.clip(1.0 + 0.15 * jax.random.normal(seeds[2], (D,), jnp.float32), 0.25, 1.75)
    early_widening_matrix = noise(seeds[3], (D, FF), D ** -0.5, 0.1875, ((1, 2),))
    early_narrowing_matrix = noise(seeds[4], (FF, D), FF ** -0.5, 0.09375, ((0, 2),))
    mixer_layernorm_scale = jnp.clip(1.0 + 0.15 * jax.random.normal(seeds[5], (D,), jnp.float32), 0.25, 1.75)
    triple_matrix = noise(seeds[6], (3, D, D), (D // 2) ** -0.5, 0.25, ((2, 2),))
    mixer_exit_matrix = noise(seeds[7], (D, D), (max(1, D // 16)) ** -0.5, 0.75, ((0, 2),))
    filter_layernorm_scale = jnp.clip(1.0 + 0.15 * jax.random.normal(seeds[8], (D,), jnp.float32), 0.25, 1.75)
    gating_pair_matrix = noise(seeds[9], (2, D, D), D ** -0.5, 0.1875, ((2, 2),))
    depthwise_filter = noise(seeds[10], (KERNEL, D), 0.4, 6.0, ((1, 2),), jnp.float32)
    running_stats_factor = jnp.clip(1.0 + 0.15 * jax.random.normal(seeds[11], (D,), jnp.float32), 0.25, 1.75)
    running_stats_offset = noise(seeds[12], (D,), 0.5, 3.0, ((0, 2),), jnp.float32)
    filter_exit_projection = noise(seeds[13], (D, D), D ** -0.5, 0.1875, ((0, 2),))
    later_layernorm_scale = jnp.clip(1.0 + 0.15 * jax.random.normal(seeds[14], (D,), jnp.float32), 0.25, 1.75)
    later_widening_matrix = noise(seeds[15], (D, FF), D ** -0.5, 0.1875, ((1, 2),))
    later_narrowing_matrix = noise(seeds[16], (FF, D), FF ** -0.5, 0.09375, ((0, 2),))
    last_layernorm_scale = jnp.clip(1.0 + 0.15 * jax.random.normal(seeds[17], (D,), jnp.float32), 0.25, 1.75)
    quantizer_projection = noise(seeds[18], (D, CODES), D ** -0.5, 0.1875, ((1, 2),))
    entry_vectors = noise(seeds[19], (CODES, D), 1.0, 6.0, ((0, 2),))
    smoothing_level = jnp.clip(jnp.exp(jax.random.uniform(seeds[20], (1,), jnp.float32, math.log(0.5), math.log(2.0))), 0.5, 2.0)
    random_flat_samples = jnp.clip(0.02 + 0.96000002 * jax.random.uniform(seeds[21], (FRAME_TOTAL, CODES), jnp.float32) ** block_scale(seeds[21], (FRAME_TOTAL, CODES), ((0, 16), (1, 2)), -0.2, 0.2), 0.02, 0.98)
    expected_entries = place_ends(ranked(seeds[22], (FRAME_TOTAL,), CODES, 2), jax.random.fold_in(seeds[22], 3), 0, CODES - 1).astype(jnp.int32)
    result_adjoint = noise(seeds[23], (FRAME_TOTAL, D), 1.0, 6.0, ((0, 16),))
    discrete_adjoint = noise(seeds[24], (FRAME_TOTAL, D), 1.0, 6.0, ((0, 16),))
    return {"acoustic_features": acoustic_features, "clip_durations": clip_durations, "early_layernorm_scale": early_layernorm_scale, "early_widening_matrix": early_widening_matrix, "early_narrowing_matrix": early_narrowing_matrix, "mixer_layernorm_scale": mixer_layernorm_scale, "triple_matrix": triple_matrix, "mixer_exit_matrix": mixer_exit_matrix, "filter_layernorm_scale": filter_layernorm_scale, "gating_pair_matrix": gating_pair_matrix, "depthwise_filter": depthwise_filter, "running_stats_factor": running_stats_factor, "running_stats_offset": running_stats_offset, "filter_exit_projection": filter_exit_projection, "later_layernorm_scale": later_layernorm_scale, "later_widening_matrix": later_widening_matrix, "later_narrowing_matrix": later_narrowing_matrix, "last_layernorm_scale": last_layernorm_scale, "quantizer_projection": quantizer_projection, "entry_vectors": entry_vectors, "smoothing_level": smoothing_level, "random_flat_samples": random_flat_samples, "expected_entries": expected_entries, "result_adjoint": result_adjoint, "discrete_adjoint": discrete_adjoint}


EPSILON = 1e-05
HIGHEST = lax.Precision.HIGHEST
MASKED = -1e+30

@jax.custom_vjp
def low(v):
    return lax.optimization_barrier(v.astype(jnp.bfloat16)).astype(jnp.float32)

@jax.custom_vjp
def low_back(v):
    return v

def low_keep(v):
    return (low(v), None)

def low_pass(kept, grad):
    return (grad,)

def back_keep(v):
    return (v, None)

def back_low(kept, grad):
    return (low(grad),)
low.defvjp(low_keep, low_pass)
low_back.defvjp(back_keep, back_low)

def matmul(first_op, second_op):
    return jnp.dot(first_op, second_op, precision=HIGHEST, preferred_element_type=jnp.float32)

def clip_of(clip_durations, positions):
    clip_ends = jnp.cumsum(clip_durations, dtype=jnp.int32)
    passed = clip_ends[None, :] <= positions[:, None]
    segment = lax.optimization_barrier(jnp.sum(passed.astype(jnp.int32), 1, dtype=jnp.int32))
    starts = lax.optimization_barrier(jnp.sum(jnp.where(passed, clip_durations[None, :], 0), 1, dtype=jnp.int32))
    return (segment, positions - starts)

def layer_norm(layer_operands, norm_gain):
    centred = layer_operands - lax.optimization_barrier(jnp.mean(layer_operands, -1, keepdims=True))
    inverse = lax.rsqrt(lax.optimization_barrier(jnp.mean(centred * centred, -1, keepdims=True)) + EPSILON)
    return centred * inverse * norm_gain

def rotary(heads_in, position, direction):
    half_width = heads_in.shape[-1] // 2
    frequency = 10000.0 ** (-jnp.arange(half_width, dtype=jnp.float32) / half_width)
    angles = position.astype(jnp.float32)[:, None] * frequency[None, :]
    cosine = jnp.cos(angles)[:, None, :]
    sine_part = direction * jnp.sin(angles)[:, None, :]
    leading = heads_in[..., :half_width]
    trailing = heads_in[..., half_width:]
    return jnp.concatenate([leading * cosine - trailing * sine_part, leading * sine_part + trailing * cosine], -1)

def ffn_branch(layer_operands, norm_gain, w_in, w_back):
    entered = low(layer_norm(layer_operands, norm_gain))
    hidden = low_back(matmul(entered, w_in))
    activated = low(jax.nn.silu(hidden))
    return low_back(matmul(activated, w_back))

def attention(layer_operands, norm_gain, triple_matrix, mixer_exit_matrix, segment, position):
    entered = low(layer_norm(layer_operands, norm_gain))
    queries = low_back(matmul(entered, triple_matrix[0])).reshape(FRAME_TOTAL, HEADS, HEAD)
    keys_all = low_back(matmul(entered, triple_matrix[1])).reshape(FRAME_TOTAL, HEADS, HEAD)
    values_all = low(low_back(matmul(entered, triple_matrix[2]))).reshape(FRAME_TOTAL, HEADS, HEAD)
    queries = low(rotary(queries, position, 1.0))
    keys_all = low(rotary(keys_all, position, 1.0))
    block_rows = min(512, FRAME_TOTAL)

    def one_block(pieces):
        query_block, seg_block = pieces
        scores = low_back(jnp.einsum('qhd,khd->hqk', query_block, keys_all, precision=HIGHEST) * HEAD ** (-0.5))
        scores = jnp.where(seg_block[None, :, None] == segment[None, None, :], scores, MASKED)
        weights = jax.nn.softmax(scores, axis=-1)
        return jnp.einsum('hqk,khd->qhd', low(weights), values_all, precision=HIGHEST)
    mixed = lax.map(jax.checkpoint(one_block), (queries.reshape(FRAME_TOTAL // block_rows, block_rows, HEADS, HEAD), segment.reshape(FRAME_TOTAL // block_rows, block_rows)))
    mixed = low(low_back(mixed.reshape(FRAME_TOTAL, D)))
    return low_back(matmul(mixed, mixer_exit_matrix))

def depthwise(gated, depthwise_filter, segment):
    half_kernel = KERNEL // 2
    padded = jnp.pad(gated, ((half_kernel, half_kernel), (0, 0)))
    seg_pad = jnp.pad(segment, (half_kernel, half_kernel), constant_values=-1)
    result = jnp.zeros_like(gated)
    for tap_index in range(KERNEL):
        matches = (seg_pad[tap_index:tap_index + FRAME_TOTAL] == segment)[:, None]
        result = result + depthwise_filter[tap_index][None, :] * jnp.where(matches, padded[tap_index:tap_index + FRAME_TOTAL], 0.0)
    return result

def convolve(layer_operands, norm_gain, gating_pair_matrix, depthwise_filter, running_stats_factor, running_stats_offset, filter_exit_projection, segment):
    entered = low(layer_norm(layer_operands, norm_gain))
    glu_value = low_back(matmul(entered, gating_pair_matrix[0]))
    glu_gate = low_back(matmul(entered, gating_pair_matrix[1]))
    gated = low(glu_value * jax.nn.sigmoid(glu_gate))
    conv_out = low_back(depthwise(gated, depthwise_filter, segment))
    bn_mean = lax.optimization_barrier(jnp.mean(conv_out, 0))
    bn_var = lax.optimization_barrier(jnp.mean(conv_out * conv_out, 0)) - bn_mean * bn_mean
    normed = (conv_out - bn_mean) * lax.rsqrt(bn_var + EPSILON) * running_stats_factor + running_stats_offset
    swished = low(jax.nn.silu(normed))
    return low_back(matmul(swished, filter_exit_projection))

def discretize_features(layer_operands, quantizer_projection, entry_vectors, smoothing_level, random_flat_samples):
    logits = low_back(matmul(layer_operands, quantizer_projection))
    noisy_entry_scores = logits - jnp.log(-jnp.log(random_flat_samples))
    smooth_assignments = jax.nn.softmax(noisy_entry_scores / smoothing_level[0], axis=-1)
    return matmul(low(smooth_assignments), entry_vectors)

def predict(final_low, entry_vectors, expected_entries):
    logits = low_back(matmul(final_low, entry_vectors.T) * D ** (-0.5))
    log_total = jax.nn.logsumexp(logits, -1)
    is_target = jnp.arange(CODES, dtype=jnp.int32)[None, :] == expected_entries[:, None]
    picked = lax.optimization_barrier(jnp.sum(jnp.where(is_target, logits, 0.0), -1))
    return log_total - picked

def reference(acoustic_features, clip_durations, early_layernorm_scale, early_widening_matrix, early_narrowing_matrix, mixer_layernorm_scale, triple_matrix, mixer_exit_matrix, filter_layernorm_scale, gating_pair_matrix, depthwise_filter, running_stats_factor, running_stats_offset, filter_exit_projection, later_layernorm_scale, later_widening_matrix, later_narrowing_matrix, last_layernorm_scale, quantizer_projection, entry_vectors, smoothing_level, random_flat_samples, expected_entries, result_adjoint, discrete_adjoint):
    segment, position = clip_of(clip_durations, jnp.arange(FRAME_TOTAL, dtype=jnp.int32))
    random_samples = random_flat_samples.astype(jnp.float32)
    model_tensors = tuple((widening_matrix.astype(jnp.float32) for widening_matrix in (acoustic_features, early_layernorm_scale, early_widening_matrix, early_narrowing_matrix, mixer_layernorm_scale, triple_matrix, mixer_exit_matrix, filter_layernorm_scale, gating_pair_matrix, depthwise_filter, running_stats_factor, running_stats_offset, filter_exit_projection, later_layernorm_scale, later_widening_matrix, later_narrowing_matrix, last_layernorm_scale, quantizer_projection, entry_vectors, smoothing_level)))

    def layer_apply(layer_operands, early_scale_vector, raise_matrix_early, lower_matrix_early, mixer_scale_vector, triple_projection, mixer_exit, filter_scale_vector, gating_matrix, filter_coefficients, stats_multiplier, stats_addend, filter_exit_matrix, later_scale_vector, raise_matrix_later, lower_matrix_later, last_scale_vector, quantizer_matrix, lookup_vectors, smoothing_coefficient):
        after_ffn = layer_operands + 0.5 * ffn_branch(layer_operands, early_scale_vector, raise_matrix_early, lower_matrix_early)
        after_att = after_ffn + attention(after_ffn, mixer_scale_vector, triple_projection, mixer_exit, segment, position)
        after_conv = after_att + convolve(after_att, filter_scale_vector, gating_matrix, filter_coefficients, stats_multiplier, stats_addend, filter_exit_matrix, segment)
        after_two = after_conv + 0.5 * ffn_branch(after_conv, later_scale_vector, raise_matrix_later, lower_matrix_later)
        final_low = low(layer_norm(after_two, last_scale_vector))
        discrete_vectors = discretize_features(layer_operands, quantizer_matrix, lookup_vectors, smoothing_coefficient, random_samples)
        row_losses = predict(final_low, lookup_vectors, expected_entries)
        return (final_low, discrete_vectors, row_losses)
    outputs, pullback = jax.vjp(layer_apply, *model_tensors)
    grads = pullback((result_adjoint.astype(jnp.float32), discrete_adjoint.astype(jnp.float32), jnp.ones((FRAME_TOTAL,), jnp.float32)))
    final_low, discrete_vectors, row_losses = outputs
    return (final_low.astype(jnp.bfloat16), discrete_vectors.astype(jnp.bfloat16), row_losses, grads[0].astype(jnp.bfloat16), grads[1], grads[2], grads[3], grads[4], grads[5], grads[6], grads[7], grads[8], grads[9], grads[10], grads[11], grads[12], grads[13], grads[14], grads[15], grads[16], grads[17], grads[18], grads[19])
```

```python
import functools
import math

import jax
import jax.numpy as jnp
from jax import lax
from jax.experimental import pallas as pl
from jax.experimental.pallas import tpu as pltpu
from jax.sharding import PartitionSpec as P

D = 1024
HEAD = 128
KERNEL = 5
LONGEST = 3008

EPSILON = 1e-05
MASKED = -1e30
SCALE = HEAD ** (-0.5)
BOTH = ("seq", "mp")
LOW = jnp.bfloat16
WIDE = jnp.float32


def dot(a, b, dims=((1,), (0,))):
    return lax.dot_general(a, b, (dims, ((), ())), preferred_element_type=WIDE)


def dot_nt(a, b):
    return dot(a, b, ((1,), (1,)))


def dot_tn(a, b):
    return dot(a, b, ((0,), (0,)))


def cut(array, start, size, axis=0):
    return lax.dynamic_slice_in_dim(array, start, size, axis)


def mp_shift(shard, by):
    count = lax.axis_size("mp")
    return lax.ppermute(shard, "mp", [(i, (i + by) % count) for i in range(count)])


def seq_xor(shard, mask):
    return lax.ppermute(shard, "seq", [(i, i ^ mask) for i in range(lax.axis_size("seq"))])


def seq_shift(shard, by):
    count = lax.axis_size("seq")
    return lax.ppermute(shard, "seq", [(i, i + by) for i in range(count) if 0 <= i + by < count])


def flat_shift(shard, by):
    count = lax.axis_size("seq") * lax.axis_size("mp")
    return lax.ppermute(shard, BOTH, [(i, i + by) for i in range(count) if 0 <= i + by < count])


def from_mp(shard):
    return [shard] + [mp_shift(shard, -k) for k in range(1, lax.axis_size("mp"))]


def to_mp(parts):
    total = parts[0].astype(WIDE)
    for k in range(1, len(parts)):
        total = total + mp_shift(parts[k].astype(LOW), k).astype(WIDE)
    return total


def mp_place(k):
    return (lax.axis_index("mp") + k) % lax.axis_size("mp")


def joined(pieces, axis=0):
    size = pieces[0].shape[axis]
    shape = list(pieces[0].shape)
    shape[axis] = size * len(pieces)
    whole = jnp.zeros(shape, pieces[0].dtype)
    for k, piece in enumerate(pieces):
        whole = lax.dynamic_update_slice_in_dim(whole, piece, mp_place(k) * size, axis)
    return whole


def fetched(shard, axis):
    core = lax.axis_index("seq") % 2
    half = shard.shape[axis] // 2
    mine = cut(shard, core * half, half, axis)
    parts = from_mp(mine)[1:]
    return [[part, seq_xor(part, 1)] for part in parts]


def whole_of(shard, axis):
    core = lax.axis_index("seq") % 2
    size = shard.shape[axis]
    half = size // 2
    shape = list(shard.shape)
    shape[axis] = size * lax.axis_size("mp")
    whole = jnp.zeros(shape, shard.dtype)
    whole = lax.dynamic_update_slice_in_dim(whole, shard, mp_place(0) * size, axis)
    for k, pair in enumerate(fetched(shard, axis)):
        for j in range(2):
            start = mp_place(k + 1) * size + (core ^ j) * half
            whole = lax.dynamic_update_slice_in_dim(whole, pair[j], start, axis)
    return whole


def halved(part, first_bit):
    place = lax.axis_index("seq")
    for bit in range(first_bit, int(math.log2(lax.axis_size("seq")))):
        half = part.shape[0] // 2
        side = (place >> bit) & 1
        sent = seq_xor(cut(part, (1 - side) * half, half), 1 << bit)
        part = cut(part, side * half, half) + sent
    return part


def summed_grad(pieces, across):
    held = [pair[0].astype(LOW) + seq_xor(pair[1].astype(LOW), 1) for pair in pieces]
    total = held[0]
    for k in range(1, len(held)):
        total = total + mp_shift(held[k], k)
    block = halved(total, 1)
    rows, columns = block.shape
    bits = int(math.log2(lax.axis_size("seq")))
    every = lax.all_gather(block, "seq", axis=0).reshape([2] * bits + [rows, columns])
    order = [bits - 1 - bit for bit in range(1, bits)] + [bits]
    spread = rows << (bits - 1)
    if across:
        every = jnp.transpose(every, order + [bits - 1, bits + 1])
        return every.reshape(spread, 2 * columns).astype(WIDE)
    every = jnp.transpose(every, [bits - 1] + order + [bits + 1])
    return every.reshape(2 * spread, columns).astype(WIDE)


def clip_of(clip_durations, positions):
    clip_ends = jnp.cumsum(clip_durations, dtype=jnp.int32)
    passed = clip_ends[None, :] <= positions[:, None]
    segment = jnp.sum(passed.astype(jnp.int32), 1, dtype=jnp.int32)
    starts = jnp.sum(jnp.where(passed, clip_durations[None, :], 0), 1, dtype=jnp.int32)
    ends = jnp.min(jnp.where(passed, 2**30, clip_ends[None, :]), 1)
    return segment, starts, ends


def norm_forward(rows, gain):
    centred = rows - jnp.mean(rows, -1, keepdims=True)
    inverse = lax.rsqrt(jnp.mean(centred * centred, -1, keepdims=True) + EPSILON)
    normed = centred * inverse
    return (normed * gain).astype(LOW), normed, inverse


def norm_backward(upstream, gain, normed, inverse):
    scaled = upstream * gain
    centred = (
        scaled
        - jnp.mean(scaled, -1, keepdims=True)
        - normed * jnp.mean(scaled * normed, -1, keepdims=True)
    )
    return centred * inverse, jnp.sum(upstream * normed, 0)


def rotary(rows, position, direction):
    half_width = rows.shape[-1] // 2
    frequency = 10000.0 ** (-jnp.arange(half_width, dtype=WIDE) / half_width)
    angles = position.astype(WIDE)[:, None] * frequency[None, :]
    cosine = jnp.cos(angles)
    sine = direction * jnp.sin(angles)
    leading = rows[..., :half_width]
    trailing = rows[..., half_width:]
    return jnp.concatenate([leading * cosine - trailing * sine, leading * sine + trailing * cosine], -1)


def silu_slope(hidden, sigma):
    return sigma * (1.0 + hidden * (1.0 - sigma))


def attend_kernel(lo_ref, hi_ref, q_ref, kv_ref, sq_ref, sk_ref, low_ref, mix_ref, lse_ref, *, depth, parts):
    i = pl.program_id(0)
    rows = q_ref.shape[0] // parts
    queries = [q_ref[j * rows : (j + 1) * rows, :] for j in range(parts)]
    query_seg = [sq_ref[j * rows : (j + 1) * rows, :] for j in range(parts)]

    def step(t, carry):
        span = pl.ds(pl.multiple_of(t * depth, depth), depth)
        keys = kv_ref[span, :HEAD]
        values = kv_ref[span, HEAD:]
        key_seg = sk_ref[t]
        out = []
        for j in range(parts):
            top, total, mixed = carry[j]
            scores = dot_nt(queries[j], keys) * SCALE
            scores = jnp.where(query_seg[j] == key_seg, scores, MASKED)
            new_top = jnp.maximum(top, jnp.max(scores, -1, keepdims=True))
            probs = jnp.exp(scores - new_top)
            fade = jnp.exp(top - new_top)
            total = fade * total + jnp.sum(probs, -1, keepdims=True)
            mixed = fade * mixed + dot(probs.astype(LOW), values)
            out.append((new_top, total, mixed))
        return tuple(out)

    start = (
        jnp.full((rows, 1), MASKED, WIDE),
        jnp.zeros((rows, 1), WIDE),
        jnp.zeros((rows, HEAD), WIDE),
    )
    done = lax.fori_loop(lo_ref[i], hi_ref[i], step, (start,) * parts)
    for j in range(parts):
        top, total, mixed = done[j]
        mixed = mixed / total
        span = slice(j * rows, (j + 1) * rows)
        mix_ref[span, :] = mixed
        low_ref[span, :] = mixed.astype(LOW)
        lse_ref[span, :] = top + jnp.log(total)


def bounds(starts, ends, key_base, rows, depth, key_rows):
    count = key_rows // depth
    lo = jnp.clip((starts[::rows] - key_base) // depth, 0, count)
    hi = jnp.clip((ends[rows - 1 :: rows] - key_base + depth - 1) // depth, 0, count)
    return lo.astype(jnp.int32), hi.astype(jnp.int32)


def whole_block(array):
    return pl.BlockSpec(array.shape, lambda i, *_: (0,) * array.ndim)


def attend(queries, kv, place, rows=512, depth=1024, parts=2):
    starts, ends, query_seg, key_seg, key_base = place
    count, key_rows = queries.shape[0], kv.shape[0]
    lo, hi = bounds(starts, ends, key_base, rows, depth, key_rows)
    key_seg = key_seg.reshape(key_rows // depth, 1, depth)

    def row(width):
        return pl.BlockSpec((rows, width), lambda i, *_: (i, 0))

    return pl.pallas_call(
        functools.partial(attend_kernel, depth=depth, parts=parts),
        grid_spec=pltpu.PrefetchScalarGridSpec(
            num_scalar_prefetch=2,
            grid=(count // rows,),
            in_specs=[row(HEAD), whole_block(kv), row(1), whole_block(key_seg)],
            out_specs=[row(HEAD), row(HEAD), row(1)],
        ),
        out_shape=[
            jax.ShapeDtypeStruct((count, HEAD), LOW),
            jax.ShapeDtypeStruct((count, HEAD), WIDE),
            jax.ShapeDtypeStruct((count, 1), WIDE),
        ],
        compiler_params=pltpu.CompilerParams(vmem_limit_bytes=50 * 2**20),
        cost_estimate=pl.CostEstimate(
            flops=4 * count * LONGEST * HEAD, bytes_accessed=16 * 2**20, transcendentals=count * LONGEST
        ),
        name="attend",
    )(lo, hi, queries, kv, query_seg.reshape(count, 1), key_seg)


def attend_back_kernel(
    lo_ref, hi_ref, q_ref, do_ref, kv_ref, sq_ref, sk_ref, lse_ref, dl_ref, dq_ref, dkv_ref, *, depth
):
    i = pl.program_id(0)

    @pl.when(i == 0)
    def _():
        dkv_ref[...] = jnp.zeros_like(dkv_ref)

    queries = q_ref[...]
    upstream = do_ref[...]
    query_seg, lse, delta = sq_ref[0], lse_ref[0], dl_ref[0]
    dq_ref[...] = jnp.zeros_like(dq_ref)

    def step(t, unused):
        span = pl.ds(pl.multiple_of(t * depth, depth), depth)
        keys = kv_ref[span, :HEAD]
        values = kv_ref[span, HEAD:]
        scores = dot_nt(keys, queries) * SCALE
        probs = jnp.where(sk_ref[span, :] == query_seg, jnp.exp(scores - lse), 0.0)
        grad_probs = dot_nt(values, upstream)
        grad_scores = (probs * (grad_probs - delta)).astype(LOW)
        dkv_ref[span, HEAD:] += dot(probs.astype(LOW), upstream)
        dkv_ref[span, :HEAD] += dot(grad_scores, queries)
        dq_ref[...] += dot_tn(grad_scores, keys)
        return unused

    lax.fori_loop(lo_ref[i], hi_ref[i], step, 0)


def attend_back(queries, upstream, kv, place, lse, delta, rows=512, depth=512):
    starts, ends, query_seg, key_seg, key_base = place
    count, key_rows = queries.shape[0], kv.shape[0]
    lo, hi = bounds(starts, ends, key_base, rows, depth, key_rows)
    key_seg = key_seg.reshape(key_rows, 1)
    row = pl.BlockSpec((rows, HEAD), lambda i, *_: (i, 0))
    lane = pl.BlockSpec((1, 1, rows), lambda i, *_: (i, 0, 0))

    def lanes(vector):
        return vector.reshape(count // rows, 1, rows)

    grad_kv = jax.ShapeDtypeStruct((key_rows, 2 * HEAD), WIDE)
    return pl.pallas_call(
        functools.partial(attend_back_kernel, depth=depth),
        grid_spec=pltpu.PrefetchScalarGridSpec(
            num_scalar_prefetch=2,
            grid=(count // rows,),
            in_specs=[row, row, whole_block(kv), lane, whole_block(key_seg), lane, lane],
            out_specs=[row, whole_block(grad_kv)],
        ),
        out_shape=[jax.ShapeDtypeStruct((count, HEAD), WIDE), grad_kv],
        compiler_params=pltpu.CompilerParams(vmem_limit_bytes=56 * 2**20),
        cost_estimate=pl.CostEstimate(
            flops=10 * count * LONGEST * HEAD, bytes_accessed=32 * 2**20, transcendentals=count * LONGEST
        ),
        name="attend_back",
    )(lo, hi, queries, upstream, kv, lanes(query_seg), key_seg, lanes(lse), lanes(delta))


def on_device(
    acoustic_features,
    clip_durations,
    early_layernorm_scale,
    early_widening_matrix,
    early_narrowing_matrix,
    mixer_layernorm_scale,
    triple_matrix,
    mixer_exit_matrix,
    filter_layernorm_scale,
    gating_pair_matrix,
    depthwise_filter,
    running_stats_factor,
    running_stats_offset,
    filter_exit_projection,
    later_layernorm_scale,
    later_widening_matrix,
    later_narrowing_matrix,
    last_layernorm_scale,
    quantizer_projection,
    entry_vectors,
    smoothing_level,
    random_flat_samples,
    expected_entries,
    result_adjoint,
    discrete_adjoint,
):
    seq_count, mp_count = lax.axis_size("seq"), lax.axis_size("mp")
    seq_at, mp_at = lax.axis_index("seq"), lax.axis_index("mp")
    core = seq_at % 2
    frame_rows = acoustic_features.shape[0]
    all_rows = frame_rows * seq_count
    own = frame_rows // mp_count
    own_base = seq_at * frame_rows + mp_at * own

    def rel_rows(array, k):
        return cut(array, mp_place(k) * own, own)

    def halves_of(array, width, k):
        half = width // 2
        return [cut(array, mp_place(k) * width + (core ^ j) * half, half, 1) for j in range(2)]

    def local_halves(array):
        half = array.shape[1] // 2
        return [cut(array, (core ^ j) * half, half, 1) for j in range(2)]

    exit_all = whole_of(mixer_exit_matrix, 0)
    gating_all = whole_of(gating_pair_matrix, 2)
    point_all = whole_of(filter_exit_projection, 0)
    small_weights = jnp.concatenate(
        [depthwise_filter, running_stats_factor[None], running_stats_offset[None]], 0
    )
    small_all = joined(from_mp(small_weights), 1)
    filter_all, factor_all, offset_all = small_all[:KERNEL], small_all[KERNEL], small_all[KERNEL + 1]
    up_other = fetched(later_widening_matrix, 1)
    down_other = fetched(later_narrowing_matrix, 0)
    book_all = whole_of(entry_vectors, 0)

    first = []
    for k in list(range(1, mp_count)) + [0]:
        rows = rel_rows(acoustic_features, k).astype(WIDE)
        entered, normed, inverse = norm_forward(rows, early_layernorm_scale)
        hidden = dot(entered, early_widening_matrix)
        activated = (hidden * jax.nn.sigmoid(hidden)).astype(LOW)
        part = dot(activated, early_narrowing_matrix)
        first.append((part, entered, hidden, activated, normed, inverse))
    first = [first[-1]] + first[:-1]
    features = rel_rows(acoustic_features, 0).astype(WIDE)
    after_ffn = features + 0.5 * to_mp([f[0] for f in first])

    local_heads = triple_matrix.shape[2] // HEAD
    group_rows = local_heads * frame_rows
    group_at = seq_at // local_heads
    groups = [
        [(z * local_heads + g) * mp_count + m for g in range(local_heads) for m in range(mp_count)]
        for z in range(seq_count // local_heads)
    ]
    att_entered, att_normed, att_inverse = norm_forward(after_ffn, mixer_layernorm_scale)
    att_group = lax.all_gather(att_entered, BOTH, axis_index_groups=groups, axis=0, tiled=True)
    head_matrix = cut(triple_matrix, (seq_at % local_heads) * HEAD, HEAD, 2)
    head_matrix = jnp.transpose(head_matrix, (1, 0, 2)).reshape(D, 3 * HEAD)
    projected = dot(att_group, head_matrix)
    reaches = range(1, -(-(LONGEST - 1) // group_rows) + 1)
    halo = [min(group_rows, -(-(LONGEST - (r - 1) * group_rows) // 1024) * 1024) for r in reaches]
    halo_rows = sum(halo)
    key_base = group_at * group_rows - halo_rows
    key_index = key_base + jnp.arange(group_rows + 2 * halo_rows, dtype=jnp.int32)
    key_seg, key_start, key_end = clip_of(clip_durations, key_index)
    key_seg = jnp.where(jnp.logical_and(key_index >= 0, key_index < all_rows), key_seg, -1)
    middle = slice(halo_rows, halo_rows + group_rows)
    group_pos = key_index[middle] - key_start[middle]
    place = (key_start[middle], key_end[middle], key_seg[middle], key_seg, key_base)
    query_rot = rotary(projected[:, :HEAD], group_pos, 1.0).astype(LOW)
    key_rot = rotary(projected[:, HEAD : 2 * HEAD], group_pos, 1.0).astype(LOW)
    kv_own = jnp.concatenate([key_rot, projected[:, 2 * HEAD :].astype(LOW)], 1)
    lower = [seq_shift(kv_own[group_rows - n :], local_heads * r) for r, n in zip(reaches, halo)]
    upper = [seq_shift(kv_own[:n], -local_heads * r) for r, n in zip(reaches, halo)]
    kv = jnp.concatenate(lower[::-1] + [kv_own] + upper, 0)
    mixed_low, mixed, row_lse = attend(query_rot, kv, place)

    def exchange(array):
        return lax.all_to_all(array, BOTH, 0, 0, axis_index_groups=groups)

    att_parts = exchange(mixed_low.reshape(local_heads * mp_count, own, HEAD))
    att_low = jnp.transpose(
        att_parts.reshape(local_heads, mp_count, own, HEAD), (2, 1, 0, 3)
    ).reshape(own, D)
    after_att = after_ffn + dot(att_low, exit_all)

    half_kernel = KERNEL // 2
    pad_index = own_base - half_kernel + jnp.arange(own + 2 * half_kernel, dtype=jnp.int32)
    pad_seg = clip_of(clip_durations, pad_index)[0]
    pad_seg = jnp.where(jnp.logical_and(pad_index >= 0, pad_index < all_rows), pad_seg, -1)
    own_seg = pad_seg[half_kernel : half_kernel + own]
    masks = [(pad_seg[j : j + own] == own_seg)[:, None] for j in range(KERNEL)]

    def padded(block):
        low = flat_shift(block[own - half_kernel :], 1)
        high = flat_shift(block[:half_kernel], -1)
        return jnp.concatenate([low, block, high], 0).astype(WIDE)

    conv_entered, conv_normed, conv_inverse = norm_forward(after_att, filter_layernorm_scale)
    glu_value = dot(conv_entered, gating_all[0])
    glu_gate = jax.nn.sigmoid(dot(conv_entered, gating_all[1]))
    glu_low = (glu_value * glu_gate).astype(LOW)
    glu_padded = padded(glu_low)
    conv_out = jnp.zeros((own, D), WIDE)
    for j in range(KERNEL):
        conv_out = conv_out + filter_all[j][None, :] * jnp.where(masks[j], glu_padded[j : j + own], 0.0)
    sums = lax.psum(jnp.stack([jnp.sum(conv_out, 0), jnp.sum(conv_out * conv_out, 0)]), BOTH)
    bn_mean = sums[0] / all_rows
    bn_inv = lax.rsqrt(sums[1] / all_rows - bn_mean * bn_mean + EPSILON)
    bn_hat = (conv_out - bn_mean) * bn_inv
    bn_out = bn_hat * factor_all + offset_all
    bn_sigma = jax.nn.sigmoid(bn_out)
    swish_low = (bn_out * bn_sigma).astype(LOW)
    after_conv = after_att + dot(swish_low, point_all)

    late_entered, late_normed, late_inverse = norm_forward(after_conv, later_layernorm_scale)
    ups = [later_widening_matrix] + [part for pair in up_other for part in pair]
    downs = [later_narrowing_matrix] + [part for pair in down_other for part in pair]
    late_hidden, late_act = [], []
    branch = 0.0
    for w_in, w_back in zip(ups, downs):
        hidden = dot(late_entered, w_in)
        activated = (hidden * jax.nn.sigmoid(hidden)).astype(LOW)
        branch = branch + dot(activated, w_back)
        late_hidden.append(hidden)
        late_act.append(activated)
    after_two = after_conv + 0.5 * branch
    final_low, final_normed, final_inverse = norm_forward(after_two, last_layernorm_scale)
    layer_out = joined(from_mp(final_low))

    codes = book_all.shape[0]
    logits = dot_nt(final_low, book_all) * D ** (-0.5)
    is_target = rel_rows(expected_entries, 0)[:, None] == jnp.arange(codes, dtype=jnp.int32)[None, :]
    pred_lse = jax.nn.logsumexp(logits, -1)
    row_loss = pred_lse - jnp.sum(jnp.where(is_target, logits, 0.0), -1)
    frame_loss = joined(from_mp(row_loss))
    grad_pred = (jnp.exp(logits - pred_lse[:, None]) - is_target.astype(WIDE)).astype(LOW)
    grad_final = rel_rows(result_adjoint, 0).astype(WIDE) + dot(grad_pred, book_all) * D ** (-0.5)
    own_codes = entry_vectors.shape[0]
    book_pieces = [
        [dot_tn(part, final_low) * D ** (-0.5) for part in halves_of(grad_pred, own_codes, k)]
        for k in range(mp_count)
    ]

    temper = smoothing_level[0]
    noisy = dot(acoustic_features, quantizer_projection) - jnp.log(-jnp.log(random_flat_samples))
    tempered = noisy / temper
    top = jnp.max(tempered, -1)
    total = jnp.sum(jnp.exp(tempered - top[:, None]), -1)
    stats = from_mp(jnp.stack([top, total]))
    full_top = functools.reduce(jnp.maximum, [s[0] for s in stats])
    full_total = sum(s[1] * jnp.exp(s[0] - full_top) for s in stats)
    assigned = jnp.exp(tempered - (full_top + jnp.log(full_total))[:, None])
    assigned_low = assigned.astype(LOW)
    quant_own = to_mp([dot(rel_rows(assigned_low, k), entry_vectors) for k in range(mp_count)])
    quantized = joined(from_mp(quant_own.astype(LOW)))
    grad_soft = dot_nt(discrete_adjoint, entry_vectors)
    row_dot = sum(from_mp(jnp.sum(assigned * grad_soft, -1)))
    grad_tempered = assigned * (grad_soft - row_dot[:, None])
    grad_temper = -jnp.sum(grad_tempered * noisy) / (temper * temper)
    grad_entry = (grad_tempered / temper).astype(LOW)
    quant_in = to_mp([dot_nt(rel_rows(grad_entry, k), quantizer_projection) for k in range(mp_count)])
    code_grad = summed_grad([[dot_tn(acoustic_features, p) for p in local_halves(grad_entry)]], True)
    soft_halves = [dot_tn(p, discrete_adjoint) for p in local_halves(assigned_low)]
    book_pieces[0] = [a + b for a, b in zip(book_pieces[0], soft_halves)]
    book_grad = summed_grad(book_pieces, False)

    grad_four, grad_ln_final = norm_backward(grad_final, last_layernorm_scale, final_normed, final_inverse)
    late_branch = (0.5 * grad_four).astype(LOW)
    late_in = 0.0
    grad_hidden = []
    for w_in, w_back, hidden in zip(ups, downs, late_hidden):
        grad_act = dot_nt(late_branch, w_back)
        grad_hid = (grad_act * silu_slope(hidden, jax.nn.sigmoid(hidden))).astype(LOW)
        grad_hidden.append(grad_hid)
        late_in = late_in + dot_nt(grad_hid, w_in)

    def pieced(parts):
        flat = local_halves(parts[0]) + parts[1:]
        return [flat[2 * k : 2 * k + 2] for k in range(mp_count)]

    down2_grad = summed_grad([[dot_tn(p, late_branch) for p in pair] for pair in pieced(late_act)], False)
    up2_grad = summed_grad([[dot_tn(late_entered, p) for p in pair] for pair in pieced(grad_hidden)], True)
    late_norm_grad, grad_ln_ffn2 = norm_backward(late_in, later_layernorm_scale, late_normed, late_inverse)
    grad_three = grad_four + late_norm_grad

    conv_branch = grad_three.astype(LOW)
    own_channels = filter_exit_projection.shape[0]
    point_grad = summed_grad(
        [[dot_tn(p, conv_branch) for p in halves_of(swish_low, own_channels, k)] for k in range(mp_count)], False
    )
    grad_swish = dot_nt(conv_branch, point_all)
    grad_bn = grad_swish * silu_slope(bn_out, bn_sigma)
    back_sums = lax.psum(jnp.stack([jnp.sum(grad_bn, 0), jnp.sum(grad_bn * bn_hat, 0)]), BOTH)
    grad_conv = (
        factor_all * bn_inv * (grad_bn - back_sums[0] / all_rows - bn_hat * back_sums[1] / all_rows)
    ).astype(LOW)
    grad_padded = padded(grad_conv)
    grad_exact = grad_conv.astype(WIDE)
    grad_taps = []
    grad_gated = jnp.zeros_like(grad_exact)
    for j in range(KERNEL):
        grad_taps.append(jnp.sum(grad_exact * jnp.where(masks[j], glu_padded[j : j + own], 0.0), 0))
        back = 2 * half_kernel - j
        grad_gated = grad_gated + filter_all[j][None, :] * jnp.where(
            masks[back], grad_padded[back : back + own], 0.0
        )
    grad_value = (grad_gated * glu_gate).astype(LOW)
    grad_gate = (grad_gated * glu_value * glu_gate * (1.0 - glu_gate)).astype(LOW)
    gate_grads = [
        summed_grad(
            [[dot_tn(conv_entered, p) for p in halves_of(g, own_channels, k)] for k in range(mp_count)], True
        )
        for g in (grad_value, grad_gate)
    ]
    conv_in = dot_nt(grad_value, gating_all[0]) + dot_nt(grad_gate, gating_all[1])
    conv_norm_grad, grad_ln_conv = norm_backward(conv_in, filter_layernorm_scale, conv_normed, conv_inverse)
    grad_two = grad_three + conv_norm_grad

    att_branch = grad_two.astype(LOW)
    exit_grad = summed_grad(
        [
            [dot_tn(p, att_branch) for p in halves_of(att_low, local_heads * HEAD, k)]
            for k in range(mp_count)
        ],
        False,
    )
    grad_heads = dot_nt(att_branch, exit_all).astype(LOW)
    grad_heads = jnp.transpose(
        grad_heads.reshape(own, mp_count, local_heads, HEAD), (2, 1, 0, 3)
    ).reshape(local_heads * mp_count, own, HEAD)
    grad_mixed = exchange(grad_heads).reshape(group_rows, HEAD)
    delta = jnp.sum(grad_mixed.astype(WIDE) * mixed, -1)
    grad_query, grad_kv = attend_back(query_rot, grad_mixed, kv, place, row_lse, delta)
    kv_grad = grad_kv[middle]
    edge = halo_rows
    for r, n in zip(reaches, halo):
        edge -= n
        back = seq_shift(grad_kv[edge : edge + n].astype(LOW), -local_heads * r)
        kv_grad = kv_grad.at[group_rows - n :].add(back.astype(WIDE))
    edge = halo_rows + group_rows
    for r, n in zip(reaches, halo):
        back = seq_shift(grad_kv[edge : edge + n].astype(LOW), local_heads * r)
        kv_grad = kv_grad.at[:n].add(back.astype(WIDE))
        edge += n
    grad_proj = jnp.concatenate(
        [
            rotary(grad_query * SCALE, group_pos, -1.0).astype(LOW),
            rotary(kv_grad[:, :HEAD] * SCALE, group_pos, -1.0).astype(LOW),
            kv_grad[:, HEAD:].astype(LOW),
        ],
        1,
    )
    head_grad = halved(dot_tn(att_group, grad_proj).astype(LOW), int(math.log2(local_heads)))
    head_every = lax.all_gather(head_grad, "seq", axis=0)
    bits = int(math.log2(seq_count))
    low_bits = int(math.log2(local_heads))
    head_rows = head_grad.shape[0]
    head_every = head_every.reshape([2] * (bits - low_bits) + [local_heads, head_rows, 3, HEAD])
    outer = bits - low_bits
    head_every = jnp.transpose(
        head_every, [outer + 2] + list(range(outer))[::-1] + [outer + 1, outer, outer + 3]
    )
    qkv_grad = head_every.reshape(3, D, local_heads * HEAD).astype(WIDE)

    blocks = grad_proj.reshape(local_heads, mp_count, own, 3 * HEAD)
    if local_heads > 1:
        split = blocks.reshape(local_heads // 2, 2, mp_count, own, 3 * HEAD)
        sides = [
            dot_nt(cut(split, core ^ j, 1, 1).reshape(-1, 3 * HEAD), head_matrix).astype(LOW) for j in range(2)
        ]
        held = sides[0] + seq_xor(sides[1], 1)
        outer_count = local_heads // 2
    else:
        held = dot_nt(grad_proj, head_matrix).astype(LOW)
        outer_count = 1
    held = held.reshape(outer_count, mp_count, own, D)
    att_in = 0.0
    outer_at = (seq_at % local_heads) // 2 if local_heads > 1 else 0
    for mask in range(outer_count):
        for k in range(mp_count):
            term = lax.dynamic_slice(held, (outer_at ^ mask, mp_place(k), 0, 0), (1, 1, own, D))[0, 0]
            if mask or k:
                pairs = [
                    (s * mp_count + m, (s ^ (2 * mask)) * mp_count + (m + k) % mp_count)
                    for s in range(seq_count)
                    for m in range(mp_count)
                ]
                term = lax.ppermute(term, BOTH, pairs)
            att_in = att_in + term.astype(WIDE)
    att_norm_grad, grad_ln_att = norm_backward(att_in, mixer_layernorm_scale, att_normed, att_inverse)
    grad_one = grad_two + att_norm_grad

    early_branch = from_mp((0.5 * grad_one).astype(LOW))
    early_in, early_grads = [], []
    for k, (_, entered, hidden, activated, _, _) in enumerate(first):
        grad_act = dot_nt(early_branch[k], early_narrowing_matrix)
        early_grads.append((grad_act * silu_slope(hidden, jax.nn.sigmoid(hidden))).astype(LOW))
        early_in.append(dot_nt(early_grads[k], early_widening_matrix))

    def stacked(parts):
        return jnp.concatenate(parts, 0)

    act_all, branch_all = stacked([f[3] for f in first]), stacked(early_branch)
    entered_all, hid_all = stacked([f[1] for f in first]), stacked(early_grads)
    down1_grad = summed_grad([[dot_tn(p, branch_all) for p in local_halves(act_all)]], False)
    up1_grad = summed_grad([[dot_tn(entered_all, p) for p in local_halves(hid_all)]], True)
    early_norm_grad, grad_ln_ffn1 = norm_backward(to_mp(early_in), early_layernorm_scale, first[0][4], first[0][5])
    grad_frames = joined(from_mp((grad_one + early_norm_grad + quant_in).astype(LOW)))

    small = lax.psum(
        jnp.concatenate(
            [grad_ln_ffn1, grad_ln_att, grad_ln_conv, grad_ln_ffn2, grad_ln_final]
            + grad_taps
            + [jnp.full((D,), grad_temper, WIDE)]
        ),
        BOTH,
    ).reshape(-1, D)

    def own_part(array):
        return cut(array, mp_at * own_channels, own_channels, array.ndim - 1)

    return (
        layer_out,
        quantized,
        frame_loss,
        grad_frames,
        small[0],
        up1_grad,
        down1_grad,
        small[1],
        qkv_grad,
        exit_grad,
        small[2],
        jnp.stack(gate_grads),
        own_part(small[5 : 5 + KERNEL]),
        own_part(back_sums[1]),
        own_part(back_sums[0]),
        point_grad,
        small[3],
        up2_grad,
        down2_grad,
        small[4],
        code_grad,
        book_grad,
        small[5 + KERNEL, :1],
    )


def solution(mesh):
    in_specs = (
        P("seq", None),
        P(),
        P(),
        P(None, "mp"),
        P("mp", None),
        P(),
        P(None, None, "mp"),
        P("mp", None),
        P(),
        P(None, None, "mp"),
        P(None, "mp"),
        P("mp"),
        P("mp"),
        P("mp", None),
        P(),
        P(None, "mp"),
        P("mp", None),
        P(),
        P(None, "mp"),
        P("mp", None),
        P(),
        P("seq", "mp"),
        P("seq"),
        P("seq", None),
        P("seq", None),
    )
    out_specs = (
        P("seq", None),
        P("seq", None),
        P("seq"),
        P("seq", None),
        P(),
        P(None, "mp"),
        P("mp", None),
        P(),
        P(None, None, "mp"),
        P("mp", None),
        P(),
        P(None, None, "mp"),
        P(None, "mp"),
        P("mp"),
        P("mp"),
        P("mp", None),
        P(),
        P(None, "mp"),
        P("mp", None),
        P(),
        P(None, "mp"),
        P("mp", None),
        P(),
    )
    return jax.shard_map(
        on_device, mesh=mesh, in_specs=in_specs, out_specs=out_specs, check_vma=False
    )
```

```python
import functools
import math

import jax
import jax.numpy as jnp
from jax import lax
from jax.experimental import pallas as pl
from jax.experimental.pallas import tpu as pltpu
from jax.sharding import PartitionSpec as P

D = 1024
HEAD = 128
KERNEL = 5
LONGEST = 3008

EPSILON = 1e-05
MASKED = -1e30
SCALE = HEAD ** (-0.5)
SCALE_2 = SCALE * math.log2(math.e)
BOTH = ("seq", "mp")
LOW = jnp.bfloat16
WIDE = jnp.float32


def dot(a, b, dims=((1,), (0,))):
    return lax.dot_general(a, b, (dims, ((), ())), preferred_element_type=WIDE)


def dot_nt(a, b):
    return dot(a, b, ((1,), (1,)))


def dot_tn(a, b):
    return dot(a, b, ((0,), (0,)))


def cut(array, start, size, axis=0):
    return lax.dynamic_slice_in_dim(array, start, size, axis)


def mp_shift(shard, by):
    count = lax.axis_size("mp")
    return lax.ppermute(shard, "mp", [(i, (i + by) % count) for i in range(count)])


def seq_xor(shard, mask):
    return lax.ppermute(shard, "seq", [(i, i ^ mask) for i in range(lax.axis_size("seq"))])


def seq_shift(shard, by):
    count = lax.axis_size("seq")
    return lax.ppermute(shard, "seq", [(i, i + by) for i in range(count) if 0 <= i + by < count])


def flat_shift(shard, by):
    count = lax.axis_size("seq") * lax.axis_size("mp")
    return lax.ppermute(shard, BOTH, [(i, i + by) for i in range(count) if 0 <= i + by < count])


def from_mp(shard):
    return [shard] + [mp_shift(shard, -k) for k in range(1, lax.axis_size("mp"))]


def to_mp(parts):
    total = parts[0].astype(WIDE)
    for k in range(1, len(parts)):
        total = total + mp_shift(parts[k].astype(LOW), k).astype(WIDE)
    return total


def mp_place(k):
    return (lax.axis_index("mp") + k) % lax.axis_size("mp")


def joined(pieces, axis=0):
    size = pieces[0].shape[axis]
    shape = list(pieces[0].shape)
    shape[axis] = size * len(pieces)
    whole = jnp.zeros(shape, pieces[0].dtype)
    for k, piece in enumerate(pieces):
        whole = lax.dynamic_update_slice_in_dim(whole, piece, mp_place(k) * size, axis)
    return whole


def halved(part, bit):
    half = part.shape[1] // 2
    side = (lax.axis_index("seq") >> bit) & 1
    sent = seq_xor(cut(part, (1 - side) * half, half, 1), 1 << bit)
    return cut(part, side * half, half, 1) + sent


def paced(*values):
    return lax.optimization_barrier(values)


def bit_count(number):
    return int(math.log2(number))


def reversed_bits(number, bits):
    out = 0
    for b in range(bits):
        out = out + (((number >> b) & 1) << (bits - 1 - b))
    return out


def laid_kernel(in_ref, out_ref, *, places, turned):
    _, _, rows, width = in_ref.shape
    for s, place in enumerate(places):
        block = in_ref[s, 0].astype(WIDE)
        span = slice(place * rows, (place + 1) * rows)
        if turned:
            out_ref[0, :, span] = block.T
        else:
            out_ref[0, span, :] = block


def laid(every, first, amount, local_heads, turned, width=256):
    count, _, rows, columns = every.shape
    line = count // local_heads
    bits = bit_count(line)
    places = [
        part_of(s % local_heads, local_heads) * line + reversed_bits(s // local_heads, bits) for s in range(count)
    ]
    if count * rows % 128:
        order = sorted(range(count), key=lambda s: places[s])
        whole = jnp.stack([every[s, first : first + amount] for s in order], 1).astype(WIDE)
        whole = whole.reshape(amount, count * rows, columns)
        return jnp.transpose(whole, (0, 2, 1)) if turned else whole
    shape = (columns, count * rows) if turned else (count * rows, columns)
    block = (1, width, count * rows) if turned else (1, count * rows, width)
    return pl.pallas_call(
        functools.partial(laid_kernel, places=places, turned=turned),
        grid=(amount, columns // width),
        in_specs=[pl.BlockSpec((count, 1, rows, width), lambda i, j: (0, first + i, 0, j))],
        out_specs=pl.BlockSpec(block, lambda i, j: (i, j, 0) if turned else (i, 0, j)),
        out_shape=jax.ShapeDtypeStruct((amount,) + shape, WIDE),
        compiler_params=pltpu.CompilerParams(vmem_limit_bytes=32 * 2**20),
        cost_estimate=pl.CostEstimate(
            flops=0, bytes_accessed=6 * amount * shape[0] * shape[1], transcendentals=0
        ),
        name="laid",
    )(every)


def laid_heads_kernel(in_ref, out_ref, *, local_heads, bits):
    rows = in_ref.shape[1]
    for s in range(in_ref.shape[0]):
        block = reversed_bits(s // local_heads, bits)
        head = part_of(s % local_heads, local_heads)
        out_ref[0, block * rows : (block + 1) * rows, head * HEAD : (head + 1) * HEAD] = in_ref[s].astype(WIDE)


def laid_heads(every, local_heads):
    count, rows, _ = every.shape
    shape = (D, local_heads * HEAD)
    return pl.pallas_call(
        functools.partial(
            laid_heads_kernel, local_heads=local_heads, bits=bit_count(count) - bit_count(local_heads)
        ),
        grid=(3,),
        in_specs=[pl.BlockSpec((count, rows, HEAD), lambda i: (0, 0, i))],
        out_specs=pl.BlockSpec((1,) + shape, lambda i: (i, 0, 0)),
        out_shape=jax.ShapeDtypeStruct((3,) + shape, WIDE),
        compiler_params=pltpu.CompilerParams(vmem_limit_bytes=32 * 2**20),
        cost_estimate=pl.CostEstimate(flops=0, bytes_accessed=18 * D * local_heads * HEAD, transcendentals=0),
        name="laid_heads",
    )(every)


def beside_kernel(in_ref, out_ref):
    out_ref[...] = in_ref[0].astype(WIDE)


def beside(halves, down, rows=1024):
    _, height, width = halves.shape
    rows = min(rows, height)
    steps = height // rows
    shape = (2 * height, width) if down else (height, 2 * width)

    def target(j, i):
        return (j * steps + i, 0) if down else (i, j)

    return pl.pallas_call(
        beside_kernel,
        grid=(2, steps),
        in_specs=[pl.BlockSpec((1, rows, width), lambda j, i: (j, i, 0))],
        out_specs=pl.BlockSpec((rows, width), target),
        out_shape=jax.ShapeDtypeStruct(shape, WIDE),
        compiler_params=pltpu.CompilerParams(vmem_limit_bytes=32 * 2**20),
        cost_estimate=pl.CostEstimate(flops=0, bytes_accessed=12 * height * width, transcendentals=0),
        name="beside",
    )(halves)


def remote(source, target, send, recv, device):
    return pltpu.make_async_remote_copy(
        src_ref=source,
        dst_ref=target,
        send_sem=send,
        recv_sem=recv,
        device_id=device,
        device_id_type=pl.DeviceIdType.MESH,
    )


def seq_partner(bit):
    return (lax.axis_index("seq") ^ (1 << bit), lax.axis_index("mp"))


def all_partners(seq_bits, mp_bits):
    mp = lax.axis_index("mp")
    across = [(lax.axis_index("seq"), mp ^ (1 << bit)) for bit in range(mp_bits)]
    return across + [seq_partner(bit) for bit in range(seq_bits)]


def meet(partners):
    barrier = pltpu.get_barrier_semaphore()
    for device in partners:
        pl.semaphore_signal(barrier, inc=1, device_id=device, device_id_type=pl.DeviceIdType.MESH)
    pl.semaphore_wait(barrier, len(partners))


class Small:
    def __init__(self, held, slots, send, recv, partners):
        self.held, self.slots, self.send, self.recv, self.partners = held, slots, send, recv, partners
        self.at = 0

    def copy(self, k):
        return remote(self.held.at[k], self.slots.at[k], self.send.at[k], self.recv.at[k], self.partners[k])

    def advance(self):
        k = self.at
        if k > len(self.partners):
            return
        if k > 0:
            self.copy(k - 1).wait_recv()
            self.held[k] = self.held[k - 1] + self.slots[k - 1]
        if k < len(self.partners):
            self.copy(k).start()
        self.at += 1

    def finish(self, out):
        while self.at <= len(self.partners):
            self.advance()
        for k in range(len(self.partners)):
            self.copy(k).wait_send()
        out[...] = self.held[len(self.partners)]


def small_scratch(shape, steps):
    dma = pltpu.SemaphoreType.DMA
    return [pltpu.VMEM((steps + 1,) + shape, WIDE), pltpu.VMEM((steps,) + shape, WIDE), dma((steps,)), dma((steps,))]


def total_kernel(in_ref, out_ref, held, slots, send, recv, *, seq_bits, mp_bits):
    partners = all_partners(seq_bits, mp_bits)
    meet(partners)
    held[0] = in_ref[...]
    Small(held, slots, send, recv, partners).finish(out_ref)


def total_over_all(values, collective_id):
    seq_bits, mp_bits = bit_count(lax.axis_size("seq")), bit_count(lax.axis_size("mp"))
    flat = values.reshape(-1, HEAD)
    space = pl.BlockSpec(memory_space=pltpu.VMEM)
    out = pl.pallas_call(
        functools.partial(total_kernel, seq_bits=seq_bits, mp_bits=mp_bits),
        in_specs=[space],
        out_specs=space,
        out_shape=jax.ShapeDtypeStruct(flat.shape, WIDE),
        scratch_shapes=small_scratch(flat.shape, seq_bits + mp_bits),
        compiler_params=pltpu.CompilerParams(collective_id=collective_id, has_side_effects=True),
        name="total_over_all",
    )(flat)
    return out.reshape(values.shape)


def seq_total_kernel(small_ref, *refs, count, chunks, seq_bits, mp_bits, share_count):
    shares, refs = refs[:share_count], refs[share_count:]
    mine, other = refs[:count], refs[count : 2 * count]
    small_out, refs = refs[2 * count], refs[2 * count + 1 :]
    shared, refs = refs[:share_count], refs[share_count:]
    outs, scratch = refs[:count], refs[count:]
    (share_local, share_send, share_recv), scratch = scratch[:3], scratch[3:]
    arrived, held = scratch[:count], scratch[count : 2 * count]
    levels = seq_bits - 1
    slots = [scratch[(2 + i) * count : (3 + i) * count] for i in range(levels)]
    core_send, core_recv, back_core_send, back_core_recv, send, recv, back_send, back_recv = scratch[
        (2 + levels) * count : (2 + levels) * count + 8
    ]
    partners = all_partners(seq_bits, mp_bits)
    mp, mp_count = lax.axis_index("mp"), 1 << mp_bits
    along_mp = [(lax.axis_index("seq"), (mp + k) % mp_count) for k in range(1, mp_count)]
    meet(along_mp + partners[mp_bits:])

    def share_rows(i, index):
        rows = shares[i].shape[0]
        return shared[i].at[pl.ds(pl.multiple_of(index * rows, 16), rows)]

    def share_copy(i, k, index):
        return remote(
            shares[i], share_rows(i, index), share_send.at[i, k - 1], share_recv.at[i, k - 1], along_mp[k - 1]
        )

    def share_own(i):
        return pltpu.make_async_copy(shares[i], share_rows(i, mp), share_local.at[i])

    for i in range(share_count):
        share_own(i).start()
        for k in range(1, mp_count):
            share_copy(i, k, mp).start()
    small = Small(*scratch[(2 + levels) * count + 8 :], partners)
    small.held[0] = small_ref[...]
    seq = lax.axis_index("seq")
    core, sibling = seq % 2, seq_partner(0)

    plan = []
    for a in range(count):
        rows = mine[a].shape[0] // chunks[a]
        plan += [(a, c * rows, rows) for c in range(chunks[a])]
    everything = range(len(plan))

    def base(n, level):
        first, rows = plan[n][1:]
        for bit in range(1, level + 1):
            first = first + ((seq >> bit) & 1) * (rows >> bit)
        return first

    def span(n, level, kept):
        side = (seq >> level) & 1
        size = plan[n][2] >> level
        first = base(n, level - 1) + (side if kept else 1 - side) * size
        return pl.ds(pl.multiple_of(first, 16), size)

    def slot(n, level):
        return pl.ds(plan[n][1] >> level, plan[n][2] >> level)

    def whole(n):
        return pl.ds(plan[n][1], plan[n][2])

    def core_copy(n):
        a = plan[n][0]
        return remote(other[a].at[whole(n)], arrived[a].at[whole(n)], core_send.at[n], core_recv.at[n], sibling)

    def copy(n, level):
        a = plan[n][0]
        return remote(
            held[a].at[span(n, level, False)],
            slots[level - 1][a].at[slot(n, level)],
            send.at[n, level - 1],
            recv.at[n, level - 1],
            seq_partner(level),
        )

    def back_copy(n, level, arriving):
        rows = outs[plan[n][0]].at[core, span(n, level, not arriving)]
        return remote(rows, rows, back_send.at[n, level - 1], back_recv.at[n, level - 1], seq_partner(level))

    def back_core_copy(n, arriving):
        rows = outs[plan[n][0]].at[1 - core if arriving else core, whole(n)]
        return remote(rows, rows, back_core_send.at[n], back_core_recv.at[n], sibling)

    def fold(n, level):
        a = plan[n][0]
        copy(n, level).wait_recv()
        kept = span(n, level, True)
        total = held[a][kept, :].astype(WIDE) + slots[level - 1][a][slot(n, level), :].astype(WIDE)
        if level < levels:
            held[a][kept, :] = total.astype(LOW)
            copy(n, level + 1).start()
        else:
            outs[a][core, kept, :] = total.astype(LOW)
            back_copy(n, level, False).start()

    def unfold(n, level):
        back_copy(n, level, True).wait_recv()
        back_copy(n, level - 1, False).start()

    small.advance()
    for n in everything:
        core_copy(n).start()
    for n in everything:
        a = plan[n][0]
        core_copy(n).wait_recv()
        held[a][whole(n), :] = (mine[a][whole(n), :].astype(WIDE) + arrived[a][whole(n), :].astype(WIDE)).astype(LOW)
        copy(n, 1).start()
    small.advance()
    stages = [functools.partial(fold, level=level) for level in range(1, levels + 1)]
    stages += [functools.partial(unfold, level=level) for level in range(levels, 1, -1)]
    for t in range(len(plan) + len(stages) - 1):
        for number in reversed(range(len(stages))):
            if 0 <= t - number < len(plan):
                stages[number](t - number)
        small.advance()
    for n in everything:
        back_copy(n, 1, True).wait_recv()
        back_core_copy(n, False).start()
    for n in everything:
        back_core_copy(n, True).wait_recv()
        core_copy(n).wait_send()
        back_core_copy(n, False).wait_send()
        for level in range(1, levels + 1):
            copy(n, level).wait_send()
            back_copy(n, level, False).wait_send()
    small.finish(small_out)
    for i in range(share_count):
        share_own(i).wait()
        for k in range(1, mp_count):
            share_copy(i, k, (mp + mp_count - k) % mp_count).wait_recv()
            share_copy(i, k, mp).wait_send()


def seq_total(shares, mine, other, small, collective_id):
    seq_bits, mp_bits = bit_count(lax.axis_size("seq")), bit_count(lax.axis_size("mp"))
    levels = seq_bits - 1
    chunks = [min(4, max(1, part.shape[0] // (16 << levels))) for part in mine]
    count, total = len(mine), sum(chunks)
    flat = small.reshape(-1, HEAD)
    space, far = pl.BlockSpec(memory_space=pltpu.VMEM), pl.BlockSpec(memory_space=pl.ANY)
    shapes = [part.shape for part in mine]
    dma = pltpu.SemaphoreType.DMA
    out = pl.pallas_call(
        functools.partial(
            seq_total_kernel,
            count=count,
            chunks=chunks,
            seq_bits=seq_bits,
            mp_bits=mp_bits,
            share_count=len(shares),
        ),
        in_specs=[space] + [far] * len(shares) + [space] * (2 * count),
        out_specs=[space] + [far] * len(shares) + [space] * count,
        out_shape=[jax.ShapeDtypeStruct(flat.shape, WIDE)]
        + [jax.ShapeDtypeStruct((part.shape[0] << mp_bits, part.shape[1]), part.dtype) for part in shares]
        + [jax.ShapeDtypeStruct((2,) + shape, LOW) for shape in shapes],
        scratch_shapes=[dma((len(shares),))]
        + [dma((len(shares), max(1, (1 << mp_bits) - 1)))] * 2
        + [pltpu.VMEM(shape, LOW) for shape in shapes] * 2
        + [pltpu.VMEM((rows >> level, width), LOW) for level in range(1, levels + 1) for rows, width in shapes]
        + [dma((total,))] * 4
        + [dma((total, levels))] * 4
        + small_scratch(flat.shape, seq_bits + mp_bits),
        compiler_params=pltpu.CompilerParams(
            collective_id=collective_id, has_side_effects=True, vmem_limit_bytes=56 * 2**20
        ),
        cost_estimate=pl.CostEstimate(flops=10**11, bytes_accessed=32 * 2**20, transcendentals=0),
        name="seq_total",
    )(flat, *shares, *mine, *other)
    return out[0].reshape(small.shape), out[1 : 1 + len(shares)], out[1 + len(shares) :]


def clip_of(clip_durations, positions):
    clip_ends = jnp.cumsum(clip_durations, dtype=jnp.int32)
    passed = clip_ends[None, :] <= positions[:, None]
    segment = jnp.sum(passed.astype(jnp.int32), 1, dtype=jnp.int32)
    starts = jnp.sum(jnp.where(passed, clip_durations[None, :], 0), 1, dtype=jnp.int32)
    ends = jnp.min(jnp.where(passed, 2**30, clip_ends[None, :]), 1)
    return segment, starts, ends


def norm_forward(rows, gain):
    centred = rows - jnp.mean(rows, -1, keepdims=True)
    inverse = lax.rsqrt(jnp.mean(centred * centred, -1, keepdims=True) + EPSILON)
    normed = centred * inverse
    return (normed * gain).astype(LOW), normed, inverse


def norm_backward(upstream, gain, normed, inverse):
    scaled = upstream * gain
    centred = (
        scaled
        - jnp.mean(scaled, -1, keepdims=True)
        - normed * jnp.mean(scaled * normed, -1, keepdims=True)
    )
    return centred * inverse, jnp.sum(upstream * normed, 0)


def part_of(place, count):
    return (place % 2) * (count // 2) + place // 2


def turn_tables(position):
    half_width = HEAD // 2
    frequency = 10000.0 ** (-jnp.arange(half_width, dtype=WIDE) / half_width)
    angles = position.astype(WIDE)[:, None] * frequency[None, :]
    cosine, sine = jnp.cos(angles), jnp.sin(angles)
    return jnp.concatenate([cosine, cosine], 1), jnp.concatenate([-sine, sine], 1)


def swapped(rows):
    return pltpu.roll(rows, HEAD // 2, 1)


def silu_slope(hidden, sigma):
    return sigma * (1.0 + hidden * (1.0 - sigma))


def project_kernel(in_ref, matrix_ref, cos_ref, sin_ref, q_ref, kv_ref):
    out = dot(in_ref[...], matrix_ref[...])
    cosine, sine = cos_ref[...], sin_ref[...]
    queries, keys = out[:, :HEAD], out[:, HEAD : 2 * HEAD]
    q_ref[...] = (queries * cosine + swapped(queries) * sine).astype(LOW)
    kv_ref[:, :HEAD] = (keys * cosine + swapped(keys) * sine).astype(LOW)
    kv_ref[:, HEAD:] = out[:, 2 * HEAD :].astype(LOW)


def project(entered, matrix, tables, rows=512):
    count = entered.shape[0]

    def row(width):
        return pl.BlockSpec((rows, width), lambda i: (i, 0))

    return pl.pallas_call(
        project_kernel,
        grid=(count // rows,),
        in_specs=[row(D), pl.BlockSpec(matrix.shape, lambda i: (0, 0)), row(HEAD), row(HEAD)],
        out_specs=[row(HEAD), row(2 * HEAD)],
        out_shape=[
            jax.ShapeDtypeStruct((count, HEAD), LOW),
            jax.ShapeDtypeStruct((count, 2 * HEAD), LOW),
        ],
        compiler_params=pltpu.CompilerParams(vmem_limit_bytes=32 * 2**20),
        cost_estimate=pl.CostEstimate(
            flops=6 * count * D * HEAD, bytes_accessed=6 * count * D, transcendentals=0
        ),
        name="project",
    )(entered, matrix, *tables)


def gather_keys(pieces, kv_ref):
    @pl.when(pl.program_id(0) == 0)
    def _():
        at = 0
        for piece in pieces:
            kv_ref[at : at + piece.shape[0], :] = piece[...]
            at += piece.shape[0]


def attend_kernel(lo_ref, hi_ref, q_ref, start_ref, end_ref, *rest, count, depth):
    pieces = rest[:count]
    low_ref, mix_ref, lse_ref, kv_ref = rest[count:]
    gather_keys(pieces, kv_ref)
    i = pl.program_id(0)
    queries = q_ref[...]
    rows = queries.shape[0]
    first, last = start_ref[0], end_ref[0]

    def step(t, carry):
        top, total, mixed = carry
        at = pl.multiple_of(t * depth, depth)
        keys = kv_ref[pl.ds(at, depth), :HEAD]
        values = kv_ref[pl.ds(at, depth), HEAD:]
        index = lax.broadcasted_iota(jnp.int32, (depth, 1), 0) + at
        scores = dot_nt(keys, queries) * SCALE_2
        inside = jnp.logical_and(index >= first, index < last)
        scores = jnp.where(inside, scores, MASKED)
        new_top = jnp.maximum(top, jnp.max(scores, 0, keepdims=True))
        probs = jnp.exp2(scores - new_top)
        fade = jnp.exp2(top - new_top)
        total = fade * total + jnp.sum(probs, 0, keepdims=True)
        mixed = fade * mixed + dot_tn(values, probs.astype(LOW))
        return new_top, total, mixed

    start = (jnp.full((1, rows), MASKED, WIDE), jnp.zeros((1, rows), WIDE), jnp.zeros((HEAD, rows), WIDE))
    top, total, mixed = lax.fori_loop(lo_ref[i], hi_ref[i], step, start)
    mixed = jnp.transpose(mixed / total)
    mix_ref[...] = mixed
    low_ref[...] = mixed.astype(LOW)
    lse_ref[0] = top + jnp.log2(total)


def attend_back_kernel(
    lo_ref, hi_ref, q_ref, do_ref, mix_ref, lse_ref, start_ref, end_ref, cos_ref, sin_ref, *rest, count, depth, parts
):
    pieces = rest[:count]
    dq_ref = rest[count]
    grads = rest[count + 1 : 2 * count + 1]
    kv_ref, dkv_ref = rest[2 * count + 1 :]
    gather_keys(pieces, kv_ref)
    i = pl.program_id(0)

    @pl.when(i == 0)
    def _():
        dkv_ref[...] = jnp.zeros_like(dkv_ref)

    queries, upstream = q_ref[...], do_ref[...]
    lse, first, last = lse_ref[0], start_ref[0], end_ref[0]
    products = jnp.transpose(upstream.astype(WIDE) * mix_ref[...])
    delta = jnp.sum(products, 0, keepdims=True)
    height = depth // parts

    def step(t, grad_query):
        for part in range(parts):
            at = pl.multiple_of(t * depth + part * height, height)
            span = pl.ds(at, height)
            keys = kv_ref[span, :HEAD]
            values = kv_ref[span, HEAD:]
            index = lax.broadcasted_iota(jnp.int32, (height, 1), 0) + at
            inside = jnp.logical_and(index >= first, index < last)
            scores = dot_nt(keys, queries) * SCALE_2
            probs = jnp.where(inside, jnp.exp2(scores - lse), 0.0)
            grad_probs = dot_nt(values, upstream)
            grad_scores = (probs * (grad_probs - delta)).astype(LOW)
            dkv_ref[span, HEAD:] += dot(probs.astype(LOW), upstream)
            dkv_ref[span, :HEAD] += dot(grad_scores, queries)
            grad_query = grad_query + dot_tn(grad_scores, keys)
        return grad_query

    grad_query = lax.fori_loop(lo_ref[i], hi_ref[i], step, jnp.zeros(queries.shape, WIDE)) * SCALE
    dq_ref[...] = (grad_query * cos_ref[...] - swapped(grad_query) * sin_ref[...]).astype(LOW)

    @pl.when(i == pl.num_programs(0) - 1)
    def _():
        at = 0
        for grad in grads:
            span = slice(at, at + grad.shape[0])
            grad[:, :HEAD] = (dkv_ref[span, :HEAD] * SCALE).astype(grad.dtype)
            grad[:, HEAD:] = dkv_ref[span, HEAD:].astype(grad.dtype)
            at += grad.shape[0]


def whole_block(array):
    return pl.BlockSpec(array.shape, lambda i, *_: (0,) * len(array.shape))


def bounds(starts, ends, rows, depth, key_rows):
    count = key_rows // depth
    lo = jnp.clip(starts[::rows] // depth, 0, count)
    hi = jnp.clip((ends[rows - 1 :: rows] + depth - 1) // depth, 0, count)
    return lo.astype(jnp.int32), hi.astype(jnp.int32)


def attention_call(kernel, by_row, by_lane, pieces, spans, out_rows, out_lanes, grads, rows, depth, name, **more):
    count = by_row[0].shape[0]
    key_rows = sum(piece.shape[0] for piece in pieces)
    lo, hi = bounds(*spans, rows, depth, key_rows)
    row = pl.BlockSpec((rows, HEAD), lambda i, *_: (i, 0))
    lane = pl.BlockSpec((1, 1, rows), lambda i, *_: (i, 0, 0))
    lanes = [v.reshape(count // rows, 1, rows) for v in by_lane + list(spans)]
    tail = more.pop("tail", [])
    scratch = [pltpu.VMEM((key_rows, 2 * HEAD), LOW)]
    if grads:
        scratch.append(pltpu.VMEM((key_rows, 2 * HEAD), WIDE))
    return pl.pallas_call(
        functools.partial(kernel, count=len(pieces), depth=depth, **more),
        grid_spec=pltpu.PrefetchScalarGridSpec(
            num_scalar_prefetch=2,
            grid=(count // rows,),
            in_specs=[row] * len(by_row) + [lane] * len(lanes) + [row] * len(tail) + [whole_block(p) for p in pieces],
            out_specs=[row] * len(out_rows) + [lane] * out_lanes + [whole_block(g) for g in grads],
            scratch_shapes=scratch,
        ),
        out_shape=[jax.ShapeDtypeStruct((count, HEAD), kind) for kind in out_rows]
        + [jax.ShapeDtypeStruct((count // rows, 1, rows), WIDE)] * out_lanes
        + grads,
        compiler_params=pltpu.CompilerParams(vmem_limit_bytes=60 * 2**20),
        cost_estimate=pl.CostEstimate(
            flops=(40 if grads else 30) * count * LONGEST * HEAD,
            bytes_accessed=16 * 2**20,
            transcendentals=count * LONGEST,
        ),
        name=name,
    )(lo, hi, *by_row, *lanes, *tail, *pieces)


def attend(queries, pieces, spans, rows=512, depth=1024):
    return attention_call(
        attend_kernel, [queries], [], pieces, spans, [LOW, WIDE], 1, [], rows, depth, "attend"
    )


def attend_back(queries, upstream, mixed, lse, tables, pieces, spans, rows=512, depth=1024):
    middle = len(pieces) // 2
    grads = [
        jax.ShapeDtypeStruct(p.shape, WIDE if j == middle else LOW) for j, p in enumerate(pieces)
    ]
    return attention_call(
        attend_back_kernel,
        [queries, upstream, mixed],
        [lse],
        pieces,
        spans,
        [LOW],
        0,
        grads,
        rows,
        depth,
        "attend_back",
        tail=list(tables),
        parts=2,
    )


def gathered_kernel(dq_ref, own_ref, cos_ref, sin_ref, *rest, places):
    out_ref = rest[-1]
    i = pl.program_id(0)
    grad = own_ref[...]
    for ref, (first, count) in zip(rest, places):
        here = jnp.logical_and(i >= first, i < first + count)
        grad = grad + jnp.where(here, ref[...].astype(WIDE), 0.0)
    keys = grad[:, :HEAD]
    out_ref[:, :HEAD] = dq_ref[...]
    out_ref[:, HEAD : 2 * HEAD] = (keys * cos_ref[...] - swapped(keys) * sin_ref[...]).astype(LOW)
    out_ref[:, 2 * HEAD :] = grad[:, HEAD:].astype(LOW)


def gathered(grad_query, own, tables, arrivals, rows=512):
    count = own.shape[0]
    places = [(first // rows, part.shape[0] // rows) for first, part in arrivals]

    def row(width):
        return pl.BlockSpec((rows, width), lambda i: (i, 0))

    def part(place):
        return pl.BlockSpec((rows, 2 * HEAD), lambda i: (jnp.clip(i - place[0], 0, place[1] - 1), 0))

    return pl.pallas_call(
        functools.partial(gathered_kernel, places=places),
        grid=(count // rows,),
        in_specs=[row(HEAD), row(2 * HEAD), row(HEAD), row(HEAD)] + [part(place) for place in places],
        out_specs=row(3 * HEAD),
        out_shape=jax.ShapeDtypeStruct((count, 3 * HEAD), LOW),
        cost_estimate=pl.CostEstimate(flops=0, bytes_accessed=16 * 2**20, transcendentals=0),
        name="gathered",
    )(grad_query, own, *tables, *[array for _, array in arrivals])


def on_device(
    acoustic_features,
    clip_durations,
    early_layernorm_scale,
    early_widening_matrix,
    early_narrowing_matrix,
    mixer_layernorm_scale,
    triple_matrix,
    mixer_exit_matrix,
    filter_layernorm_scale,
    gating_pair_matrix,
    depthwise_filter,
    running_stats_factor,
    running_stats_offset,
    filter_exit_projection,
    later_layernorm_scale,
    later_widening_matrix,
    later_narrowing_matrix,
    last_layernorm_scale,
    quantizer_projection,
    entry_vectors,
    smoothing_level,
    random_flat_samples,
    expected_entries,
    result_adjoint,
    discrete_adjoint,
):
    seq_count, mp_count = lax.axis_size("seq"), lax.axis_size("mp")
    seq_at, mp_at = lax.axis_index("seq"), lax.axis_index("mp")
    core = seq_at % 2
    frame_rows = acoustic_features.shape[0]
    all_rows = frame_rows * seq_count
    own = frame_rows // mp_count
    own_base = seq_at * frame_rows + mp_at * own

    local_heads = triple_matrix.shape[2] // HEAD
    group_place = seq_at % local_heads
    groups = [
        [(z * local_heads + g) * mp_count + m for g in range(local_heads) for m in range(mp_count)]
        for z in range(seq_count // local_heads)
    ]
    group_size = local_heads * mp_count

    def own_rows(shard):
        size = shard.shape[0] // local_heads
        return cut(shard, part_of(group_place, local_heads) * size, size)

    def own_columns(shard):
        size = shard.shape[1] // local_heads
        return cut(shard, part_of(group_place, local_heads) * size, size, 1).T

    def over_group(part):
        return lax.all_gather(part, BOTH, axis_index_groups=groups, axis=0)

    def grouped(array):
        parts = array.reshape(-1, mp_count, local_heads, array.shape[1] // group_size)
        parts = jnp.stack([parts[:, :, part_of(g, local_heads)] for g in range(local_heads)], 1)
        return parts.reshape(array.shape)

    def ungrouped(array):
        parts = array.reshape(-1, local_heads, mp_count, array.shape[1] // group_size)
        places = sorted(range(local_heads), key=lambda g: part_of(g, local_heads))
        return jnp.stack([parts[:, g] for g in places], 2).reshape(array.shape)

    def group_total(array, over=None):
        return lax.psum_scatter(array, BOTH, scatter_dimension=0, axis_index_groups=over or groups, tiled=True)

    def interleaved(arrays, count):
        parts = [a.astype(LOW).reshape(count, a.shape[0] // count, D) for a in arrays]
        return jnp.concatenate(parts, 1).reshape(-1, D)

    def rel_rows(array, k):
        return cut(array, mp_place(k) * own, own)

    def local_halves(array):
        half = array.shape[1] // 2
        return [cut(array, (core ^ j) * half, half, 1) for j in range(2)]

    head_matrix = cut(triple_matrix, part_of(group_place, local_heads) * HEAD, HEAD, 2)
    head_matrix = jnp.concatenate([head_matrix[i] for i in range(3)], 1)
    small_weights = jnp.concatenate(
        [depthwise_filter, running_stats_factor[None], running_stats_offset[None]], 0
    )
    small_all = grouped(joined(from_mp(small_weights), 1))
    filter_all, factor_all, offset_all = small_all[:KERNEL], small_all[KERNEL], small_all[KERNEL + 1]

    code_parts = jnp.stack([own_columns(quantizer_projection), own_rows(entry_vectors)])
    noise_parts = [rel_rows(random_flat_samples, k) for k in range(mp_count)]
    first_rows, code_parts, noise_parts = paced(acoustic_features, code_parts, noise_parts)
    code_every = over_group(code_parts)
    noise_parts = [noise_parts[0]] + [mp_shift(part, k) for k, part in enumerate(noise_parts) if k]

    first = []
    for k in list(range(1, mp_count)) + [0]:
        rows = rel_rows(first_rows, k).astype(WIDE)
        entered, normed, inverse = norm_forward(rows, early_layernorm_scale)
        hidden = dot(entered, early_widening_matrix)
        activated = (hidden * jax.nn.sigmoid(hidden)).astype(LOW)
        part = dot(activated, early_narrowing_matrix)
        first.append((part, entered, hidden, activated, normed, inverse))
    first = [first[-1]] + first[:-1]
    features = rel_rows(acoustic_features, 0).astype(WIDE)
    after_ffn = features + 0.5 * to_mp([f[0] for f in first])

    quantizer_all, book_all = code_every[:, 0].reshape(-1, D), code_every[:, 1].reshape(-1, D)
    noise = grouped(joined([noise_parts[0]] + noise_parts[:0:-1], 1))
    temper = smoothing_level[0]
    own_features = rel_rows(acoustic_features, 0)
    noisy = dot_nt(own_features, quantizer_all) - jnp.log(-jnp.log(noise))
    tempered = noisy / temper
    assigned = jnp.exp(tempered - jax.nn.logsumexp(tempered, -1)[:, None])
    assigned_low = assigned.astype(LOW)
    quant_low = dot(assigned_low, book_all).astype(LOW)
    own_discrete = rel_rows(discrete_adjoint, 0)
    grad_soft = dot_nt(own_discrete, book_all)
    row_dot = jnp.sum(assigned * grad_soft, -1)
    grad_tempered = assigned * (grad_soft - row_dot[:, None])
    grad_temper = -jnp.sum(grad_tempered * noisy) / (temper * temper)
    grad_entry = (grad_tempered / temper).astype(LOW)
    quant_in = dot(grad_entry, quantizer_all)
    code_grads = dot_tn(assigned_low, own_discrete), dot_tn(grad_entry, own_features)

    group_rows = local_heads * frame_rows
    group_at = seq_at // local_heads
    att_entered, att_normed, att_inverse = norm_forward(after_ffn, mixer_layernorm_scale)
    att_group = over_group(att_entered).reshape(group_rows, D)
    reaches = range(1, -(-(LONGEST - 1) // group_rows) + 1)
    halo = [min(group_rows, -(-(LONGEST - (r - 1) * group_rows) // 1024) * 1024) for r in reaches]
    halo_rows = sum(halo)
    key_base = group_at * group_rows - halo_rows
    group_index = group_at * group_rows + jnp.arange(group_rows, dtype=jnp.int32)
    _, group_start, group_end = clip_of(clip_durations, group_index)
    tables = turn_tables(group_index - group_start)
    spans = (group_start - key_base, group_end - key_base)
    middle_parts = [
        own_rows(mixer_exit_matrix),
        own_columns(gating_pair_matrix[0]),
        own_columns(gating_pair_matrix[1]),
        own_rows(filter_exit_projection),
    ]
    up_part, down_part = own_columns(later_widening_matrix), own_rows(later_narrowing_matrix)
    att_group, tables, code_grads, quant_low, quant_in, grad_temper, sent = paced(
        att_group,
        tables,
        code_grads,
        quant_low,
        quant_in,
        grad_temper,
        (jnp.stack(middle_parts), up_part, down_part, head_matrix),
    )
    middle_every = over_group(sent[0])
    head_matrix = sent[3]
    exit_all, value_all, gate_all, point_all = [middle_every[:, i].reshape(-1, D) for i in range(4)]
    up_all = over_group(sent[1]).reshape(-1, D)
    down_all = over_group(sent[2]).reshape(-1, D)
    query_rot, kv_own = project(att_group, head_matrix, tables)
    lower = [seq_shift(kv_own[group_rows - n :], local_heads * r) for r, n in zip(reaches, halo)]
    upper = [seq_shift(kv_own[:n], -local_heads * r) for r, n in zip(reaches, halo)]
    kv_pieces = lower[::-1] + [kv_own] + upper
    mixed_low, mixed, row_lse = attend(query_rot, kv_pieces, spans)
    mixed_low, head_sent = paced(mixed_low, head_matrix)
    heads_all = over_group(head_sent)

    def exchange(array):
        return lax.all_to_all(array, BOTH, 0, 0, axis_index_groups=groups)

    att_parts = exchange(mixed_low.reshape(group_size, own, HEAD))
    att_low = jnp.transpose(att_parts, (1, 0, 2)).reshape(own, D)
    after_att = after_ffn + dot(att_low, exit_all)

    half_kernel = KERNEL // 2
    pad_index = own_base - half_kernel + jnp.arange(own + 2 * half_kernel, dtype=jnp.int32)
    pad_seg = clip_of(clip_durations, pad_index)[0]
    pad_seg = jnp.where(jnp.logical_and(pad_index >= 0, pad_index < all_rows), pad_seg, -1)
    own_seg = pad_seg[half_kernel : half_kernel + own]
    masks = [(pad_seg[j : j + own] == own_seg)[:, None] for j in range(KERNEL)]

    def padded(block):
        low = flat_shift(block[own - half_kernel :], 1)
        high = flat_shift(block[:half_kernel], -1)
        return jnp.concatenate([low, block, high], 0).astype(WIDE)

    conv_entered, conv_normed, conv_inverse = norm_forward(after_att, filter_layernorm_scale)
    glu_value = dot_nt(conv_entered, value_all)
    glu_gate = jax.nn.sigmoid(dot_nt(conv_entered, gate_all))
    glu_low = (glu_value * glu_gate).astype(LOW)
    glu_padded = padded(glu_low)
    conv_out = jnp.zeros((own, D), WIDE)
    for j in range(KERNEL):
        conv_out = conv_out + filter_all[j][None, :] * jnp.where(masks[j], glu_padded[j : j + own], 0.0)
    sums = total_over_all(jnp.stack([jnp.sum(conv_out, 0), jnp.sum(conv_out * conv_out, 0)]), 1)
    bn_mean = sums[0] / all_rows
    bn_inv = lax.rsqrt(sums[1] / all_rows - bn_mean * bn_mean + EPSILON)
    bn_hat = (conv_out - bn_mean) * bn_inv
    bn_out = bn_hat * factor_all + offset_all
    bn_sigma = jax.nn.sigmoid(bn_out)
    swish_low = (bn_out * bn_sigma).astype(LOW)
    after_conv = after_att + dot(swish_low, point_all)

    late_entered, late_normed, late_inverse = norm_forward(after_conv, later_layernorm_scale)
    late_hidden = dot_nt(late_entered, up_all)
    late_act = (late_hidden * jax.nn.sigmoid(late_hidden)).astype(LOW)
    branch = dot(late_act, down_all)
    after_two = after_conv + 0.5 * branch
    final_low, final_normed, final_inverse = norm_forward(after_two, last_layernorm_scale)

    codes = book_all.shape[0]
    logits = dot_nt(final_low, book_all) * D ** (-0.5)
    code_index = grouped(jnp.arange(codes, dtype=jnp.int32)[None, :])
    is_target = rel_rows(expected_entries, 0)[:, None] == code_index
    pred_lse = jax.nn.logsumexp(logits, -1)
    row_loss = pred_lse - jnp.sum(jnp.where(is_target, logits, 0.0), -1)
    grad_pred = (jnp.exp(logits - pred_lse[:, None]) - is_target.astype(WIDE)).astype(LOW)
    grad_final = rel_rows(result_adjoint, 0).astype(WIDE) + dot(grad_pred, book_all) * D ** (-0.5)
    book_grad = dot_tn(grad_pred, final_low) * D ** (-0.5) + code_grads[0]
    grad_final, loss_shares = paced(grad_final, from_mp(row_loss))
    frame_loss = joined(loss_shares)
    grad_four, grad_ln_final = norm_backward(grad_final, last_layernorm_scale, final_normed, final_inverse)
    late_branch = (0.5 * grad_four).astype(LOW)
    grad_act = dot_nt(late_branch, down_all)
    grad_hidden = (grad_act * silu_slope(late_hidden, jax.nn.sigmoid(late_hidden))).astype(LOW)
    late_in = dot(grad_hidden, up_all)
    down_grad = dot_tn(late_act, late_branch).astype(LOW)
    up_grad = dot_tn(grad_hidden, late_entered).astype(LOW)
    late_norm_grad, grad_ln_ffn2 = norm_backward(late_in, later_layernorm_scale, late_normed, late_inverse)
    grad_three = grad_four + late_norm_grad

    conv_branch = grad_three.astype(LOW)
    grad_swish = dot_nt(conv_branch, point_all)
    grad_bn = grad_swish * silu_slope(bn_out, bn_sigma)
    back_sums = jnp.stack([jnp.sum(grad_bn, 0), jnp.sum(grad_bn * bn_hat, 0)])
    back_sums, up_grad, down_grad, heads_all = paced(back_sums, up_grad, down_grad, heads_all)
    down_total, up_total = group_total(down_grad), group_total(up_grad)
    back_sums = total_over_all(back_sums, 2)
    grad_conv = (
        factor_all * bn_inv * (grad_bn - back_sums[0] / all_rows - bn_hat * back_sums[1] / all_rows)
    ).astype(LOW)
    grad_padded = padded(grad_conv)
    grad_exact = grad_conv.astype(WIDE)
    grad_taps = []
    grad_gated = jnp.zeros_like(grad_exact)
    for j in range(KERNEL):
        grad_taps.append(jnp.sum(grad_exact * jnp.where(masks[j], glu_padded[j : j + own], 0.0), 0))
        back = 2 * half_kernel - j
        grad_gated = grad_gated + filter_all[j][None, :] * jnp.where(
            masks[back], grad_padded[back : back + own], 0.0
        )
    grad_value = (grad_gated * glu_gate).astype(LOW)
    grad_gate = (grad_gated * glu_value * glu_gate * (1.0 - glu_gate)).astype(LOW)
    conv_in = dot(grad_value, value_all) + dot(grad_gate, gate_all)
    conv_norm_grad, grad_ln_conv = norm_backward(conv_in, filter_layernorm_scale, conv_normed, conv_inverse)
    grad_two = grad_three + conv_norm_grad

    att_branch = grad_two.astype(LOW)
    mixer_grads = [
        dot_tn(grad_value, conv_entered),
        dot_tn(grad_gate, conv_entered),
        dot_tn(swish_low, conv_branch),
        dot_tn(att_low, att_branch),
        book_grad,
        code_grads[1],
    ]
    grad_heads = dot_nt(att_branch, exit_all).astype(LOW)
    grad_heads = jnp.transpose(grad_heads.reshape(own, group_size, HEAD), (1, 0, 2))
    grad_mixed = exchange(grad_heads).reshape(group_rows, HEAD)
    mixer_grads = interleaved(mixer_grads, group_size)
    grad_mixed, mixer_grads = paced(grad_mixed, mixer_grads)
    mixer_total = group_total(mixer_grads)
    grad_query, *grad_pieces = attend_back(query_rot, grad_mixed, mixed, row_lse, tables, kv_pieces, spans)
    grad_pieces, up_total, down_total = paced(grad_pieces, up_total, down_total)
    arrivals = []
    reach_count = len(halo)
    for r, n in zip(reaches, halo):
        back = seq_shift(grad_pieces[reach_count - r], -local_heads * r)
        arrivals.append((group_rows - n, back))
        back = seq_shift(grad_pieces[reach_count + r], local_heads * r)
        arrivals.append((0, back))
    grad_proj = gathered(grad_query, grad_pieces[reach_count], tables, arrivals)
    bits, low_bits = bit_count(seq_count), bit_count(local_heads)
    late_total = halved(jnp.stack([up_total, down_total]), low_bits)

    proj_parts = exchange(grad_proj.reshape(group_size, own, 3 * HEAD))
    head_total = halved(dot_tn(att_group, grad_proj).astype(LOW)[None], low_bits)
    proj_parts, late_total = paced(proj_parts, late_total)
    for bit in range(low_bits + 1, bits):
        late_total = halved(late_total, bit)
    att_in = lax.dot_general(
        proj_parts, heads_all, (((0, 2), (0, 2)), ((), ())), preferred_element_type=WIDE
    )
    att_norm_grad, grad_ln_att = norm_backward(att_in, mixer_layernorm_scale, att_normed, att_inverse)
    grad_one = grad_two + att_norm_grad
    grad_one, late_total, mixer_total, head_total = paced(grad_one, late_total, mixer_total, head_total)
    late_every = lax.all_gather(late_total, "seq", axis=0)
    mixed_total = halved(mixer_total.reshape(6, -1, D), low_bits)

    early_branch = from_mp((0.5 * grad_one).astype(LOW))
    early_branch, mixed_total = paced(early_branch, mixed_total)
    for bit in range(low_bits + 1, bits):
        mixed_total, head_total = halved(mixed_total, bit), halved(head_total, bit)
    early_in, early_grads = [], []
    for k, (_, entered, hidden, activated, _, _) in enumerate(first):
        grad_act = dot_nt(early_branch[k], early_narrowing_matrix)
        early_grads.append((grad_act * silu_slope(hidden, jax.nn.sigmoid(hidden))).astype(LOW))
        early_in.append(dot_nt(early_grads[k], early_widening_matrix))

    early_in, head_total, mixed_total = paced(early_in, head_total, mixed_total)
    mixed_every = lax.all_gather(mixed_total, "seq", axis=0)
    head_every = lax.all_gather(head_total[0], "seq", axis=0)
    act_all = jnp.concatenate([f[3] for f in first], 0)
    branch_all = jnp.concatenate(early_branch, 0)
    entered_all = jnp.concatenate([f[1] for f in first], 0)
    hid_all = jnp.concatenate(early_grads, 0)
    up_parts = [dot_tn(entered_all, hid).astype(LOW) for hid in local_halves(hid_all)]
    down_parts = [dot_tn(act, branch_all).astype(LOW) for act in local_halves(act_all)]
    up2_grad, down2_grad = laid(late_every, 0, 1, local_heads, True)[0], laid(late_every, 1, 1, local_heads, False)[0]
    gate_grads = laid(mixed_every, 0, 2, local_heads, True)
    point_grad, exit_grad, book_grad = [laid(mixed_every, i, 1, local_heads, False)[0] for i in (2, 3, 4)]
    code_grad = laid(mixed_every, 5, 1, local_heads, True)[0]
    qkv_grad = laid_heads(head_every, local_heads)
    early_norm_grad, grad_ln_ffn1 = norm_backward(to_mp(early_in), early_layernorm_scale, first[0][4], first[0][5])
    frames_low = (grad_one + early_norm_grad + quant_in).astype(LOW)
    small, (grad_frames, layer_out, quantized), (up1_halves, down1_halves) = seq_total(
        [frames_low, final_low, quant_low],
        [up_parts[0], down_parts[0]],
        [up_parts[1], down_parts[1]],
        jnp.stack(
            [grad_ln_ffn1, grad_ln_att, grad_ln_conv, grad_ln_ffn2, grad_ln_final]
            + grad_taps
            + [jnp.full((D,), grad_temper, WIDE)]
        ),
        3,
    )
    up1_grad, down1_grad = beside(up1_halves, False), beside(down1_halves, True)
    own_channels = filter_exit_projection.shape[0]

    def own_part(array):
        return cut(ungrouped(array), mp_at * own_channels, own_channels, 1)

    bn_grads = own_part(back_sums)

    return (
        layer_out,
        quantized,
        frame_loss,
        grad_frames,
        small[0],
        up1_grad,
        down1_grad,
        small[1],
        qkv_grad,
        exit_grad,
        small[2],
        gate_grads,
        own_part(small[5 : 5 + KERNEL]),
        bn_grads[1],
        bn_grads[0],
        point_grad,
        small[3],
        up2_grad,
        down2_grad,
        small[4],
        code_grad,
        book_grad,
        small[5 + KERNEL, :1],
    )


def solution(mesh):
    in_specs = (
        P("seq", None),
        P(),
        P(),
        P(None, "mp"),
        P("mp", None),
        P(),
        P(None, None, "mp"),
        P("mp", None),
        P(),
        P(None, None, "mp"),
        P(None, "mp"),
        P("mp"),
        P("mp"),
        P("mp", None),
        P(),
        P(None, "mp"),
        P("mp", None),
        P(),
        P(None, "mp"),
        P("mp", None),
        P(),
        P("seq", "mp"),
        P("seq"),
        P("seq", None),
        P("seq", None),
    )
    out_specs = (
        P("seq", None),
        P("seq", None),
        P("seq"),
        P("seq", None),
        P(),
        P(None, "mp"),
        P("mp", None),
        P(),
        P(None, None, "mp"),
        P("mp", None),
        P(),
        P(None, None, "mp"),
        P(None, "mp"),
        P("mp"),
        P("mp"),
        P("mp", None),
        P(),
        P(None, "mp"),
        P("mp", None),
        P(),
        P(None, "mp"),
        P("mp", None),
        P(),
    )
    return jax.shard_map(
        on_device, mesh=mesh, in_specs=in_specs, out_specs=out_specs, check_vma=False
    )
```

```python
import functools
import math

import jax
import jax.numpy as jnp
from jax import lax
from jax.experimental import pallas as pl
from jax.experimental.pallas import tpu as pltpu
from jax.sharding import PartitionSpec as P

D = 1024
HEAD = 128
KERNEL = 5
LONGEST = 3008

EPSILON = 1e-05
MASKED = -1e30
SCALE = HEAD ** (-0.5)
SCALE_2 = SCALE * math.log2(math.e)
BOTH = ("seq", "mp")
LOW = jnp.bfloat16
WIDE = jnp.float32


def dot(a, b, dims=((1,), (0,))):
    return lax.dot_general(a, b, (dims, ((), ())), preferred_element_type=WIDE)


def dot_nt(a, b):
    return dot(a, b, ((1,), (1,)))


def dot_tn(a, b):
    return dot(a, b, ((0,), (0,)))


def cut(array, start, size, axis=0):
    return lax.dynamic_slice_in_dim(array, start, size, axis)


def mp_shift(shard, by):
    count = lax.axis_size("mp")
    return lax.ppermute(shard, "mp", [(i, (i + by) % count) for i in range(count)])


def seq_xor(shard, mask):
    return lax.ppermute(shard, "seq", [(i, i ^ mask) for i in range(lax.axis_size("seq"))])


def seq_shift(shard, by):
    count = lax.axis_size("seq")
    return lax.ppermute(shard, "seq", [(i, i + by) for i in range(count) if 0 <= i + by < count])


def flat_shift(shard, by):
    count = lax.axis_size("seq") * lax.axis_size("mp")
    return lax.ppermute(shard, BOTH, [(i, i + by) for i in range(count) if 0 <= i + by < count])


def from_mp(shard):
    return [shard] + [mp_shift(shard, -k) for k in range(1, lax.axis_size("mp"))]


def to_mp(parts):
    total = parts[0].astype(WIDE)
    for k in range(1, len(parts)):
        total = total + mp_shift(parts[k].astype(LOW), k).astype(WIDE)
    return total


def mp_place(k):
    return (lax.axis_index("mp") + k) % lax.axis_size("mp")


def joined(pieces, axis=0):
    size = pieces[0].shape[axis]
    shape = list(pieces[0].shape)
    shape[axis] = size * len(pieces)
    whole = jnp.zeros(shape, pieces[0].dtype)
    for k, piece in enumerate(pieces):
        whole = lax.dynamic_update_slice_in_dim(whole, piece, mp_place(k) * size, axis)
    return whole


def paced(*values):
    return lax.optimization_barrier(values)


def bit_count(number):
    return int(math.log2(number))


def laid_kernel(in_ref, out_ref, *, places, turned):
    rows = in_ref.shape[1]
    for s, place in enumerate(places):
        block = in_ref[s].astype(WIDE)
        span = slice(place * rows, (place + 1) * rows)
        if turned:
            out_ref[0, :, span] = block.T
        else:
            out_ref[0, span, :] = block


def laid(every, first, rows, amount, local_heads, turned):
    count, _, columns = every.shape
    line = count // local_heads
    places = [part_of(s % local_heads, local_heads) * line + s // local_heads for s in range(count)]
    if rows % 16 or count * rows % 128:
        order = sorted(range(count), key=lambda s: places[s])
        whole = every[:, first : first + amount * rows].reshape(count, amount, rows, columns)
        whole = jnp.stack([whole[s] for s in order], 1).astype(WIDE).reshape(amount, count * rows, columns)
        return jnp.transpose(whole, (0, 2, 1)) if turned else whole
    shape = (columns, count * rows) if turned else (count * rows, columns)
    width = min(columns, 2**19 // (count * rows))
    block = (1, width, count * rows) if turned else (1, count * rows, width)
    return pl.pallas_call(
        functools.partial(laid_kernel, places=places, turned=turned),
        grid=(amount, columns // width),
        in_specs=[pl.BlockSpec((count, rows, width), lambda i, j: (0, first // rows + i, j))],
        out_specs=pl.BlockSpec(block, lambda i, j: (i, j, 0) if turned else (i, 0, j)),
        out_shape=jax.ShapeDtypeStruct((amount,) + shape, WIDE),
        compiler_params=pltpu.CompilerParams(vmem_limit_bytes=32 * 2**20),
        cost_estimate=pl.CostEstimate(
            flops=0, bytes_accessed=6 * amount * shape[0] * shape[1], transcendentals=0
        ),
        name="laid",
    )(every)


def products_kernel(*refs, plan, line):
    out_ref = refs[-1]
    at = ref = 0
    for terms in plan:
        sum_of = None
        for scale in terms:
            term = dot_tn(refs[ref][...], refs[ref + 1][...])
            term = term if scale is None else term * scale
            sum_of = term if sum_of is None else sum_of + term
            ref += 2
        rows = sum_of.shape[0] // line
        for z in range(line):
            to = z * (out_ref.shape[1] // line) + at
            out_ref[0, to : to + rows, :] = sum_of[z * rows : (z + 1) * rows].astype(LOW)
        at += rows


def products(matrices, count, line):
    frames = matrices[0][0][0].shape[0]
    plan = [[term[2] for term in terms] for terms in matrices]
    operands, specs, height = [], [], 0
    for terms in matrices:
        width = terms[0][0].shape[1] // count
        height += width
        for left, right, _ in terms:
            operands += [left, right]
            specs += [
                pl.BlockSpec((frames, width), lambda i: (0, i)),
                pl.BlockSpec(right.shape, lambda i: (0, 0)),
            ]
    out = pl.pallas_call(
        functools.partial(products_kernel, plan=plan, line=line),
        grid=(count,),
        in_specs=specs,
        out_specs=pl.BlockSpec((1, height, D), lambda i: (i, 0, 0)),
        out_shape=jax.ShapeDtypeStruct((count, height, D), LOW),
        compiler_params=pltpu.CompilerParams(vmem_limit_bytes=50 * 2**20),
        cost_estimate=pl.CostEstimate(
            flops=2 * frames * height * count * D, bytes_accessed=2 * height * count * D, transcendentals=0
        ),
        name="products",
    )(*operands)
    return out.reshape(count * height, D)


def beside_kernel(in_ref, out_ref):
    out_ref[...] = in_ref[0].astype(WIDE)


def beside(halves, down, rows=1024):
    _, height, width = halves.shape
    rows = min(rows, height)
    steps = height // rows
    shape = (2 * height, width) if down else (height, 2 * width)

    def target(j, i):
        return (j * steps + i, 0) if down else (i, j)

    return pl.pallas_call(
        beside_kernel,
        grid=(2, steps),
        in_specs=[pl.BlockSpec((1, rows, width), lambda j, i: (j, i, 0))],
        out_specs=pl.BlockSpec((rows, width), target),
        out_shape=jax.ShapeDtypeStruct(shape, WIDE),
        compiler_params=pltpu.CompilerParams(vmem_limit_bytes=32 * 2**20),
        cost_estimate=pl.CostEstimate(flops=0, bytes_accessed=12 * height * width, transcendentals=0),
        name="beside",
    )(halves)


def remote(source, target, send, recv, device):
    return pltpu.make_async_remote_copy(
        src_ref=source,
        dst_ref=target,
        send_sem=send,
        recv_sem=recv,
        device_id=device,
        device_id_type=pl.DeviceIdType.MESH,
    )


def seq_partner(bit):
    return (lax.axis_index("seq") ^ (1 << bit), lax.axis_index("mp"))


def all_partners(seq_bits, mp_bits):
    mp = lax.axis_index("mp")
    across = [(lax.axis_index("seq"), mp ^ (1 << bit)) for bit in range(mp_bits)]
    return across + [seq_partner(bit) for bit in range(seq_bits)]


def meet(partners):
    barrier = pltpu.get_barrier_semaphore()
    for device in partners:
        pl.semaphore_signal(barrier, inc=1, device_id=device, device_id_type=pl.DeviceIdType.MESH)
    pl.semaphore_wait(barrier, len(partners))


class Small:
    def __init__(self, held, slots, send, recv, partners):
        self.held, self.slots, self.send, self.recv, self.partners = held, slots, send, recv, partners
        self.at = 0

    def copy(self, k):
        return remote(self.held.at[k], self.slots.at[k], self.send.at[k], self.recv.at[k], self.partners[k])

    def advance(self):
        k = self.at
        if k > len(self.partners):
            return
        if k > 0:
            self.copy(k - 1).wait_recv()
            self.held[k] = self.held[k - 1] + self.slots[k - 1]
        if k < len(self.partners):
            self.copy(k).start()
        self.at += 1

    def finish(self, out):
        while self.at <= len(self.partners):
            self.advance()
        for k in range(len(self.partners)):
            self.copy(k).wait_send()
        out[...] = self.held[len(self.partners)]


def small_scratch(shape, steps):
    dma = pltpu.SemaphoreType.DMA
    return [pltpu.VMEM((steps + 1,) + shape, WIDE), pltpu.VMEM((steps,) + shape, WIDE), dma((steps,)), dma((steps,))]


def total_kernel(in_ref, out_ref, held, slots, send, recv, *, seq_bits, mp_bits):
    partners = all_partners(seq_bits, mp_bits)
    meet(partners)
    held[0] = in_ref[...]
    Small(held, slots, send, recv, partners).finish(out_ref)


def total_over_all(values, collective_id):
    seq_bits, mp_bits = bit_count(lax.axis_size("seq")), bit_count(lax.axis_size("mp"))
    flat = values.reshape(-1, HEAD)
    space = pl.BlockSpec(memory_space=pltpu.VMEM)
    out = pl.pallas_call(
        functools.partial(total_kernel, seq_bits=seq_bits, mp_bits=mp_bits),
        in_specs=[space],
        out_specs=space,
        out_shape=jax.ShapeDtypeStruct(flat.shape, WIDE),
        scratch_shapes=small_scratch(flat.shape, seq_bits + mp_bits),
        compiler_params=pltpu.CompilerParams(collective_id=collective_id, has_side_effects=True),
        name="total_over_all",
    )(flat)
    return out.reshape(values.shape)


def seq_total_kernel(small_ref, *refs, count, chunks, seq_bits, mp_bits, share_count):
    shares, refs = refs[:share_count], refs[share_count:]
    mine, other = refs[:count], refs[count : 2 * count]
    small_out, refs = refs[2 * count], refs[2 * count + 1 :]
    shared, refs = refs[:share_count], refs[share_count:]
    outs, scratch = refs[:count], refs[count:]
    (share_local, share_send, share_recv), scratch = scratch[:3], scratch[3:]
    arrived, held = scratch[:count], scratch[count : 2 * count]
    levels = seq_bits - 1
    slots = [scratch[(2 + i) * count : (3 + i) * count] for i in range(levels)]
    core_send, core_recv, back_core_send, back_core_recv, send, recv, back_send, back_recv = scratch[
        (2 + levels) * count : (2 + levels) * count + 8
    ]
    partners = all_partners(seq_bits, mp_bits)
    mp, mp_count = lax.axis_index("mp"), 1 << mp_bits
    along_mp = [(lax.axis_index("seq"), (mp + k) % mp_count) for k in range(1, mp_count)]
    meet(along_mp + partners[mp_bits:])

    def share_rows(i, index):
        rows = shares[i].shape[0]
        return shared[i].at[pl.ds(pl.multiple_of(index * rows, 16), rows)]

    def share_copy(i, k, index):
        return remote(
            shares[i], share_rows(i, index), share_send.at[i, k - 1], share_recv.at[i, k - 1], along_mp[k - 1]
        )

    def share_own(i):
        return pltpu.make_async_copy(shares[i], share_rows(i, mp), share_local.at[i])

    small = Small(*scratch[(2 + levels) * count + 8 :], partners)
    small.held[0] = small_ref[...]
    seq = lax.axis_index("seq")
    core, sibling = seq % 2, seq_partner(0)

    plan = []
    for a in range(count):
        rows = mine[a].shape[0] // chunks[a]
        plan += [(a, c * rows, rows) for c in range(chunks[a])]
    everything = range(len(plan))

    def base(n, level):
        first, rows = plan[n][1:]
        for bit in range(1, level + 1):
            first = first + ((seq >> bit) & 1) * (rows >> bit)
        return first

    def span(n, level, kept):
        side = (seq >> level) & 1
        size = plan[n][2] >> level
        first = base(n, level - 1) + (side if kept else 1 - side) * size
        return pl.ds(pl.multiple_of(first, 16), size)

    def slot(n, level):
        return pl.ds(plan[n][1] >> level, plan[n][2] >> level)

    def whole(n):
        return pl.ds(plan[n][1], plan[n][2])

    def core_copy(n):
        a = plan[n][0]
        return remote(other[a].at[whole(n)], arrived[a].at[whole(n)], core_send.at[n], core_recv.at[n], sibling)

    def copy(n, level):
        a = plan[n][0]
        return remote(
            held[a].at[span(n, level, False)],
            slots[level - 1][a].at[slot(n, level)],
            send.at[n, level - 1],
            recv.at[n, level - 1],
            seq_partner(level),
        )

    def back_copy(n, level, arriving):
        rows = outs[plan[n][0]].at[core, span(n, level, not arriving)]
        return remote(rows, rows, back_send.at[n, level - 1], back_recv.at[n, level - 1], seq_partner(level))

    def back_core_copy(n, arriving):
        rows = outs[plan[n][0]].at[1 - core if arriving else core, whole(n)]
        return remote(rows, rows, back_core_send.at[n], back_core_recv.at[n], sibling)

    def fold(n, level):
        a = plan[n][0]
        copy(n, level).wait_recv()
        kept = span(n, level, True)
        total = held[a][kept, :].astype(WIDE) + slots[level - 1][a][slot(n, level), :].astype(WIDE)
        if level < levels:
            held[a][kept, :] = total.astype(LOW)
            copy(n, level + 1).start()
        else:
            outs[a][core, kept, :] = total.astype(LOW)
            back_copy(n, level, False).start()

    def unfold(n, level):
        back_copy(n, level, True).wait_recv()
        back_copy(n, level - 1, False).start()

    small.advance()
    for n in everything:
        core_copy(n).start()
    def enter(n):
        a = plan[n][0]
        core_copy(n).wait_recv()
        held[a][whole(n), :] = (mine[a][whole(n), :].astype(WIDE) + arrived[a][whole(n), :].astype(WIDE)).astype(LOW)
        copy(n, 1).start()

    for n in range(2):
        enter(n)
    small.advance()
    for i in range(share_count):
        share_own(i).start()
        for k in range(1, mp_count):
            share_copy(i, k, mp).start()
    stages = [functools.partial(fold, level=level) for level in range(1, levels + 1)]
    stages += [functools.partial(unfold, level=level) for level in range(levels, 1, -1)]
    for t in range(len(plan) + len(stages) - 1):
        if t + 2 < len(plan):
            enter(t + 2)
        for number in reversed(range(len(stages))):
            if 0 <= t - number < len(plan):
                stages[number](t - number)
        small.advance()
    for n in everything:
        back_copy(n, 1, True).wait_recv()
        back_core_copy(n, False).start()
    for n in everything:
        back_core_copy(n, True).wait_recv()
        core_copy(n).wait_send()
        back_core_copy(n, False).wait_send()
        for level in range(1, levels + 1):
            copy(n, level).wait_send()
            back_copy(n, level, False).wait_send()
    small.finish(small_out)
    for i in range(share_count):
        share_own(i).wait()
        for k in range(1, mp_count):
            share_copy(i, k, (mp + mp_count - k) % mp_count).wait_recv()
            share_copy(i, k, mp).wait_send()


def seq_total(shares, mine, other, small, collective_id):
    seq_bits, mp_bits = bit_count(lax.axis_size("seq")), bit_count(lax.axis_size("mp"))
    levels = seq_bits - 1
    chunks = [min(4, max(1, part.shape[0] // (16 << levels))) for part in mine]
    count, total = len(mine), sum(chunks)
    flat = small.reshape(-1, HEAD)
    space, far = pl.BlockSpec(memory_space=pltpu.VMEM), pl.BlockSpec(memory_space=pl.ANY)
    shapes = [part.shape for part in mine]
    dma = pltpu.SemaphoreType.DMA
    out = pl.pallas_call(
        functools.partial(
            seq_total_kernel,
            count=count,
            chunks=chunks,
            seq_bits=seq_bits,
            mp_bits=mp_bits,
            share_count=len(shares),
        ),
        in_specs=[space] + [far] * len(shares) + [space] * (2 * count),
        out_specs=[space] + [far] * len(shares) + [space] * count,
        out_shape=[jax.ShapeDtypeStruct(flat.shape, WIDE)]
        + [jax.ShapeDtypeStruct((part.shape[0] << mp_bits, part.shape[1]), part.dtype) for part in shares]
        + [jax.ShapeDtypeStruct((2,) + shape, LOW) for shape in shapes],
        scratch_shapes=[dma((len(shares),))]
        + [dma((len(shares), max(1, (1 << mp_bits) - 1)))] * 2
        + [pltpu.VMEM(shape, LOW) for shape in shapes] * 2
        + [pltpu.VMEM((rows >> level, width), LOW) for level in range(1, levels + 1) for rows, width in shapes]
        + [dma((total,))] * 4
        + [dma((total, levels))] * 4
        + small_scratch(flat.shape, seq_bits + mp_bits),
        compiler_params=pltpu.CompilerParams(
            collective_id=collective_id, has_side_effects=True, vmem_limit_bytes=56 * 2**20
        ),
        cost_estimate=pl.CostEstimate(flops=10**11, bytes_accessed=32 * 2**20, transcendentals=0),
        name="seq_total",
    )(flat, *shares, *mine, *other)
    return out[0].reshape(small.shape), out[1 : 1 + len(shares)], out[1 + len(shares) :]


def clip_of(clip_durations, positions):
    clip_ends = jnp.cumsum(clip_durations, dtype=jnp.int32)
    passed = clip_ends[None, :] <= positions[:, None]
    segment = jnp.sum(passed.astype(jnp.int32), 1, dtype=jnp.int32)
    starts = jnp.sum(jnp.where(passed, clip_durations[None, :], 0), 1, dtype=jnp.int32)
    ends = jnp.min(jnp.where(passed, 2**30, clip_ends[None, :]), 1)
    return segment, starts, ends


def norm_forward(rows, gain):
    centred = rows - jnp.mean(rows, -1, keepdims=True)
    inverse = lax.rsqrt(jnp.mean(centred * centred, -1, keepdims=True) + EPSILON)
    normed = centred * inverse
    return (normed * gain).astype(LOW), normed, inverse


def norm_backward(upstream, gain, normed, inverse):
    scaled = upstream * gain
    centred = (
        scaled
        - jnp.mean(scaled, -1, keepdims=True)
        - normed * jnp.mean(scaled * normed, -1, keepdims=True)
    )
    return centred * inverse, jnp.sum(upstream * normed, 0)


def part_of(place, count):
    return (place % 2) * (count // 2) + place // 2


def turn_tables(position):
    half_width = HEAD // 2
    frequency = 10000.0 ** (-jnp.arange(half_width, dtype=WIDE) / half_width)
    angles = position.astype(WIDE)[:, None] * frequency[None, :]
    cosine, sine = jnp.cos(angles), jnp.sin(angles)
    return jnp.concatenate([cosine, cosine], 1), jnp.concatenate([-sine, sine], 1)


def swapped(rows):
    return pltpu.roll(rows, HEAD // 2, 1)


def silu_slope(hidden, sigma):
    return sigma * (1.0 + hidden * (1.0 - sigma))


def project_kernel(in_ref, matrix_ref, cos_ref, sin_ref, q_ref, kv_ref):
    out = dot(in_ref[...], matrix_ref[...])
    cosine, sine = cos_ref[...], sin_ref[...]
    queries, keys = out[:, :HEAD], out[:, HEAD : 2 * HEAD]
    q_ref[...] = (queries * cosine + swapped(queries) * sine).astype(LOW)
    kv_ref[:, :HEAD] = (keys * cosine + swapped(keys) * sine).astype(LOW)
    kv_ref[:, HEAD:] = out[:, 2 * HEAD :].astype(LOW)


def project(entered, matrix, tables, rows=512):
    count = entered.shape[0]

    def row(width):
        return pl.BlockSpec((rows, width), lambda i: (i, 0))

    return pl.pallas_call(
        project_kernel,
        grid=(count // rows,),
        in_specs=[row(D), pl.BlockSpec(matrix.shape, lambda i: (0, 0)), row(HEAD), row(HEAD)],
        out_specs=[row(HEAD), row(2 * HEAD)],
        out_shape=[
            jax.ShapeDtypeStruct((count, HEAD), LOW),
            jax.ShapeDtypeStruct((count, 2 * HEAD), LOW),
        ],
        compiler_params=pltpu.CompilerParams(vmem_limit_bytes=32 * 2**20),
        cost_estimate=pl.CostEstimate(
            flops=6 * count * D * HEAD, bytes_accessed=6 * count * D, transcendentals=0
        ),
        name="project",
    )(entered, matrix, *tables)


def gather_keys(pieces, kv_ref):
    @pl.when(pl.program_id(0) == 0)
    def _():
        at = 0
        for piece in pieces:
            kv_ref[at : at + piece.shape[0], :] = piece[...]
            at += piece.shape[0]


def attend_kernel(lo_ref, hi_ref, q_ref, start_ref, end_ref, *rest, count, depth):
    pieces = rest[:count]
    low_ref, mix_ref, lse_ref, kv_ref = rest[count:]
    gather_keys(pieces, kv_ref)
    i = pl.program_id(0)
    queries = q_ref[...]
    rows = queries.shape[0]
    first, last = start_ref[0], end_ref[0]

    def step(t, carry):
        top, total, mixed = carry
        at = pl.multiple_of(t * depth, depth)
        keys = kv_ref[pl.ds(at, depth), :HEAD]
        values = kv_ref[pl.ds(at, depth), HEAD:]
        index = lax.broadcasted_iota(jnp.int32, (depth, 1), 0) + at
        scores = dot_nt(keys, queries) * SCALE_2
        inside = jnp.logical_and(index >= first, index < last)
        scores = jnp.where(inside, scores, MASKED)
        new_top = jnp.maximum(top, jnp.max(scores, 0, keepdims=True))
        probs = jnp.exp2(scores - new_top)
        fade = jnp.exp2(top - new_top)
        total = fade * total + jnp.sum(probs, 0, keepdims=True)
        mixed = fade * mixed + dot_tn(values, probs.astype(LOW))
        return new_top, total, mixed

    start = (jnp.full((1, rows), MASKED, WIDE), jnp.zeros((1, rows), WIDE), jnp.zeros((HEAD, rows), WIDE))
    top, total, mixed = lax.fori_loop(lo_ref[i], hi_ref[i], step, start)
    mixed = jnp.transpose(mixed / total)
    mix_ref[...] = mixed
    low_ref[...] = mixed.astype(LOW)
    lse_ref[0] = top + jnp.log2(total)


def attend_back_kernel(
    lo_ref, hi_ref, q_ref, do_ref, mix_ref, lse_ref, start_ref, end_ref, cos_ref, sin_ref, *rest, count, depth, parts
):
    pieces = rest[:count]
    dq_ref = rest[count]
    grads = rest[count + 1 : 2 * count + 1]
    kv_ref, dkv_ref = rest[2 * count + 1 :]
    gather_keys(pieces, kv_ref)
    i = pl.program_id(0)

    @pl.when(i == 0)
    def _():
        dkv_ref[...] = jnp.zeros_like(dkv_ref)

    queries, upstream = q_ref[...], do_ref[...]
    lse, first, last = lse_ref[0], start_ref[0], end_ref[0]
    products = jnp.transpose(upstream.astype(WIDE) * mix_ref[...])
    delta = jnp.sum(products, 0, keepdims=True)
    height = depth // parts

    def step(t, grad_query):
        for part in range(parts):
            at = pl.multiple_of(t * depth + part * height, height)
            span = pl.ds(at, height)
            keys = kv_ref[span, :HEAD]
            values = kv_ref[span, HEAD:]
            index = lax.broadcasted_iota(jnp.int32, (height, 1), 0) + at
            inside = jnp.logical_and(index >= first, index < last)
            scores = dot_nt(keys, queries) * SCALE_2
            probs = jnp.where(inside, jnp.exp2(scores - lse), 0.0)
            grad_probs = dot_nt(values, upstream)
            grad_scores = (probs * (grad_probs - delta)).astype(LOW)
            dkv_ref[span, HEAD:] += dot(probs.astype(LOW), upstream)
            dkv_ref[span, :HEAD] += dot(grad_scores, queries)
            grad_query = grad_query + dot_tn(grad_scores, keys)
        return grad_query

    grad_query = lax.fori_loop(lo_ref[i], hi_ref[i], step, jnp.zeros(queries.shape, WIDE)) * SCALE
    dq_ref[...] = (grad_query * cos_ref[...] - swapped(grad_query) * sin_ref[...]).astype(LOW)

    @pl.when(i == pl.num_programs(0) - 1)
    def _():
        at = 0
        for grad in grads:
            span = slice(at, at + grad.shape[0])
            grad[:, :HEAD] = (dkv_ref[span, :HEAD] * SCALE).astype(grad.dtype)
            grad[:, HEAD:] = dkv_ref[span, HEAD:].astype(grad.dtype)
            at += grad.shape[0]


def whole_block(array):
    return pl.BlockSpec(array.shape, lambda i, *_: (0,) * len(array.shape))


def bounds(starts, ends, rows, depth, key_rows):
    count = key_rows // depth
    lo = jnp.clip(starts[::rows] // depth, 0, count)
    hi = jnp.clip((ends[rows - 1 :: rows] + depth - 1) // depth, 0, count)
    return lo.astype(jnp.int32), hi.astype(jnp.int32)


def attention_call(kernel, by_row, by_lane, pieces, spans, out_rows, out_lanes, grads, rows, depth, name, **more):
    count = by_row[0].shape[0]
    key_rows = sum(piece.shape[0] for piece in pieces)
    lo, hi = bounds(*spans, rows, depth, key_rows)
    row = pl.BlockSpec((rows, HEAD), lambda i, *_: (i, 0))
    lane = pl.BlockSpec((1, 1, rows), lambda i, *_: (i, 0, 0))
    lanes = [v.reshape(count // rows, 1, rows) for v in by_lane + list(spans)]
    tail = more.pop("tail", [])
    scratch = [pltpu.VMEM((key_rows, 2 * HEAD), LOW)]
    if grads:
        scratch.append(pltpu.VMEM((key_rows, 2 * HEAD), WIDE))
    return pl.pallas_call(
        functools.partial(kernel, count=len(pieces), depth=depth, **more),
        grid_spec=pltpu.PrefetchScalarGridSpec(
            num_scalar_prefetch=2,
            grid=(count // rows,),
            in_specs=[row] * len(by_row) + [lane] * len(lanes) + [row] * len(tail) + [whole_block(p) for p in pieces],
            out_specs=[row] * len(out_rows) + [lane] * out_lanes + [whole_block(g) for g in grads],
            scratch_shapes=scratch,
        ),
        out_shape=[jax.ShapeDtypeStruct((count, HEAD), kind) for kind in out_rows]
        + [jax.ShapeDtypeStruct((count // rows, 1, rows), WIDE)] * out_lanes
        + grads,
        compiler_params=pltpu.CompilerParams(vmem_limit_bytes=60 * 2**20),
        cost_estimate=pl.CostEstimate(
            flops=(40 if grads else 30) * count * LONGEST * HEAD,
            bytes_accessed=16 * 2**20,
            transcendentals=count * LONGEST,
        ),
        name=name,
    )(lo, hi, *by_row, *lanes, *tail, *pieces)


def attend(queries, pieces, spans, rows=512, depth=1024):
    return attention_call(
        attend_kernel, [queries], [], pieces, spans, [LOW, WIDE], 1, [], rows, depth, "attend"
    )


def attend_back(queries, upstream, mixed, lse, tables, pieces, spans, rows=512, depth=1024):
    middle = len(pieces) // 2
    grads = [
        jax.ShapeDtypeStruct(p.shape, WIDE if j == middle else LOW) for j, p in enumerate(pieces)
    ]
    return attention_call(
        attend_back_kernel,
        [queries, upstream, mixed],
        [lse],
        pieces,
        spans,
        [LOW],
        0,
        grads,
        rows,
        depth,
        "attend_back",
        tail=list(tables),
        parts=2,
    )


def gathered_kernel(dq_ref, own_ref, cos_ref, sin_ref, *rest, places):
    out_ref = rest[-1]
    i = pl.program_id(0)
    grad = own_ref[...]
    for ref, (first, count) in zip(rest, places):
        here = jnp.logical_and(i >= first, i < first + count)
        grad = grad + jnp.where(here, ref[...].astype(WIDE), 0.0)
    keys = grad[:, :HEAD]
    out_ref[:, :HEAD] = dq_ref[...]
    out_ref[:, HEAD : 2 * HEAD] = (keys * cos_ref[...] - swapped(keys) * sin_ref[...]).astype(LOW)
    out_ref[:, 2 * HEAD :] = grad[:, HEAD:].astype(LOW)


def gathered(grad_query, own, tables, arrivals, rows=512):
    count = own.shape[0]
    places = [(first // rows, part.shape[0] // rows) for first, part in arrivals]

    def row(width):
        return pl.BlockSpec((rows, width), lambda i: (i, 0))

    def part(place):
        return pl.BlockSpec((rows, 2 * HEAD), lambda i: (jnp.clip(i - place[0], 0, place[1] - 1), 0))

    return pl.pallas_call(
        functools.partial(gathered_kernel, places=places),
        grid=(count // rows,),
        in_specs=[row(HEAD), row(2 * HEAD), row(HEAD), row(HEAD)] + [part(place) for place in places],
        out_specs=row(3 * HEAD),
        out_shape=jax.ShapeDtypeStruct((count, 3 * HEAD), LOW),
        cost_estimate=pl.CostEstimate(flops=0, bytes_accessed=16 * 2**20, transcendentals=0),
        name="gathered",
    )(grad_query, own, *tables, *[array for _, array in arrivals])


def on_device(
    acoustic_features,
    clip_durations,
    early_layernorm_scale,
    early_widening_matrix,
    early_narrowing_matrix,
    mixer_layernorm_scale,
    triple_matrix,
    mixer_exit_matrix,
    filter_layernorm_scale,
    gating_pair_matrix,
    depthwise_filter,
    running_stats_factor,
    running_stats_offset,
    filter_exit_projection,
    later_layernorm_scale,
    later_widening_matrix,
    later_narrowing_matrix,
    last_layernorm_scale,
    quantizer_projection,
    entry_vectors,
    smoothing_level,
    random_flat_samples,
    expected_entries,
    result_adjoint,
    discrete_adjoint,
):
    seq_count, mp_count = lax.axis_size("seq"), lax.axis_size("mp")
    seq_at, mp_at = lax.axis_index("seq"), lax.axis_index("mp")
    core = seq_at % 2
    frame_rows = acoustic_features.shape[0]
    all_rows = frame_rows * seq_count
    own = frame_rows // mp_count
    own_base = seq_at * frame_rows + mp_at * own

    local_heads = triple_matrix.shape[2] // HEAD
    group_place = seq_at % local_heads
    groups = [
        [(z * local_heads + g) * mp_count + m for g in range(local_heads) for m in range(mp_count)]
        for z in range(seq_count // local_heads)
    ]
    group_size = local_heads * mp_count
    line = seq_count // local_heads
    lines = [
        [(z * local_heads + g) * mp_count + m for z in range(line)] for g in range(local_heads) for m in range(mp_count)
    ]

    def own_rows(shard):
        size = shard.shape[0] // local_heads
        return cut(shard, part_of(group_place, local_heads) * size, size)

    def own_columns(shard):
        size = shard.shape[1] // local_heads
        return cut(shard, part_of(group_place, local_heads) * size, size, 1).T

    def over_group(part):
        return lax.all_gather(part, BOTH, axis_index_groups=groups, axis=0)

    def grouped(array):
        parts = array.reshape(-1, mp_count, local_heads, array.shape[1] // group_size)
        parts = jnp.stack([parts[:, :, part_of(g, local_heads)] for g in range(local_heads)], 1)
        return parts.reshape(array.shape)

    def ungrouped(array):
        parts = array.reshape(-1, local_heads, mp_count, array.shape[1] // group_size)
        places = sorted(range(local_heads), key=lambda g: part_of(g, local_heads))
        return jnp.stack([parts[:, g] for g in places], 2).reshape(array.shape)

    def group_total(array, over=None):
        return lax.psum_scatter(array, BOTH, scatter_dimension=0, axis_index_groups=over or groups, tiled=True)

    def rel_rows(array, k):
        return cut(array, mp_place(k) * own, own)

    def local_halves(array):
        half = array.shape[1] // 2
        return [cut(array, (core ^ j) * half, half, 1) for j in range(2)]

    small_weights = jnp.concatenate(
        [depthwise_filter, running_stats_factor[None], running_stats_offset[None]], 0
    )
    small_all = grouped(joined(from_mp(small_weights), 1))
    filter_all, factor_all, offset_all = small_all[:KERNEL], small_all[KERNEL], small_all[KERNEL + 1]

    code_parts = jnp.stack([own_columns(quantizer_projection), own_rows(entry_vectors)])
    noise_parts = [-jnp.log(-jnp.log(rel_rows(random_flat_samples, k))) for k in range(mp_count)]
    noise_parts = noise_parts[:1] + [part.astype(LOW) for part in noise_parts[1:]]
    first_rows, code_parts, noise_parts = paced(acoustic_features, code_parts, noise_parts)
    code_every = over_group(code_parts)
    noise_parts = noise_parts[:1] + [mp_shift(part, k).astype(WIDE) for k, part in enumerate(noise_parts) if k]

    first = []
    for k in list(range(1, mp_count)) + [0]:
        rows = rel_rows(first_rows, k).astype(WIDE)
        entered, normed, inverse = norm_forward(rows, early_layernorm_scale)
        hidden = dot(entered, early_widening_matrix)
        activated = (hidden * jax.nn.sigmoid(hidden)).astype(LOW)
        part = dot(activated, early_narrowing_matrix).astype(LOW)
        first.append((part, entered, hidden, activated, normed, inverse))
    first = [first[-1]] + first[:-1]
    features = rel_rows(acoustic_features, 0).astype(WIDE)
    group_rows = local_heads * frame_rows
    group_at = seq_at // local_heads
    group_index = group_at * group_rows + jnp.arange(group_rows, dtype=jnp.int32)
    _, group_start, group_end = clip_of(clip_durations, group_index)
    tables = turn_tables(group_index - group_start)
    head_matrix = cut(triple_matrix, part_of(group_place, local_heads) * HEAD, HEAD, 2)
    head_matrix = jnp.concatenate([head_matrix[i] for i in range(3)], 1)
    middle_parts = [
        own_rows(mixer_exit_matrix),
        own_columns(gating_pair_matrix[0]),
        own_columns(gating_pair_matrix[1]),
        own_rows(filter_exit_projection),
    ]
    up_part, down_part = own_columns(later_widening_matrix), own_rows(later_narrowing_matrix)
    after_ffn = features + 0.5 * to_mp([f[0] for f in first])
    after_ffn, tables, sent = paced(
        after_ffn, tables, (jnp.stack(middle_parts), up_part, down_part, head_matrix)
    )

    quantizer_all, book_all = code_every[:, 0].reshape(-1, D), code_every[:, 1].reshape(-1, D)
    noise = grouped(joined([noise_parts[0]] + noise_parts[:0:-1], 1))
    temper = smoothing_level[0]
    own_features = rel_rows(acoustic_features, 0)
    noisy = dot_nt(own_features, quantizer_all) + noise
    tempered = noisy / temper
    assigned = jnp.exp(tempered - jax.nn.logsumexp(tempered, -1)[:, None])
    assigned_low = assigned.astype(LOW)
    quant_low = dot(assigned_low, book_all).astype(LOW)
    own_discrete = rel_rows(discrete_adjoint, 0)
    grad_soft = dot_nt(own_discrete, book_all)
    row_dot = jnp.sum(assigned * grad_soft, -1)
    grad_tempered = assigned * (grad_soft - row_dot[:, None])
    grad_temper = -jnp.sum(grad_tempered * noisy) / (temper * temper)
    grad_entry = (grad_tempered / temper).astype(LOW)
    quant_in = dot(grad_entry, quantizer_all)

    att_entered, att_normed, att_inverse = norm_forward(after_ffn, mixer_layernorm_scale)
    att_group = over_group(att_entered).reshape(group_rows, D)
    reaches = range(1, -(-(LONGEST - 1) // group_rows) + 1)
    halo = [min(group_rows, -(-(LONGEST - (r - 1) * group_rows) // 1024) * 1024) for r in reaches]
    halo_rows = sum(halo)
    key_base = group_at * group_rows - halo_rows
    spans = (group_start - key_base, group_end - key_base)
    att_group, assigned_low, quant_low, sent = paced(att_group, assigned_low, quant_low, sent)
    middle_every = over_group(sent[0])
    head_matrix = sent[3]
    exit_all, value_all, gate_all, point_all = [middle_every[:, i].reshape(-1, D) for i in range(4)]
    up_all = over_group(sent[1]).reshape(-1, D)
    down_all = over_group(sent[2]).reshape(-1, D)
    query_rot, kv_own = project(att_group, head_matrix, tables)
    lower = [seq_shift(kv_own[group_rows - n :], local_heads * r) for r, n in zip(reaches, halo)]
    upper = [seq_shift(kv_own[:n], -local_heads * r) for r, n in zip(reaches, halo)]
    kv_pieces = lower[::-1] + [kv_own] + upper
    mixed_low, mixed, row_lse = attend(query_rot, kv_pieces, spans)
    mixed_low, head_sent, grad_entry, quant_in, grad_temper = paced(
        mixed_low, head_matrix, grad_entry, quant_in, grad_temper
    )
    heads_all = over_group(head_sent)

    def exchange(array):
        return lax.all_to_all(array, BOTH, 0, 0, axis_index_groups=groups)

    att_parts = exchange(mixed_low.reshape(group_size, own, HEAD))
    att_low = jnp.transpose(att_parts, (1, 0, 2)).reshape(own, D)
    after_att = after_ffn + dot(att_low, exit_all)

    half_kernel = KERNEL // 2
    pad_index = own_base - half_kernel + jnp.arange(own + 2 * half_kernel, dtype=jnp.int32)
    pad_seg = clip_of(clip_durations, pad_index)[0]
    pad_seg = jnp.where(jnp.logical_and(pad_index >= 0, pad_index < all_rows), pad_seg, -1)
    own_seg = pad_seg[half_kernel : half_kernel + own]
    masks = [(pad_seg[j : j + own] == own_seg)[:, None] for j in range(KERNEL)]

    def padded(block):
        low = flat_shift(block[own - half_kernel :], 1)
        high = flat_shift(block[:half_kernel], -1)
        return jnp.concatenate([low, block, high], 0).astype(WIDE)

    conv_entered, conv_normed, conv_inverse = norm_forward(after_att, filter_layernorm_scale)
    glu_value = dot_nt(conv_entered, value_all)
    glu_gate = jax.nn.sigmoid(dot_nt(conv_entered, gate_all))
    glu_low = (glu_value * glu_gate).astype(LOW)
    glu_padded = padded(glu_low)
    conv_out = jnp.zeros((own, D), WIDE)
    for j in range(KERNEL):
        conv_out = conv_out + filter_all[j][None, :] * jnp.where(masks[j], glu_padded[j : j + own], 0.0)
    sums = total_over_all(jnp.stack([jnp.sum(conv_out, 0), jnp.sum(conv_out * conv_out, 0)]), 1)
    bn_mean = sums[0] / all_rows
    bn_inv = lax.rsqrt(sums[1] / all_rows - bn_mean * bn_mean + EPSILON)
    bn_hat = (conv_out - bn_mean) * bn_inv
    bn_out = bn_hat * factor_all + offset_all
    bn_sigma = jax.nn.sigmoid(bn_out)
    swish_low = (bn_out * bn_sigma).astype(LOW)
    after_conv = after_att + dot(swish_low, point_all)

    late_entered, late_normed, late_inverse = norm_forward(after_conv, later_layernorm_scale)
    late_hidden = dot_nt(late_entered, up_all)
    late_act = (late_hidden * jax.nn.sigmoid(late_hidden)).astype(LOW)
    branch = dot(late_act, down_all)
    after_two = after_conv + 0.5 * branch
    final_low, final_normed, final_inverse = norm_forward(after_two, last_layernorm_scale)

    codes = book_all.shape[0]
    logits = dot_nt(final_low, book_all) * D ** (-0.5)
    code_index = grouped(jnp.arange(codes, dtype=jnp.int32)[None, :])
    is_target = rel_rows(expected_entries, 0)[:, None] == code_index
    pred_lse = jax.nn.logsumexp(logits, -1)
    row_loss = pred_lse - jnp.sum(jnp.where(is_target, logits, 0.0), -1)
    grad_pred = (jnp.exp(logits - pred_lse[:, None]) - is_target.astype(WIDE)).astype(LOW)
    grad_final = rel_rows(result_adjoint, 0).astype(WIDE) + dot(grad_pred, book_all) * D ** (-0.5)
    grad_final, loss_shares = paced(grad_final, from_mp(row_loss))
    frame_loss = joined(loss_shares)
    grad_four, grad_ln_final = norm_backward(grad_final, last_layernorm_scale, final_normed, final_inverse)
    late_branch = (0.5 * grad_four).astype(LOW)
    grad_act = dot_nt(late_branch, down_all)
    grad_hidden = (grad_act * silu_slope(late_hidden, jax.nn.sigmoid(late_hidden))).astype(LOW)
    late_in = dot(grad_hidden, up_all)
    late_grads = products([[(grad_hidden, late_entered, None)], [(late_act, late_branch, None)]], group_size, line)
    late_norm_grad, grad_ln_ffn2 = norm_backward(late_in, later_layernorm_scale, late_normed, late_inverse)
    grad_three = grad_four + late_norm_grad

    conv_branch = grad_three.astype(LOW)
    grad_swish = dot_nt(conv_branch, point_all)
    grad_bn = grad_swish * silu_slope(bn_out, bn_sigma)
    back_sums = jnp.stack([jnp.sum(grad_bn, 0), jnp.sum(grad_bn * bn_hat, 0)])
    back_sums, late_grads, heads_all = paced(back_sums, late_grads, heads_all)
    late_part = group_total(late_grads)
    back_sums = total_over_all(back_sums, 2)
    grad_conv = (
        factor_all * bn_inv * (grad_bn - back_sums[0] / all_rows - bn_hat * back_sums[1] / all_rows)
    ).astype(LOW)
    grad_padded = padded(grad_conv)
    grad_exact = grad_conv.astype(WIDE)
    grad_taps = []
    grad_gated = jnp.zeros_like(grad_exact)
    for j in range(KERNEL):
        grad_taps.append(jnp.sum(grad_exact * jnp.where(masks[j], glu_padded[j : j + own], 0.0), 0))
        back = 2 * half_kernel - j
        grad_gated = grad_gated + filter_all[j][None, :] * jnp.where(
            masks[back], grad_padded[back : back + own], 0.0
        )
    grad_value = (grad_gated * glu_gate).astype(LOW)
    grad_gate = (grad_gated * glu_value * glu_gate * (1.0 - glu_gate)).astype(LOW)
    conv_in = dot(grad_value, value_all) + dot(grad_gate, gate_all)
    conv_norm_grad, grad_ln_conv = norm_backward(conv_in, filter_layernorm_scale, conv_normed, conv_inverse)
    grad_two = grad_three + conv_norm_grad

    att_branch = grad_two.astype(LOW)
    mixer_grads = products(
        [
            [(grad_value, conv_entered, None)],
            [(grad_gate, conv_entered, None)],
            [(swish_low, conv_branch, None)],
            [(att_low, att_branch, None)],
            [(grad_pred, final_low, D ** (-0.5)), (assigned_low, own_discrete, None)],
            [(grad_entry, own_features, None)],
        ],
        group_size,
        line,
    )
    grad_heads = dot_nt(att_branch, exit_all).astype(LOW)
    grad_heads = jnp.transpose(grad_heads.reshape(own, group_size, HEAD), (1, 0, 2))
    grad_mixed = exchange(grad_heads).reshape(group_rows, HEAD)
    grad_mixed, mixer_grads = paced(grad_mixed, mixer_grads)
    mixer_total = group_total(mixer_grads)
    grad_query, *grad_pieces = attend_back(query_rot, grad_mixed, mixed, row_lse, tables, kv_pieces, spans)
    grad_pieces, late_part = paced(grad_pieces, late_part)
    arrivals = []
    reach_count = len(halo)
    for r, n in zip(reaches, halo):
        back = seq_shift(grad_pieces[reach_count - r], -local_heads * r)
        arrivals.append((group_rows - n, back))
        back = seq_shift(grad_pieces[reach_count + r], local_heads * r)
        arrivals.append((0, back))
    grad_proj = gathered(grad_query, grad_pieces[reach_count], tables, arrivals)

    proj_parts = exchange(grad_proj.reshape(group_size, own, 3 * HEAD))
    head_grads = dot_tn(grad_proj, att_group).astype(LOW)
    proj_parts, head_grads = paced(proj_parts, head_grads)
    head_grads = jnp.transpose(head_grads.reshape(3, line, HEAD // line, D), (1, 0, 2, 3)).reshape(line, -1, D)
    att_in = lax.dot_general(
        proj_parts, heads_all, (((0, 2), (0, 2)), ((), ())), preferred_element_type=WIDE
    )
    att_norm_grad, grad_ln_att = norm_backward(att_in, mixer_layernorm_scale, att_normed, att_inverse)
    grad_one = grad_two + att_norm_grad
    grad_one, late_part, mixer_total, head_grads = paced(grad_one, late_part, mixer_total, head_grads)
    every_total = [part.reshape(line, -1, D) for part in (late_part, mixer_total, head_grads)]
    every_total = group_total(jnp.concatenate(every_total, 1).reshape(-1, D), lines)

    early_branch = from_mp((0.5 * grad_one).astype(LOW))
    early_in, early_grads = [], []
    for k, (_, entered, hidden, activated, _, _) in enumerate(first):
        grad_act = dot_nt(early_branch[k], early_narrowing_matrix)
        early_grads.append((grad_act * silu_slope(hidden, jax.nn.sigmoid(hidden))).astype(LOW))
        early_in.append(dot_nt(early_grads[k], early_widening_matrix))

    act_all = jnp.concatenate([f[3] for f in first], 0)
    branch_all = jnp.concatenate(early_branch, 0)
    entered_all = jnp.concatenate([f[1] for f in first], 0)
    hid_all = jnp.concatenate(early_grads, 0)
    up_parts = [dot_tn(entered_all, hid).astype(LOW) for hid in local_halves(hid_all)]
    down_parts = [dot_tn(act, branch_all).astype(LOW) for act in local_halves(act_all)]
    early_norm_grad, grad_ln_ffn1 = norm_backward(to_mp(early_in), early_layernorm_scale, first[0][4], first[0][5])
    frames_low = (grad_one + early_norm_grad + quant_in).astype(LOW)
    frames_low, every_total = paced(frames_low, every_total)
    every = lax.all_gather(every_total, "seq", axis=0)
    small, (grad_frames, layer_out, quantized), (up1_halves, down1_halves) = seq_total(
        [frames_low, final_low, quant_low],
        [up_parts[0], down_parts[0]],
        [up_parts[1], down_parts[1]],
        jnp.stack(
            [grad_ln_ffn1, grad_ln_att, grad_ln_conv, grad_ln_ffn2, grad_ln_final]
            + grad_taps
            + [jnp.full((D,), grad_temper, WIDE)]
        ),
        3,
    )
    late_rows = late_part.shape[0] // line // 2
    mixer_rows = mixer_total.shape[0] // line // 6
    up2_grad = laid(every, 0, late_rows, 1, local_heads, True)[0]
    down2_grad = laid(every, late_rows, late_rows, 1, local_heads, False)[0]

    def mixer_laid(at, amount, turned):
        return laid(every, 2 * late_rows + at * mixer_rows, mixer_rows, amount, local_heads, turned)

    gate_grads = mixer_laid(0, 2, True)
    point_grad, exit_grad, book_grad = [mixer_laid(at, 1, False)[0] for at in (2, 3, 4)]
    code_grad, qkv_grad = mixer_laid(5, 1, True)[0], mixer_laid(6, 3, True)
    up1_grad, down1_grad = beside(up1_halves, False), beside(down1_halves, True)
    own_channels = filter_exit_projection.shape[0]

    def own_part(array):
        return cut(ungrouped(array), mp_at * own_channels, own_channels, 1)

    bn_grads = own_part(back_sums)

    return (
        layer_out,
        quantized,
        frame_loss,
        grad_frames,
        small[0],
        up1_grad,
        down1_grad,
        small[1],
        qkv_grad,
        exit_grad,
        small[2],
        gate_grads,
        own_part(small[5 : 5 + KERNEL]),
        bn_grads[1],
        bn_grads[0],
        point_grad,
        small[3],
        up2_grad,
        down2_grad,
        small[4],
        code_grad,
        book_grad,
        small[5 + KERNEL, :1],
    )


def solution(mesh):
    in_specs = (
        P("seq", None),
        P(),
        P(),
        P(None, "mp"),
        P("mp", None),
        P(),
        P(None, None, "mp"),
        P("mp", None),
        P(),
        P(None, None, "mp"),
        P(None, "mp"),
        P("mp"),
        P("mp"),
        P("mp", None),
        P(),
        P(None, "mp"),
        P("mp", None),
        P(),
        P(None, "mp"),
        P("mp", None),
        P(),
        P("seq", "mp"),
        P("seq"),
        P("seq", None),
        P("seq", None),
    )
    out_specs = (
        P("seq", None),
        P("seq", None),
        P("seq"),
        P("seq", None),
        P(),
        P(None, "mp"),
        P("mp", None),
        P(),
        P(None, None, "mp"),
        P("mp", None),
        P(),
        P(None, None, "mp"),
        P(None, "mp"),
        P("mp"),
        P("mp"),
        P("mp", None),
        P(),
        P(None, "mp"),
        P("mp", None),
        P(),
        P(None, "mp"),
        P("mp", None),
        P(),
    )
    return jax.shard_map(
        on_device, mesh=mesh, in_specs=in_specs, out_specs=out_specs, check_vma=False
    )
```

```python
import functools
import math

import jax
import jax.numpy as jnp
from jax import lax
from jax.experimental import pallas as pl
from jax.experimental.pallas import tpu as pltpu
from jax.sharding import PartitionSpec as P

D = 1024
HEAD = 128
KERNEL = 5
LONGEST = 3008

EPSILON = 1e-05
MASKED = -1e30
SCALE = HEAD ** (-0.5)
SCALE_2 = SCALE * math.log2(math.e)
BOTH = ("seq", "mp")
LOW = jnp.bfloat16
WIDE = jnp.float32


def dot(a, b, dims=((1,), (0,))):
    return lax.dot_general(a, b, (dims, ((), ())), preferred_element_type=WIDE)


def dot_nt(a, b):
    return dot(a, b, ((1,), (1,)))


def dot_tn(a, b):
    return dot(a, b, ((0,), (0,)))


def cut(array, start, size, axis=0):
    return lax.dynamic_slice_in_dim(array, start, size, axis)


def mp_shift(shard, by):
    count = lax.axis_size("mp")
    return lax.ppermute(shard, "mp", [(i, (i + by) % count) for i in range(count)])


def seq_xor(shard, mask):
    return lax.ppermute(shard, "seq", [(i, i ^ mask) for i in range(lax.axis_size("seq"))])


def seq_shift(shard, by):
    count = lax.axis_size("seq")
    return lax.ppermute(shard, "seq", [(i, i + by) for i in range(count) if 0 <= i + by < count])


def flat_shift(shard, by):
    count = lax.axis_size("seq") * lax.axis_size("mp")
    return lax.ppermute(shard, BOTH, [(i, i + by) for i in range(count) if 0 <= i + by < count])


def from_mp(shard):
    return [shard] + [mp_shift(shard, -k) for k in range(1, lax.axis_size("mp"))]


def to_mp(parts):
    total = parts[0].astype(WIDE)
    for k in range(1, len(parts)):
        total = total + mp_shift(parts[k].astype(LOW), k).astype(WIDE)
    return total


def mp_place(k):
    return (lax.axis_index("mp") + k) % lax.axis_size("mp")


def joined(pieces, axis=0):
    size = pieces[0].shape[axis]
    shape = list(pieces[0].shape)
    shape[axis] = size * len(pieces)
    whole = jnp.zeros(shape, pieces[0].dtype)
    for k, piece in enumerate(pieces):
        whole = lax.dynamic_update_slice_in_dim(whole, piece, mp_place(k) * size, axis)
    return whole


def paced(*values):
    return lax.optimization_barrier(values)


def bit_count(number):
    return int(math.log2(number))


def laid_kernel(in_ref, out_ref, *, local_heads, turned):
    count, rows, _ = in_ref.shape
    height = count * rows // local_heads
    for g in range(local_heads):
        block = jnp.concatenate([in_ref[s] for s in range(g, count, local_heads)], 0).astype(WIDE)
        part = part_of(g, local_heads)
        if turned:
            out_ref[0, :, part * height : (part + 1) * height] = block.T
        else:
            out_ref[0, part * height : (part + 1) * height, :] = block


def laid(every, first, rows, amount, local_heads, turned):
    count, _, columns = every.shape
    if rows % 16 or count * rows % 128:
        order = sorted(range(count), key=lambda s: (part_of(s % local_heads, local_heads), s // local_heads))
        whole = every[:, first : first + amount * rows].reshape(count, amount, rows, columns)
        whole = jnp.stack([whole[s] for s in order], 1).astype(WIDE).reshape(amount, count * rows, columns)
        return jnp.transpose(whole, (0, 2, 1)) if turned else whole
    shape = (columns, count * rows) if turned else (count * rows, columns)
    width = min(columns, 2**19 // (count * rows))
    block = (1, width, count * rows) if turned else (1, count * rows, width)
    return pl.pallas_call(
        functools.partial(laid_kernel, local_heads=local_heads, turned=turned),
        grid=(amount, columns // width),
        in_specs=[pl.BlockSpec((count, rows, width), lambda i, j: (0, first // rows + i, j))],
        out_specs=pl.BlockSpec(block, lambda i, j: (i, j, 0) if turned else (i, 0, j)),
        out_shape=jax.ShapeDtypeStruct((amount,) + shape, WIDE),
        compiler_params=pltpu.CompilerParams(vmem_limit_bytes=32 * 2**20),
        cost_estimate=pl.CostEstimate(
            flops=0, bytes_accessed=6 * amount * shape[0] * shape[1], transcendentals=0
        ),
        name="laid",
    )(every)


def products_kernel(*refs, plan, line):
    out_ref = refs[-1]
    at = ref = 0
    for terms in plan:
        sum_of = None
        for scale in terms:
            term = dot_tn(refs[ref][...], refs[ref + 1][...])
            term = term if scale is None else term * scale
            sum_of = term if sum_of is None else sum_of + term
            ref += 2
        rows = sum_of.shape[0] // line
        for z in range(line):
            to = z * (out_ref.shape[1] // line) + at
            out_ref[0, to : to + rows, :] = sum_of[z * rows : (z + 1) * rows].astype(LOW)
        at += rows


def products(matrices, count, line):
    frames = matrices[0][0][0].shape[0]
    plan = [[term[2] for term in terms] for terms in matrices]
    operands, specs, height = [], [], 0
    for terms in matrices:
        width = terms[0][0].shape[1] // count
        height += width
        for left, right, _ in terms:
            operands += [left, right]
            specs += [
                pl.BlockSpec((frames, width), lambda i: (0, i)),
                pl.BlockSpec(right.shape, lambda i: (0, 0)),
            ]
    out = pl.pallas_call(
        functools.partial(products_kernel, plan=plan, line=line),
        grid=(count,),
        in_specs=specs,
        out_specs=pl.BlockSpec((1, height, D), lambda i: (i, 0, 0)),
        out_shape=jax.ShapeDtypeStruct((count, height, D), LOW),
        compiler_params=pltpu.CompilerParams(vmem_limit_bytes=50 * 2**20),
        cost_estimate=pl.CostEstimate(
            flops=2 * frames * height * count * D, bytes_accessed=2 * height * count * D, transcendentals=0
        ),
        name="products",
    )(*operands)
    return out.reshape(count * height, D)


def beside_kernel(in_ref, out_ref):
    out_ref[...] = in_ref[0].astype(WIDE)


def beside(halves, down, rows=1024):
    _, height, width = halves.shape
    rows = min(rows, height)
    steps = height // rows
    shape = (2 * height, width) if down else (height, 2 * width)

    def target(j, i):
        return (j * steps + i, 0) if down else (i, j)

    return pl.pallas_call(
        beside_kernel,
        grid=(2, steps),
        in_specs=[pl.BlockSpec((1, rows, width), lambda j, i: (j, i, 0))],
        out_specs=pl.BlockSpec((rows, width), target),
        out_shape=jax.ShapeDtypeStruct(shape, WIDE),
        compiler_params=pltpu.CompilerParams(vmem_limit_bytes=32 * 2**20),
        cost_estimate=pl.CostEstimate(flops=0, bytes_accessed=12 * height * width, transcendentals=0),
        name="beside",
    )(halves)


def remote(source, target, send, recv, device):
    return pltpu.make_async_remote_copy(
        src_ref=source,
        dst_ref=target,
        send_sem=send,
        recv_sem=recv,
        device_id=device,
        device_id_type=pl.DeviceIdType.MESH,
    )


def seq_partner(bit):
    return (lax.axis_index("seq") ^ (1 << bit), lax.axis_index("mp"))


def all_partners(seq_bits, mp_bits):
    mp = lax.axis_index("mp")
    across = [(lax.axis_index("seq"), mp ^ (1 << bit)) for bit in range(mp_bits)]
    return across + [seq_partner(bit) for bit in range(seq_bits)]


def meet(partners):
    barrier = pltpu.get_barrier_semaphore()
    for device in partners:
        pl.semaphore_signal(barrier, inc=1, device_id=device, device_id_type=pl.DeviceIdType.MESH)
    pl.semaphore_wait(barrier, len(partners))


class Small:
    def __init__(self, held, slots, send, recv, partners):
        self.held, self.slots, self.send, self.recv, self.partners = held, slots, send, recv, partners
        self.at = 0

    def copy(self, k):
        return remote(self.held.at[k], self.slots.at[k], self.send.at[k], self.recv.at[k], self.partners[k])

    def advance(self):
        k = self.at
        if k > len(self.partners):
            return
        if k > 0:
            self.copy(k - 1).wait_recv()
            self.held[k] = self.held[k - 1] + self.slots[k - 1]
        if k < len(self.partners):
            self.copy(k).start()
        self.at += 1

    def finish(self, out):
        while self.at <= len(self.partners):
            self.advance()
        for k in range(len(self.partners)):
            self.copy(k).wait_send()
        out[...] = self.held[len(self.partners)]


def small_scratch(shape, steps):
    dma = pltpu.SemaphoreType.DMA
    return [pltpu.VMEM((steps + 1,) + shape, WIDE), pltpu.VMEM((steps,) + shape, WIDE), dma((steps,)), dma((steps,))]


def total_kernel(in_ref, out_ref, held, slots, send, recv, *, seq_bits, mp_bits):
    partners = all_partners(seq_bits, mp_bits)
    meet(partners)
    held[0] = in_ref[...]
    Small(held, slots, send, recv, partners).finish(out_ref)


def total_over_all(values, collective_id):
    seq_bits, mp_bits = bit_count(lax.axis_size("seq")), bit_count(lax.axis_size("mp"))
    flat = values.reshape(-1, HEAD)
    space = pl.BlockSpec(memory_space=pltpu.VMEM)
    out = pl.pallas_call(
        functools.partial(total_kernel, seq_bits=seq_bits, mp_bits=mp_bits),
        in_specs=[space],
        out_specs=space,
        out_shape=jax.ShapeDtypeStruct(flat.shape, WIDE),
        scratch_shapes=small_scratch(flat.shape, seq_bits + mp_bits),
        compiler_params=pltpu.CompilerParams(collective_id=collective_id, has_side_effects=True),
        name="total_over_all",
    )(flat)
    return out.reshape(values.shape)


def seq_total_kernel(small_ref, *refs, count, chunks, seq_bits, mp_bits, share_count):
    shares, refs = refs[:share_count], refs[share_count:]
    mine, other = refs[:count], refs[count : 2 * count]
    small_out, refs = refs[2 * count], refs[2 * count + 1 :]
    shared, refs = refs[:share_count], refs[share_count:]
    outs, scratch = refs[:count], refs[count:]
    (share_local, share_send, share_recv), scratch = scratch[:3], scratch[3:]
    arrived, held = scratch[:count], scratch[count : 2 * count]
    levels = seq_bits - 1
    slots = [scratch[(2 + i) * count : (3 + i) * count] for i in range(levels)]
    core_send, core_recv, back_core_send, back_core_recv, send, recv, back_send, back_recv = scratch[
        (2 + levels) * count : (2 + levels) * count + 8
    ]
    partners = all_partners(seq_bits, mp_bits)
    mp, mp_count = lax.axis_index("mp"), 1 << mp_bits
    along_mp = [(lax.axis_index("seq"), (mp + k) % mp_count) for k in range(1, mp_count)]
    meet(along_mp + partners[mp_bits:])

    def share_rows(i, index):
        rows = shares[i].shape[0]
        return shared[i].at[pl.ds(pl.multiple_of(index * rows, 16), rows)]

    def share_copy(i, k, index):
        return remote(
            shares[i], share_rows(i, index), share_send.at[i, k - 1], share_recv.at[i, k - 1], along_mp[k - 1]
        )

    def share_own(i):
        return pltpu.make_async_copy(shares[i], share_rows(i, mp), share_local.at[i])

    small = Small(*scratch[(2 + levels) * count + 8 :], partners)
    small.held[0] = small_ref[...]
    seq = lax.axis_index("seq")
    core, sibling = seq % 2, seq_partner(0)

    plan = []
    for a in range(count):
        rows = mine[a].shape[0] // chunks[a]
        plan += [(a, c * rows, rows) for c in range(chunks[a])]
    everything = range(len(plan))

    def base(n, level):
        first, rows = plan[n][1:]
        for bit in range(1, level + 1):
            first = first + ((seq >> bit) & 1) * (rows >> bit)
        return first

    def span(n, level, kept):
        side = (seq >> level) & 1
        size = plan[n][2] >> level
        first = base(n, level - 1) + (side if kept else 1 - side) * size
        return pl.ds(pl.multiple_of(first, 16), size)

    def slot(n, level):
        return pl.ds(plan[n][1] >> level, plan[n][2] >> level)

    def whole(n):
        return pl.ds(plan[n][1], plan[n][2])

    def core_copy(n):
        a = plan[n][0]
        return remote(other[a].at[whole(n)], arrived[a].at[whole(n)], core_send.at[n], core_recv.at[n], sibling)

    def copy(n, level):
        a = plan[n][0]
        return remote(
            held[a].at[span(n, level, False)],
            slots[level - 1][a].at[slot(n, level)],
            send.at[n, level - 1],
            recv.at[n, level - 1],
            seq_partner(level),
        )

    def back_copy(n, level, arriving):
        rows = outs[plan[n][0]].at[core, span(n, level, not arriving)]
        return remote(rows, rows, back_send.at[n, level - 1], back_recv.at[n, level - 1], seq_partner(level))

    def back_core_copy(n, arriving):
        rows = outs[plan[n][0]].at[1 - core if arriving else core, whole(n)]
        return remote(rows, rows, back_core_send.at[n], back_core_recv.at[n], sibling)

    def fold(n, level):
        a = plan[n][0]
        copy(n, level).wait_recv()
        kept = span(n, level, True)
        total = held[a][kept, :].astype(WIDE) + slots[level - 1][a][slot(n, level), :].astype(WIDE)
        if level < levels:
            held[a][kept, :] = total.astype(LOW)
            copy(n, level + 1).start()
        else:
            outs[a][core, kept, :] = total.astype(LOW)
            back_copy(n, level, False).start()

    def unfold(n, level):
        back_copy(n, level, True).wait_recv()
        back_copy(n, level - 1, False).start()

    small.advance()
    for n in everything:
        core_copy(n).start()
    def enter(n):
        a = plan[n][0]
        core_copy(n).wait_recv()
        held[a][whole(n), :] = (mine[a][whole(n), :].astype(WIDE) + arrived[a][whole(n), :].astype(WIDE)).astype(LOW)
        copy(n, 1).start()

    for n in range(2):
        enter(n)
    small.advance()
    for i in range(share_count):
        share_own(i).start()
        for k in range(1, mp_count):
            share_copy(i, k, mp).start()
    stages = [functools.partial(fold, level=level) for level in range(1, levels + 1)]
    stages += [functools.partial(unfold, level=level) for level in range(levels, 1, -1)]
    for t in range(len(plan) + len(stages) - 1):
        if t + 2 < len(plan):
            enter(t + 2)
        for number in reversed(range(len(stages))):
            if 0 <= t - number < len(plan):
                stages[number](t - number)
        small.advance()
    for n in everything:
        back_copy(n, 1, True).wait_recv()
        back_core_copy(n, False).start()
    for n in everything:
        back_core_copy(n, True).wait_recv()
        core_copy(n).wait_send()
        back_core_copy(n, False).wait_send()
        for level in range(1, levels + 1):
            copy(n, level).wait_send()
            back_copy(n, level, False).wait_send()
    small.finish(small_out)
    for i in range(share_count):
        share_own(i).wait()
        for k in range(1, mp_count):
            share_copy(i, k, (mp + mp_count - k) % mp_count).wait_recv()
            share_copy(i, k, mp).wait_send()


def seq_total(shares, mine, other, small, collective_id):
    seq_bits, mp_bits = bit_count(lax.axis_size("seq")), bit_count(lax.axis_size("mp"))
    levels = seq_bits - 1
    chunks = [min(4, max(1, part.shape[0] // (16 << levels))) for part in mine]
    count, total = len(mine), sum(chunks)
    flat = small.reshape(-1, HEAD)
    space, far = pl.BlockSpec(memory_space=pltpu.VMEM), pl.BlockSpec(memory_space=pl.ANY)
    shapes = [part.shape for part in mine]
    dma = pltpu.SemaphoreType.DMA
    out = pl.pallas_call(
        functools.partial(
            seq_total_kernel,
            count=count,
            chunks=chunks,
            seq_bits=seq_bits,
            mp_bits=mp_bits,
            share_count=len(shares),
        ),
        in_specs=[space] + [far] * len(shares) + [space] * (2 * count),
        out_specs=[space] + [far] * len(shares) + [space] * count,
        out_shape=[jax.ShapeDtypeStruct(flat.shape, WIDE)]
        + [jax.ShapeDtypeStruct((part.shape[0] << mp_bits, part.shape[1]), part.dtype) for part in shares]
        + [jax.ShapeDtypeStruct((2,) + shape, LOW) for shape in shapes],
        scratch_shapes=[dma((len(shares),))]
        + [dma((len(shares), max(1, (1 << mp_bits) - 1)))] * 2
        + [pltpu.VMEM(shape, LOW) for shape in shapes] * 2
        + [pltpu.VMEM((rows >> level, width), LOW) for level in range(1, levels + 1) for rows, width in shapes]
        + [dma((total,))] * 4
        + [dma((total, levels))] * 4
        + small_scratch(flat.shape, seq_bits + mp_bits),
        compiler_params=pltpu.CompilerParams(
            collective_id=collective_id, has_side_effects=True, vmem_limit_bytes=56 * 2**20
        ),
        cost_estimate=pl.CostEstimate(flops=10**11, bytes_accessed=32 * 2**20, transcendentals=0),
        name="seq_total",
    )(flat, *shares, *mine, *other)
    return out[0].reshape(small.shape), out[1 : 1 + len(shares)], out[1 + len(shares) :]


def clip_of(clip_durations, positions):
    clip_ends = jnp.cumsum(clip_durations, dtype=jnp.int32)
    passed = clip_ends[None, :] <= positions[:, None]
    segment = jnp.sum(passed.astype(jnp.int32), 1, dtype=jnp.int32)
    starts = jnp.sum(jnp.where(passed, clip_durations[None, :], 0), 1, dtype=jnp.int32)
    ends = jnp.min(jnp.where(passed, 2**30, clip_ends[None, :]), 1)
    return segment, starts, ends


def norm_forward(rows, gain):
    centred = rows - jnp.mean(rows, -1, keepdims=True)
    inverse = lax.rsqrt(jnp.mean(centred * centred, -1, keepdims=True) + EPSILON)
    normed = centred * inverse
    return (normed * gain).astype(LOW), normed, inverse


def norm_backward(upstream, gain, normed, inverse):
    scaled = upstream * gain
    centred = (
        scaled
        - jnp.mean(scaled, -1, keepdims=True)
        - normed * jnp.mean(scaled * normed, -1, keepdims=True)
    )
    return centred * inverse, jnp.sum(upstream * normed, 0)


def part_of(place, count):
    return (place % 2) * (count // 2) + place // 2


def turn_tables(position):
    half_width = HEAD // 2
    frequency = 10000.0 ** (-jnp.arange(half_width, dtype=WIDE) / half_width)
    angles = position.astype(WIDE)[:, None] * frequency[None, :]
    cosine, sine = jnp.cos(angles), jnp.sin(angles)
    return jnp.concatenate([cosine, cosine], 1), jnp.concatenate([-sine, sine], 1)


def swapped(rows):
    return pltpu.roll(rows, HEAD // 2, 1)


def silu_slope(hidden, sigma):
    return sigma * (1.0 + hidden * (1.0 - sigma))


def project_kernel(in_ref, matrix_ref, cos_ref, sin_ref, q_ref, kv_ref):
    out = dot(in_ref[...], matrix_ref[...])
    cosine, sine = cos_ref[...], sin_ref[...]
    queries, keys = out[:, :HEAD], out[:, HEAD : 2 * HEAD]
    q_ref[...] = (queries * cosine + swapped(queries) * sine).astype(LOW)
    kv_ref[:, :HEAD] = (keys * cosine + swapped(keys) * sine).astype(LOW)
    kv_ref[:, HEAD:] = out[:, 2 * HEAD :].astype(LOW)


def project(entered, matrix, tables, rows=512):
    count = entered.shape[0]

    def row(width):
        return pl.BlockSpec((rows, width), lambda i: (i, 0))

    return pl.pallas_call(
        project_kernel,
        grid=(count // rows,),
        in_specs=[row(D), pl.BlockSpec(matrix.shape, lambda i: (0, 0)), row(HEAD), row(HEAD)],
        out_specs=[row(HEAD), row(2 * HEAD)],
        out_shape=[
            jax.ShapeDtypeStruct((count, HEAD), LOW),
            jax.ShapeDtypeStruct((count, 2 * HEAD), LOW),
        ],
        compiler_params=pltpu.CompilerParams(vmem_limit_bytes=32 * 2**20),
        cost_estimate=pl.CostEstimate(
            flops=6 * count * D * HEAD, bytes_accessed=6 * count * D, transcendentals=0
        ),
        name="project",
    )(entered, matrix, *tables)


def gather_keys(pieces, kv_ref):
    @pl.when(pl.program_id(0) == 0)
    def _():
        at = 0
        for piece in pieces:
            kv_ref[at : at + piece.shape[0], :] = piece[...]
            at += piece.shape[0]


def attend_kernel(lo_ref, inner_ref, outer_ref, hi_ref, q_ref, start_ref, end_ref, *rest, count, depth):
    pieces = rest[:count]
    low_ref, mix_ref, lse_ref, kv_ref = rest[count:]
    gather_keys(pieces, kv_ref)
    i = pl.program_id(0)
    queries = q_ref[...]
    rows = queries.shape[0]
    first, last = start_ref[0], end_ref[0]

    def step(masked, t, carry):
        top, total, mixed = carry
        at = pl.multiple_of(t * depth, depth)
        keys = kv_ref[pl.ds(at, depth), :HEAD]
        values = kv_ref[pl.ds(at, depth), HEAD:]
        scores = dot_nt(keys, queries) * SCALE_2
        if masked:
            index = lax.broadcasted_iota(jnp.int32, (depth, 1), 0) + at
            inside = jnp.logical_and(index >= first, index < last)
            scores = jnp.where(inside, scores, MASKED)
        new_top = jnp.maximum(top, jnp.max(scores, 0, keepdims=True))
        probs = jnp.exp2(scores - new_top)
        fade = jnp.exp2(top - new_top)
        total = fade * total + jnp.sum(probs, 0, keepdims=True)
        mixed = fade * mixed + dot_tn(values, probs.astype(LOW))
        return new_top, total, mixed

    start = (jnp.full((1, rows), MASKED, WIDE), jnp.zeros((1, rows), WIDE), jnp.zeros((HEAD, rows), WIDE))
    top, total, mixed = over_blocks(step, start, lo_ref[i], inner_ref[i], outer_ref[i], hi_ref[i])
    mixed = jnp.transpose(mixed / total)
    mix_ref[...] = mixed
    low_ref[...] = mixed.astype(LOW)
    lse_ref[0] = top + jnp.log2(total)


def attend_back_kernel(
    lo_ref, inner_ref, outer_ref, hi_ref, q_ref, do_ref, mix_ref, lse_ref, start_ref, end_ref, cos_ref, sin_ref, *rest, count, depth, parts
):
    pieces = rest[:count]
    dq_ref = rest[count]
    grads = rest[count + 1 : 2 * count + 1]
    kv_ref, dkv_ref = rest[2 * count + 1 :]
    gather_keys(pieces, kv_ref)
    i = pl.program_id(0)

    @pl.when(i == 0)
    def _():
        dkv_ref[...] = jnp.zeros_like(dkv_ref)

    queries, upstream = q_ref[...], do_ref[...]
    lse, first, last = lse_ref[0], start_ref[0], end_ref[0]
    products = jnp.transpose(upstream.astype(WIDE) * mix_ref[...])
    delta = jnp.sum(products, 0, keepdims=True)
    height = depth // parts

    def step(masked, t, grad_query):
        for part in range(parts):
            at = pl.multiple_of(t * depth + part * height, height)
            span = pl.ds(at, height)
            keys = kv_ref[span, :HEAD]
            values = kv_ref[span, HEAD:]
            scores = dot_nt(keys, queries) * SCALE_2
            probs = jnp.exp2(scores - lse)
            if masked:
                index = lax.broadcasted_iota(jnp.int32, (height, 1), 0) + at
                inside = jnp.logical_and(index >= first, index < last)
                probs = jnp.where(inside, probs, 0.0)
            grad_probs = dot_nt(values, upstream)
            grad_scores = (probs * (grad_probs - delta)).astype(LOW)
            dkv_ref[span, HEAD:] += dot(probs.astype(LOW), upstream)
            dkv_ref[span, :HEAD] += dot(grad_scores, queries)
            grad_query = grad_query + dot_tn(grad_scores, keys)
        return grad_query

    nothing = jnp.zeros(queries.shape, WIDE)
    grad_query = over_blocks(step, nothing, lo_ref[i], inner_ref[i], outer_ref[i], hi_ref[i]) * SCALE
    dq_ref[...] = (grad_query * cos_ref[...] - swapped(grad_query) * sin_ref[...]).astype(LOW)

    @pl.when(i == pl.num_programs(0) - 1)
    def _():
        at = 0
        for grad in grads:
            span = slice(at, at + grad.shape[0])
            grad[:, :HEAD] = (dkv_ref[span, :HEAD] * SCALE).astype(grad.dtype)
            grad[:, HEAD:] = dkv_ref[span, HEAD:].astype(grad.dtype)
            at += grad.shape[0]


def whole_block(array):
    return pl.BlockSpec(array.shape, lambda i, *_: (0,) * len(array.shape))


def over_blocks(step, carry, lo, inner, outer, hi):
    carry = lax.fori_loop(lo, inner, functools.partial(step, True), carry)
    carry = lax.fori_loop(inner, outer, functools.partial(step, False), carry)
    return lax.fori_loop(outer, hi, functools.partial(step, True), carry)


def bounds(starts, ends, rows, depth, key_rows):
    count = key_rows // depth
    lo = jnp.clip(starts[::rows] // depth, 0, count)
    hi = jnp.clip((ends[rows - 1 :: rows] + depth - 1) // depth, 0, count)
    inner = jnp.clip((starts[rows - 1 :: rows] + depth - 1) // depth, lo, hi)
    outer = jnp.clip(ends[::rows] // depth, inner, hi)
    return [b.astype(jnp.int32) for b in (lo, inner, outer, hi)]


def attention_call(kernel, by_row, by_lane, pieces, spans, out_rows, out_lanes, grads, rows, depth, name, **more):
    count = by_row[0].shape[0]
    key_rows = sum(piece.shape[0] for piece in pieces)
    blocks = bounds(*spans, rows, depth, key_rows)
    row = pl.BlockSpec((rows, HEAD), lambda i, *_: (i, 0))
    lane = pl.BlockSpec((1, 1, rows), lambda i, *_: (i, 0, 0))
    lanes = [v.reshape(count // rows, 1, rows) for v in by_lane + list(spans)]
    tail = more.pop("tail", [])
    scratch = [pltpu.VMEM((key_rows, 2 * HEAD), LOW)]
    if grads:
        scratch.append(pltpu.VMEM((key_rows, 2 * HEAD), WIDE))
    return pl.pallas_call(
        functools.partial(kernel, count=len(pieces), depth=depth, **more),
        grid_spec=pltpu.PrefetchScalarGridSpec(
            num_scalar_prefetch=4,
            grid=(count // rows,),
            in_specs=[row] * len(by_row) + [lane] * len(lanes) + [row] * len(tail) + [whole_block(p) for p in pieces],
            out_specs=[row] * len(out_rows) + [lane] * out_lanes + [whole_block(g) for g in grads],
            scratch_shapes=scratch,
        ),
        out_shape=[jax.ShapeDtypeStruct((count, HEAD), kind) for kind in out_rows]
        + [jax.ShapeDtypeStruct((count // rows, 1, rows), WIDE)] * out_lanes
        + grads,
        compiler_params=pltpu.CompilerParams(vmem_limit_bytes=60 * 2**20),
        cost_estimate=pl.CostEstimate(
            flops=(40 if grads else 30) * count * LONGEST * HEAD,
            bytes_accessed=16 * 2**20,
            transcendentals=count * LONGEST,
        ),
        name=name,
    )(*blocks, *by_row, *lanes, *tail, *pieces)


def attend(queries, pieces, spans, rows=512, depth=512):
    return attention_call(
        attend_kernel, [queries], [], pieces, spans, [LOW, WIDE], 1, [], rows, depth, "attend"
    )


def attend_back(queries, upstream, mixed, lse, tables, pieces, spans, rows=512, depth=512):
    middle = len(pieces) // 2
    grads = [
        jax.ShapeDtypeStruct(p.shape, WIDE if j == middle else LOW) for j, p in enumerate(pieces)
    ]
    return attention_call(
        attend_back_kernel,
        [queries, upstream, mixed],
        [lse],
        pieces,
        spans,
        [LOW],
        0,
        grads,
        rows,
        depth,
        "attend_back",
        tail=list(tables),
        parts=1,
    )


def gathered_kernel(dq_ref, own_ref, cos_ref, sin_ref, *rest, places):
    out_ref = rest[-1]
    i = pl.program_id(0)
    grad = own_ref[...]
    for ref, (first, count) in zip(rest, places):
        here = jnp.logical_and(i >= first, i < first + count)
        grad = grad + jnp.where(here, ref[...].astype(WIDE), 0.0)
    keys = grad[:, :HEAD]
    out_ref[:, :HEAD] = dq_ref[...]
    out_ref[:, HEAD : 2 * HEAD] = (keys * cos_ref[...] - swapped(keys) * sin_ref[...]).astype(LOW)
    out_ref[:, 2 * HEAD :] = grad[:, HEAD:].astype(LOW)


def gathered(grad_query, own, tables, arrivals, rows=512):
    count = own.shape[0]
    places = [(first // rows, part.shape[0] // rows) for first, part in arrivals]

    def row(width):
        return pl.BlockSpec((rows, width), lambda i: (i, 0))

    def part(place):
        return pl.BlockSpec((rows, 2 * HEAD), lambda i: (jnp.clip(i - place[0], 0, place[1] - 1), 0))

    return pl.pallas_call(
        functools.partial(gathered_kernel, places=places),
        grid=(count // rows,),
        in_specs=[row(HEAD), row(2 * HEAD), row(HEAD), row(HEAD)] + [part(place) for place in places],
        out_specs=row(3 * HEAD),
        out_shape=jax.ShapeDtypeStruct((count, 3 * HEAD), LOW),
        cost_estimate=pl.CostEstimate(flops=0, bytes_accessed=16 * 2**20, transcendentals=0),
        name="gathered",
    )(grad_query, own, *tables, *[array for _, array in arrivals])


def on_device(
    acoustic_features,
    clip_durations,
    early_layernorm_scale,
    early_widening_matrix,
    early_narrowing_matrix,
    mixer_layernorm_scale,
    triple_matrix,
    mixer_exit_matrix,
    filter_layernorm_scale,
    gating_pair_matrix,
    depthwise_filter,
    running_stats_factor,
    running_stats_offset,
    filter_exit_projection,
    later_layernorm_scale,
    later_widening_matrix,
    later_narrowing_matrix,
    last_layernorm_scale,
    quantizer_projection,
    entry_vectors,
    smoothing_level,
    random_flat_samples,
    expected_entries,
    result_adjoint,
    discrete_adjoint,
):
    seq_count, mp_count = lax.axis_size("seq"), lax.axis_size("mp")
    seq_at, mp_at = lax.axis_index("seq"), lax.axis_index("mp")
    core = seq_at % 2
    frame_rows = acoustic_features.shape[0]
    all_rows = frame_rows * seq_count
    own = frame_rows // mp_count
    own_base = seq_at * frame_rows + mp_at * own

    local_heads = triple_matrix.shape[2] // HEAD
    group_place = seq_at % local_heads
    groups = [
        [(z * local_heads + g) * mp_count + m for g in range(local_heads) for m in range(mp_count)]
        for z in range(seq_count // local_heads)
    ]
    group_size = local_heads * mp_count
    line = seq_count // local_heads
    lines = [
        [(z * local_heads + g) * mp_count + m for z in range(line)] for g in range(local_heads) for m in range(mp_count)
    ]

    def own_rows(shard):
        size = shard.shape[0] // local_heads
        return cut(shard, part_of(group_place, local_heads) * size, size)

    def own_columns(shard):
        size = shard.shape[1] // local_heads
        return cut(shard, part_of(group_place, local_heads) * size, size, 1).T

    def over_group(part):
        return lax.all_gather(part, BOTH, axis_index_groups=groups, axis=0)

    def grouped(array):
        parts = array.reshape(-1, mp_count, local_heads, array.shape[1] // group_size)
        parts = jnp.stack([parts[:, :, part_of(g, local_heads)] for g in range(local_heads)], 1)
        return parts.reshape(array.shape)

    def ungrouped(array):
        parts = array.reshape(-1, local_heads, mp_count, array.shape[1] // group_size)
        places = sorted(range(local_heads), key=lambda g: part_of(g, local_heads))
        return jnp.stack([parts[:, g] for g in places], 2).reshape(array.shape)

    def group_total(array, over=None):
        return lax.psum_scatter(array, BOTH, scatter_dimension=0, axis_index_groups=over or groups, tiled=True)

    def rel_rows(array, k):
        return cut(array, mp_place(k) * own, own)

    def local_halves(array):
        half = array.shape[1] // 2
        return [cut(array, (core ^ j) * half, half, 1) for j in range(2)]

    small_weights = jnp.concatenate(
        [depthwise_filter, running_stats_factor[None], running_stats_offset[None]], 0
    )
    small_all = grouped(joined(from_mp(small_weights), 1))
    filter_all, factor_all, offset_all = small_all[:KERNEL], small_all[KERNEL], small_all[KERNEL + 1]

    code_parts = jnp.stack([own_columns(quantizer_projection), own_rows(entry_vectors)])
    noise_parts = [-jnp.log(-jnp.log(rel_rows(random_flat_samples, k))) for k in range(mp_count)]
    noise_parts = noise_parts[:1] + [part.astype(LOW) for part in noise_parts[1:]]
    first_rows, code_parts, noise_parts = paced(acoustic_features, code_parts, noise_parts)
    code_every = over_group(code_parts)
    noise_parts = noise_parts[:1] + [mp_shift(part, k).astype(WIDE) for k, part in enumerate(noise_parts) if k]

    first = []
    for k in list(range(1, mp_count)) + [0]:
        rows = rel_rows(first_rows, k).astype(WIDE)
        entered, normed, inverse = norm_forward(rows, early_layernorm_scale)
        hidden = dot(entered, early_widening_matrix)
        activated = (hidden * jax.nn.sigmoid(hidden)).astype(LOW)
        part = dot(activated, early_narrowing_matrix).astype(LOW)
        first.append((part, entered, hidden, activated, normed, inverse))
    first = [first[-1]] + first[:-1]
    features = rel_rows(acoustic_features, 0).astype(WIDE)
    group_rows = local_heads * frame_rows
    group_at = seq_at // local_heads
    group_index = group_at * group_rows + jnp.arange(group_rows, dtype=jnp.int32)
    _, group_start, group_end = clip_of(clip_durations, group_index)
    tables = turn_tables(group_index - group_start)
    head_matrix = cut(triple_matrix, part_of(group_place, local_heads) * HEAD, HEAD, 2)
    head_matrix = jnp.concatenate([head_matrix[i] for i in range(3)], 1)
    middle_parts = [
        own_rows(mixer_exit_matrix),
        own_columns(gating_pair_matrix[0]),
        own_columns(gating_pair_matrix[1]),
        own_rows(filter_exit_projection),
    ]
    up_part, down_part = own_columns(later_widening_matrix), own_rows(later_narrowing_matrix)
    after_ffn = features + 0.5 * to_mp([f[0] for f in first])
    after_ffn, tables, sent = paced(
        after_ffn, tables, (jnp.stack(middle_parts), up_part, down_part, head_matrix)
    )

    quantizer_all, book_all = code_every[:, 0].reshape(-1, D), code_every[:, 1].reshape(-1, D)
    noise = grouped(joined([noise_parts[0]] + noise_parts[:0:-1], 1))
    temper = smoothing_level[0]
    own_features = rel_rows(acoustic_features, 0)
    noisy = dot_nt(own_features, quantizer_all) + noise
    tempered = noisy / temper
    assigned = jnp.exp(tempered - jax.nn.logsumexp(tempered, -1)[:, None])
    assigned_low = assigned.astype(LOW)
    quant_low = dot(assigned_low, book_all).astype(LOW)
    own_discrete = rel_rows(discrete_adjoint, 0)
    grad_soft = dot_nt(own_discrete, book_all)
    row_dot = jnp.sum(assigned * grad_soft, -1)
    grad_tempered = assigned * (grad_soft - row_dot[:, None])
    grad_temper = -jnp.sum(grad_tempered * noisy) / (temper * temper)
    grad_entry = (grad_tempered / temper).astype(LOW)
    quant_in = dot(grad_entry, quantizer_all)

    att_entered, att_normed, att_inverse = norm_forward(after_ffn, mixer_layernorm_scale)
    att_group = over_group(att_entered).reshape(group_rows, D)
    reaches = range(1, -(-(LONGEST - 1) // group_rows) + 1)
    halo = [min(group_rows, -(-(LONGEST - (r - 1) * group_rows) // 1024) * 1024) for r in reaches]
    halo_rows = sum(halo)
    key_base = group_at * group_rows - halo_rows
    spans = (group_start - key_base, group_end - key_base)
    att_group, assigned_low, quant_low, sent = paced(att_group, assigned_low, quant_low, sent)
    middle_every = over_group(sent[0])
    head_matrix = sent[3]
    exit_all, value_all, gate_all, point_all = [middle_every[:, i].reshape(-1, D) for i in range(4)]
    up_all = over_group(sent[1]).reshape(-1, D)
    down_all = over_group(sent[2]).reshape(-1, D)
    query_rot, kv_own = project(att_group, head_matrix, tables)
    lower = [seq_shift(kv_own[group_rows - n :], local_heads * r) for r, n in zip(reaches, halo)]
    upper = [seq_shift(kv_own[:n], -local_heads * r) for r, n in zip(reaches, halo)]
    kv_pieces = lower[::-1] + [kv_own] + upper
    mixed_low, mixed, row_lse = attend(query_rot, kv_pieces, spans)
    mixed_low, head_sent, grad_entry, quant_in, grad_temper = paced(
        mixed_low, head_matrix, grad_entry, quant_in, grad_temper
    )
    heads_all = over_group(head_sent)

    def exchange(array):
        return lax.all_to_all(array, BOTH, 0, 0, axis_index_groups=groups)

    att_parts = exchange(mixed_low.reshape(group_size, own, HEAD))
    att_low = jnp.transpose(att_parts, (1, 0, 2)).reshape(own, D)
    after_att = after_ffn + dot(att_low, exit_all)

    half_kernel = KERNEL // 2
    pad_index = own_base - half_kernel + jnp.arange(own + 2 * half_kernel, dtype=jnp.int32)
    pad_seg = clip_of(clip_durations, pad_index)[0]
    pad_seg = jnp.where(jnp.logical_and(pad_index >= 0, pad_index < all_rows), pad_seg, -1)
    own_seg = pad_seg[half_kernel : half_kernel + own]
    masks = [(pad_seg[j : j + own] == own_seg)[:, None] for j in range(KERNEL)]

    def padded(block):
        low = flat_shift(block[own - half_kernel :], 1)
        high = flat_shift(block[:half_kernel], -1)
        return jnp.concatenate([low, block, high], 0).astype(WIDE)

    conv_entered, conv_normed, conv_inverse = norm_forward(after_att, filter_layernorm_scale)
    glu_value = dot_nt(conv_entered, value_all)
    glu_gate = jax.nn.sigmoid(dot_nt(conv_entered, gate_all))
    glu_low = (glu_value * glu_gate).astype(LOW)
    glu_padded = padded(glu_low)
    conv_out = jnp.zeros((own, D), WIDE)
    for j in range(KERNEL):
        conv_out = conv_out + filter_all[j][None, :] * jnp.where(masks[j], glu_padded[j : j + own], 0.0)
    sums = total_over_all(jnp.stack([jnp.sum(conv_out, 0), jnp.sum(conv_out * conv_out, 0)]), 1)
    bn_mean = sums[0] / all_rows
    bn_inv = lax.rsqrt(sums[1] / all_rows - bn_mean * bn_mean + EPSILON)
    bn_hat = (conv_out - bn_mean) * bn_inv
    bn_out = bn_hat * factor_all + offset_all
    bn_sigma = jax.nn.sigmoid(bn_out)
    swish_low = (bn_out * bn_sigma).astype(LOW)
    after_conv = after_att + dot(swish_low, point_all)

    late_entered, late_normed, late_inverse = norm_forward(after_conv, later_layernorm_scale)
    late_hidden = dot_nt(late_entered, up_all)
    late_act = (late_hidden * jax.nn.sigmoid(late_hidden)).astype(LOW)
    branch = dot(late_act, down_all)
    after_two = after_conv + 0.5 * branch
    final_low, final_normed, final_inverse = norm_forward(after_two, last_layernorm_scale)

    codes = book_all.shape[0]
    logits = dot_nt(final_low, book_all) * D ** (-0.5)
    code_index = grouped(jnp.arange(codes, dtype=jnp.int32)[None, :])
    is_target = rel_rows(expected_entries, 0)[:, None] == code_index
    pred_lse = jax.nn.logsumexp(logits, -1)
    row_loss = pred_lse - jnp.sum(jnp.where(is_target, logits, 0.0), -1)
    grad_pred = (jnp.exp(logits - pred_lse[:, None]) - is_target.astype(WIDE)).astype(LOW)
    grad_final = rel_rows(result_adjoint, 0).astype(WIDE) + dot(grad_pred, book_all) * D ** (-0.5)
    grad_final, loss_shares = paced(grad_final, from_mp(row_loss))
    frame_loss = joined(loss_shares)
    grad_four, grad_ln_final = norm_backward(grad_final, last_layernorm_scale, final_normed, final_inverse)
    late_branch = (0.5 * grad_four).astype(LOW)
    grad_act = dot_nt(late_branch, down_all)
    grad_hidden = (grad_act * silu_slope(late_hidden, jax.nn.sigmoid(late_hidden))).astype(LOW)
    late_in = dot(grad_hidden, up_all)
    late_grads = products([[(grad_hidden, late_entered, None)], [(late_act, late_branch, None)]], group_size, line)
    late_norm_grad, grad_ln_ffn2 = norm_backward(late_in, later_layernorm_scale, late_normed, late_inverse)
    grad_three = grad_four + late_norm_grad

    conv_branch = grad_three.astype(LOW)
    grad_swish = dot_nt(conv_branch, point_all)
    grad_bn = grad_swish * silu_slope(bn_out, bn_sigma)
    back_sums = jnp.stack([jnp.sum(grad_bn, 0), jnp.sum(grad_bn * bn_hat, 0)])
    back_sums, late_grads, heads_all = paced(back_sums, late_grads, heads_all)
    late_part = group_total(late_grads)
    back_sums = total_over_all(back_sums, 2)
    grad_conv = (
        factor_all * bn_inv * (grad_bn - back_sums[0] / all_rows - bn_hat * back_sums[1] / all_rows)
    ).astype(LOW)
    grad_padded = padded(grad_conv)
    grad_exact = grad_conv.astype(WIDE)
    grad_taps = []
    grad_gated = jnp.zeros_like(grad_exact)
    for j in range(KERNEL):
        grad_taps.append(jnp.sum(grad_exact * jnp.where(masks[j], glu_padded[j : j + own], 0.0), 0))
        back = 2 * half_kernel - j
        grad_gated = grad_gated + filter_all[j][None, :] * jnp.where(
            masks[back], grad_padded[back : back + own], 0.0
        )
    grad_value = (grad_gated * glu_gate).astype(LOW)
    grad_gate = (grad_gated * glu_value * glu_gate * (1.0 - glu_gate)).astype(LOW)
    conv_in = dot(grad_value, value_all) + dot(grad_gate, gate_all)
    conv_norm_grad, grad_ln_conv = norm_backward(conv_in, filter_layernorm_scale, conv_normed, conv_inverse)
    grad_two = grad_three + conv_norm_grad

    att_branch = grad_two.astype(LOW)
    mixer_grads = products(
        [
            [(grad_value, conv_entered, None)],
            [(grad_gate, conv_entered, None)],
            [(swish_low, conv_branch, None)],
            [(att_low, att_branch, None)],
            [(grad_pred, final_low, D ** (-0.5)), (assigned_low, own_discrete, None)],
            [(grad_entry, own_features, None)],
        ],
        group_size,
        line,
    )
    grad_heads = dot_nt(att_branch, exit_all).astype(LOW)
    grad_heads = jnp.transpose(grad_heads.reshape(own, group_size, HEAD), (1, 0, 2))
    grad_mixed = exchange(grad_heads).reshape(group_rows, HEAD)
    grad_mixed, mixer_grads = paced(grad_mixed, mixer_grads)
    mixer_total = group_total(mixer_grads)
    grad_query, *grad_pieces = attend_back(query_rot, grad_mixed, mixed, row_lse, tables, kv_pieces, spans)
    grad_pieces, late_part = paced(grad_pieces, late_part)
    arrivals = []
    reach_count = len(halo)
    for r, n in zip(reaches, halo):
        back = seq_shift(grad_pieces[reach_count - r], -local_heads * r)
        arrivals.append((group_rows - n, back))
        back = seq_shift(grad_pieces[reach_count + r], local_heads * r)
        arrivals.append((0, back))
    grad_proj = gathered(grad_query, grad_pieces[reach_count], tables, arrivals)

    proj_parts = exchange(grad_proj.reshape(group_size, own, 3 * HEAD))
    head_grads = dot_tn(grad_proj, att_group).astype(LOW)
    proj_parts, head_grads = paced(proj_parts, head_grads)
    head_grads = jnp.transpose(head_grads.reshape(3, line, HEAD // line, D), (1, 0, 2, 3)).reshape(line, -1, D)
    att_in = lax.dot_general(
        proj_parts, heads_all, (((0, 2), (0, 2)), ((), ())), preferred_element_type=WIDE
    )
    att_norm_grad, grad_ln_att = norm_backward(att_in, mixer_layernorm_scale, att_normed, att_inverse)
    grad_one = grad_two + att_norm_grad
    grad_one, late_part, mixer_total, head_grads = paced(grad_one, late_part, mixer_total, head_grads)
    every_total = [part.reshape(line, -1, D) for part in (late_part, mixer_total, head_grads)]
    every_total = group_total(jnp.concatenate(every_total, 1).reshape(-1, D), lines)

    early_branch = from_mp((0.5 * grad_one).astype(LOW))
    early_in, early_grads = [], []
    for k, (_, entered, hidden, activated, _, _) in enumerate(first):
        grad_act = dot_nt(early_branch[k], early_narrowing_matrix)
        early_grads.append((grad_act * silu_slope(hidden, jax.nn.sigmoid(hidden))).astype(LOW))
        early_in.append(dot_nt(early_grads[k], early_widening_matrix))

    act_all = jnp.concatenate([f[3] for f in first], 0)
    branch_all = jnp.concatenate(early_branch, 0)
    entered_all = jnp.concatenate([f[1] for f in first], 0)
    hid_all = jnp.concatenate(early_grads, 0)
    up_parts = [dot_tn(entered_all, hid).astype(LOW) for hid in local_halves(hid_all)]
    down_parts = [dot_tn(act, branch_all).astype(LOW) for act in local_halves(act_all)]
    early_norm_grad, grad_ln_ffn1 = norm_backward(to_mp(early_in), early_layernorm_scale, first[0][4], first[0][5])
    frames_low = (grad_one + early_norm_grad + quant_in).astype(LOW)
    frames_low, every_total = paced(frames_low, every_total)
    every = lax.all_gather(every_total, "seq", axis=0)
    small, (grad_frames, layer_out, quantized), (up1_halves, down1_halves) = seq_total(
        [frames_low, final_low, quant_low],
        [up_parts[0], down_parts[0]],
        [up_parts[1], down_parts[1]],
        jnp.stack(
            [grad_ln_ffn1, grad_ln_att, grad_ln_conv, grad_ln_ffn2, grad_ln_final]
            + grad_taps
            + [jnp.full((D,), grad_temper, WIDE)]
        ),
        3,
    )
    late_rows = late_part.shape[0] // line // 2
    mixer_rows = mixer_total.shape[0] // line // 6
    up2_grad = laid(every, 0, late_rows, 1, local_heads, True)[0]
    down2_grad = laid(every, late_rows, late_rows, 1, local_heads, False)[0]

    def mixer_laid(at, amount, turned):
        return laid(every, 2 * late_rows + at * mixer_rows, mixer_rows, amount, local_heads, turned)

    gate_grads = mixer_laid(0, 2, True)
    point_grad, exit_grad, book_grad = [mixer_laid(at, 1, False)[0] for at in (2, 3, 4)]
    code_grad, qkv_grad = mixer_laid(5, 1, True)[0], mixer_laid(6, 3, True)
    up1_grad, down1_grad = beside(up1_halves, False), beside(down1_halves, True)
    own_channels = filter_exit_projection.shape[0]

    def own_part(array):
        return cut(ungrouped(array), mp_at * own_channels, own_channels, 1)

    bn_grads = own_part(back_sums)

    return (
        layer_out,
        quantized,
        frame_loss,
        grad_frames,
        small[0],
        up1_grad,
        down1_grad,
        small[1],
        qkv_grad,
        exit_grad,
        small[2],
        gate_grads,
        own_part(small[5 : 5 + KERNEL]),
        bn_grads[1],
        bn_grads[0],
        point_grad,
        small[3],
        up2_grad,
        down2_grad,
        small[4],
        code_grad,
        book_grad,
        small[5 + KERNEL, :1],
    )


def solution(mesh):
    in_specs = (
        P("seq", None),
        P(),
        P(),
        P(None, "mp"),
        P("mp", None),
        P(),
        P(None, None, "mp"),
        P("mp", None),
        P(),
        P(None, None, "mp"),
        P(None, "mp"),
        P("mp"),
        P("mp"),
        P("mp", None),
        P(),
        P(None, "mp"),
        P("mp", None),
        P(),
        P(None, "mp"),
        P("mp", None),
        P(),
        P("seq", "mp"),
        P("seq"),
        P("seq", None),
        P("seq", None),
    )
    out_specs = (
        P("seq", None),
        P("seq", None),
        P("seq"),
        P("seq", None),
        P(),
        P(None, "mp"),
        P("mp", None),
        P(),
        P(None, None, "mp"),
        P("mp", None),
        P(),
        P(None, None, "mp"),
        P(None, "mp"),
        P("mp"),
        P("mp"),
        P("mp", None),
        P(),
        P(None, "mp"),
        P("mp", None),
        P(),
        P(None, "mp"),
        P("mp", None),
        P(),
    )
    return jax.shard_map(
        on_device, mesh=mesh, in_specs=in_specs, out_specs=out_specs, check_vma=False
    )
```
